32 devices in a mesh: dp: 8 (over z, x), tensor: 4 (over y, core).
Axes of the slice: x: 2, y: 2, z: 4, core: 2. Of those that a mesh axis runs over, the one named last changes fastest.
Arguments:
- tokens: bfloat16 [8192, 2048], P('dp'), may hold values from -6 to 6
- seq_lengths: int32 [8, 5], P('dp'), may hold values from 1 to 512, 1024 in all within a row
- qkv_weight: bfloat16 [3, 2048, 2048], P(None, None, 'tensor'), may hold values from -0.125 to 0.125
- qkv_bias: bfloat16 [3, 2048], P(None, 'tensor'), may hold values from -4 to 4
- out_weight: bfloat16 [2048, 2048], P('tensor'), may hold values from -0.375 to 0.375
- gate_up_weight: bfloat16 [2, 2048, 5632], P(None, None, 'tensor'), may hold values from -0.125 to 0.125
- down_weight: bfloat16 [5632, 2048], P('tensor'), may hold values from -0.078125 to 0.078125
- norm_gains: float32 [2, 2048], replicated, may hold values from 0.25 to 1.75
- norm_shifts: float32 [2, 2048], replicated, may hold values from -2 to 2
- cotangent: bfloat16 [8192, 2048], P('dp'), may hold values from -6 to 6
Outputs:
- block_out: bfloat16 [8192, 2048], P(('dp', 'tensor'))
- input_grad: float32 [8192, 2048], P(('dp', 'tensor'))
- qkv_weight_grad: float32 [3, 2048, 2048], P(None, 'dp', 'tensor')
- qkv_bias_grad: float32 [3, 2048], replicated
- out_weight_grad: float32 [2048, 2048], P('tensor', 'dp')
- gate_up_weight_grad: float32 [2, 2048, 5632], P(None, 'dp', 'tensor')
- down_weight_grad: float32 [5632, 2048], P('tensor', 'dp')
- norm_gains_grad: float32 [2, 2048], replicated
- norm_shifts_grad: float32 [2, 2048], replicated
The draws below stay inside these ranges and needn't reach their ends.
All inputs are finite; a program needn't handle non-finite values.
Results may differ from the reference program's by a relative error of at most 0.018.
Values may be sent and summed in bfloat16 or wider, within the bound.
A program may use at most 384 MiB of HBM per device.

```python
import math
import jax
import jax.numpy as jnp
import numpy as np
from jax import lax

D = 2048
H = 32
HD = 64
FF = 5632
TOK_DEV = 1024
SEQ_MAX = 512
NSEQ = 5
TOKENS = 8192
N_DP = 8


def spiked(array, rng, source, target, shards_of, factor):
    owner, partner = [(jnp.arange(array.shape[dim]) // (array.shape[dim] // shards_of)).reshape([-1 if axis == dim else 1 for axis in range(array.ndim)]) for dim in (source, target)]
    chosen = jax.random.permutation(rng, shards_of)[partner]
    strong = (owner == chosen) | (owner == (partner + shards_of // 2) % shards_of)
    return jnp.where(strong, factor * array, array)


def shard_levels(rng, dims, shards, least, top_value):
    gain = 1.0
    for axis_at, parts in shards:
        steps = jax.random.uniform(jax.random.fold_in(jax.random.fold_in(rng, 6), axis_at), (parts,), jnp.float32, least / len(shards), top_value / len(shards))
        gain = gain * jnp.repeat(jnp.exp(steps), dims[axis_at] // parts).reshape((-1,) + (1,) * (len(dims) - 1 - axis_at))
    return gain


def profile(amount, total, reach, slope):
    weights = [(1 << 20) // math.isqrt(rank ** slope) + 1 for rank in range(2, amount + 1)]
    rest, given = total - reach - (amount - 1), [1] * (amount - 1)
    while rest > 0:
        movable = [i for i in range(amount - 1) if given[i] < reach]
        whole, budget = sum([weights[i] for i in movable]), rest
        for i in movable:
            extra = min(reach - given[i], max(1, budget * weights[i] // whole), rest)
            given[i] = given[i] + extra
            rest = rest - extra
    return np.array([reach] + given)


def uneven(stream_key, amount, total, bound, slope):
    if amount == 2:
        one = jax.random.randint(stream_key, (), max(1, total - bound), min(bound, total - 1) + 1)
        return jnp.stack([one, total - one])
    tallies = jnp.asarray(profile(amount, total, bound, slope), jnp.int32)
    twos = (amount - 1) // 2
    source_of, taker = tallies[1:1 + 2 * twos:2], tallies[2:2 + 2 * twos:2]
    room = jnp.minimum(source_of - 1, bound - taker)
    moved = jax.random.randint(jax.random.fold_in(stream_key, 1), (twos,), 0, 1 << 20) % (room + 1)
    tallies = tallies.at[1:1 + 2 * twos:2].set(source_of - moved).at[2:2 + 2 * twos:2].set(taker + moved)
    return tallies[jax.random.permutation(jax.random.fold_in(stream_key, 2), amount)]


def noise(key, shape, scale, most, cuts=(), kind=jnp.bfloat16):
    level = shard_levels(key, shape, cuts, -0.22, 0.18) if cuts else 1.0
    values = jax.random.normal(key, shape, jnp.float32) * scale * level
    return jnp.minimum(jnp.maximum(values, -most), most).astype(kind)


def bell_draw_with(rng, shape, scale, bound, split, heavy, kind=jnp.bfloat16):
    array = scale * jax.random.normal(rng, shape, jnp.float32)
    if split:
        array = array * shard_levels(rng, shape, split, -0.22, 0.18)
    return jnp.clip(spiked(array, jax.random.fold_in(rng, 3), *heavy), -bound, bound).astype(kind)


def setup_inputs(seed: int = 0) -> dict:
    keys = jax.random.split(jax.random.key(seed), 11)
    tokens = bell_draw_with(keys[0], (TOKENS, D), 1.0, 6.0, ((0, 8),), (0, 1, 8, 2.0))
    seq_lengths = jax.vmap(lambda own: uneven(own, NSEQ, TOK_DEV, SEQ_MAX, 2))(jax.random.split(keys[1], N_DP)).reshape((N_DP, NSEQ)).astype(jnp.int32)
    qkv_weight = noise(keys[2], (3, D, D), D ** -0.5, 0.125, ((2, 4),))
    qkv_bias = noise(keys[3], (3, D), 0.5, 4.0, ((1, 4),))
    out_weight = noise(keys[4], (D, D), (D // 8) ** -0.5, 0.375, ((0, 4),))
    gate_up_weight = noise(keys[5], (2, D, FF), D ** -0.5, 0.125, ((2, 4),))
    down_weight = noise(keys[6], (FF, D), FF ** -0.5, 0.078125, ((0, 4),))
    norm_gains = jnp.clip(1.0 + 0.15 * jax.random.normal(keys[7], (2, D), jnp.float32), 0.25, 1.75)
    norm_shifts = noise(keys[8], (2, D), 0.3, 2.0, (), jnp.float32)
    cotangent = bell_draw_with(keys[9], (TOKENS, D), 1.0, 6.0, ((0, 8),), (0, 1, 8, 2.0))
    return dict(tokens=tokens, seq_lengths=seq_lengths, qkv_weight=qkv_weight, qkv_bias=qkv_bias, out_weight=out_weight, gate_up_weight=gate_up_weight, down_weight=down_weight, norm_gains=norm_gains, norm_shifts=norm_shifts, cotangent=cotangent)


@jax.custom_vjp
def low(v):
    return lax.optimization_barrier(v.astype(jnp.bfloat16)).astype(jnp.float32)

@jax.custom_vjp
def low_back(v):
    return v

def low_keep(v):
    return (low(v), None)

def low_pass(kept, grad):
    return (grad,)

def back_keep(v):
    return (v, None)

def back_low(kept, grad):
    return (low(grad),)
low.defvjp(low_keep, low_pass)
low_back.defvjp(back_keep, back_low)

def layer_norm(values, gain_row, shift_row):
    centred = values - lax.optimization_barrier(jnp.mean(values, axis=-1, keepdims=True))
    spread = lax.optimization_barrier(jnp.mean(centred * centred, axis=-1, keepdims=True))
    return centred * lax.rsqrt(spread + 1e-05) * gain_row + shift_row

def positions(lengths, row_count):
    indices = jnp.arange(row_count, dtype=jnp.int32)
    ends_at = jnp.cumsum(lengths, dtype=jnp.int32)
    passed = indices[:, None] >= ends_at[None, :]
    segment = lax.optimization_barrier(jnp.sum(passed.astype(jnp.int32), axis=1, dtype=jnp.int32))
    begins = lax.optimization_barrier(jnp.sum(jnp.where(passed, lengths[None, :], 0), axis=1, dtype=jnp.int32))
    places = (indices - begins).astype(jnp.float32)
    halfway = HD // 8
    rates = 10000.0 ** (-(jnp.arange(halfway, dtype=jnp.float32) / halfway))
    angles = places[:, None] * rates[None, :]
    return (jnp.cos(angles), jnp.sin(angles), segment, indices)

def rotate(values, cosine, sine):
    halfway = cosine.shape[-1]
    first_half = values[..., :halfway]
    second_half = values[..., halfway:2 * halfway]
    cos_rows = cosine[:, None, :]
    sin_rows = sine[:, None, :]
    return jnp.concatenate([first_half * cos_rows - second_half * sin_rows, second_half * cos_rows + first_half * sin_rows, values[..., 2 * halfway:]], axis=-1)

def layer_block(inputs, lengths, weights):
    qkv_w, qkv_b, out_w, gate_up_w, down_w, gains, shifts = weights
    highest = lax.Precision.HIGHEST
    row_count = inputs.shape[0]
    cosine, sine, segment, indices = positions(lengths, row_count)
    normed = low(layer_norm(inputs, gains[0], shifts[0]))
    projected = jnp.einsum('td,kde->kte', normed, qkv_w, precision=highest) + qkv_b[:, None, :]
    projected = low_back(projected)
    queries = low(rotate(projected[0].reshape(row_count, H, HD), cosine, sine))
    keys_all = low(rotate(projected[1].reshape(row_count, H, HD), cosine, sine))
    values_all = low(projected[2].reshape(row_count, H, HD))
    scores = jnp.einsum('qhd,khd->hqk', queries, keys_all, precision=highest) * HD ** (-0.5)
    scores = low_back(scores)
    allowed = (segment[:, None] == segment[None, :]) & (indices[None, :] <= indices[:, None])
    masked = jnp.where(allowed[None], scores, -1e+30)
    shifted = jnp.exp(masked - lax.optimization_barrier(jnp.max(masked, axis=-1, keepdims=True)))
    probs = shifted / lax.optimization_barrier(jnp.sum(shifted, axis=-1, keepdims=True))
    heads_out = jnp.einsum('hqk,khd->qhd', low(probs), values_all, precision=highest).reshape(row_count, D)
    heads_out = low_back(low(heads_out))
    attended = low_back(jnp.dot(heads_out, out_w, precision=highest))
    residual = inputs + attended
    second = low(layer_norm(residual, gains[1], shifts[1]))
    gate_up = low_back(jnp.einsum('td,kdf->ktf', second, gate_up_w, precision=highest))
    hidden = low(jax.nn.silu(gate_up[0]) * gate_up[1])
    branch = low_back(jnp.dot(hidden, down_w, precision=highest))
    return residual + branch

def reference(tokens, seq_lengths, qkv_weight, qkv_bias, out_weight, gate_up_weight, down_weight, norm_gains, norm_shifts, cotangent):
    inputs = tokens.astype(jnp.float32).reshape(N_DP, TOK_DEV, D)
    params = (qkv_weight.astype(jnp.float32), qkv_bias.astype(jnp.float32), out_weight.astype(jnp.float32), gate_up_weight.astype(jnp.float32), down_weight.astype(jnp.float32), norm_gains.astype(jnp.float32), norm_shifts.astype(jnp.float32))

    def forward(block_inputs, qkv_w, qkv_b, out_w, gate_up_w, down_w, gains, shifts):
        weights = (qkv_w, qkv_b, out_w, gate_up_w, down_w, gains, shifts)

        def one_block(paired):
            return layer_block(paired[0], paired[1], weights)
        return lax.map(jax.checkpoint(one_block), (block_inputs, seq_lengths))
    result, pullback = jax.vjp(forward, inputs, *params)
    grads = pullback(cotangent.astype(jnp.float32).reshape(N_DP, TOK_DEV, D))
    return (result.reshape(TOKENS, D).astype(jnp.bfloat16), grads[0].reshape(TOKENS, D), grads[1], grads[2], grads[3], grads[4], grads[5], grads[6], grads[7])
```

```python
import functools

import jax
import jax.numpy as jnp
from jax import lax
from jax.experimental import pallas as pl
from jax.experimental.pallas import tpu as pltpu
from jax.sharding import PartitionSpec as P

HD = 64
SEQ_MAX = 512
BQ = 256
F32 = jnp.float32
BF16 = jnp.bfloat16
LOG2E = 1.4426950408889634
VMEM_LIMIT = 60 * 1024 * 1024


def norm_parts(values):
    centred = values - jnp.mean(values, axis=-1, keepdims=True)
    inverse = lax.rsqrt(jnp.mean(centred * centred, axis=-1, keepdims=True) + 1e-05)
    return (centred * inverse, inverse)


def norm_back(unit, inverse, gain_row, grad_rows):
    scaled = grad_rows * gain_row
    return inverse * (
        scaled
        - jnp.mean(scaled, axis=-1, keepdims=True)
        - unit * jnp.mean(scaled * unit, axis=-1, keepdims=True)
    )


def positions(lengths, row_count):
    indices = jnp.arange(row_count, dtype=jnp.int32)
    count = lengths.shape[0]
    order = jnp.arange(count, dtype=jnp.int32)
    ends_at = jnp.sum(jnp.where(order[:, None] <= order[None, :], lengths[:, None], 0), axis=0)
    passed = indices[:, None] >= ends_at[None, :]
    begins = jnp.sum(jnp.where(passed, lengths[None, :], 0), axis=1, dtype=jnp.int32)
    places = (indices - begins).astype(F32)
    half = HD // 8
    lane = jnp.arange(128, dtype=jnp.int32) % HD
    rates = 10000.0 ** (-((lane % half).astype(F32) / half))
    angles = places[:, None] * rates[None, :]
    cosine, sine = jnp.cos(angles), jnp.sin(angles)
    turn = jnp.where(lane < 2 * half, cosine, 1.0)
    ahead = jnp.where(lane < half, -sine, 0.0)
    behind = jnp.where((lane >= half) & (lane < 2 * half), sine, 0.0)
    return begins, turn, ahead, behind


def turned(values, turn, ahead, behind):
    half = HD // 8
    width = values.shape[1]
    times = width // turn.shape[1]

    def wide(table):
        return jnp.concatenate([table] * times, axis=1) if times > 1 else table

    return (
        values * wide(turn)
        + pltpu.roll(values, width - half, 1) * wide(ahead)
        + pltpu.roll(values, half, 1) * wide(behind)
    )


def qkv_kernel(x_ref, w_ref, b_ref, g_ref, s_ref, c_ref, a_ref, h_ref, n_ref, q_ref, k_ref, v_ref):
    unit, _ = norm_parts(x_ref[...].astype(F32))
    normed = (unit * g_ref[...] + s_ref[...]).astype(BF16)
    n_ref[...] = normed
    for j, out in enumerate((q_ref, k_ref, v_ref)):
        got = jnp.dot(normed, w_ref[j], preferred_element_type=F32) + b_ref[j : j + 1, :]
        if j < 2:
            got = turned(got, c_ref[...], a_ref[...], h_ref[...])
        out[...] = got.astype(BF16)


def project(tokens, weight, bias, gain, shift, tables):
    rows, full = tokens.shape
    width = weight.shape[2]
    block = min(256, rows)

    def whole(*dims):
        return pl.BlockSpec(dims, lambda i: (0,) * len(dims))

    def by_row(columns):
        return pl.BlockSpec((block, columns), lambda i: (i, 0))

    return pl.pallas_call(
        qkv_kernel,
        grid=(rows // block,),
        in_specs=[
            by_row(full),
            whole(3, full, width),
            whole(3, width),
            whole(1, full),
            whole(1, full),
            by_row(128),
            by_row(128),
            by_row(128),
        ],
        out_specs=[by_row(full), by_row(width), by_row(width), by_row(width)],
        out_shape=[jax.ShapeDtypeStruct((rows, full), BF16)]
        + [jax.ShapeDtypeStruct((rows, width), BF16)] * 3,
        compiler_params=pltpu.CompilerParams(vmem_limit_bytes=VMEM_LIMIT),
        cost_estimate=pl.CostEstimate(
            flops=6 * rows * full * width,
            bytes_accessed=2 * (2 * rows * full + 3 * full * width + 3 * rows * width),
            transcendentals=0,
        ),
    )(tokens, weight, bias.astype(F32), gain[None], shift[None], *tables)


def spans(step, blocks):
    most = SEQ_MAX // BQ + 1
    forms = []
    for at in range(min(most - 1, blocks)):
        forms.append((step == at, 0, (at + 1) * BQ))
    if blocks >= most:
        first = pl.multiple_of((step - (most - 1)) * BQ, BQ)
        forms.append((step >= most - 1, first, most * BQ))
    return forms


def allowed_bias(begin_row, first, count, step):
    key_at = first + lax.broadcasted_iota(jnp.int32, (count, BQ), 0)
    query_at = step * BQ + lax.broadcasted_iota(jnp.int32, (count, BQ), 1)
    return jnp.where((key_at >= begin_row) & (key_at <= query_at), 0.0, -1e30)


def over_rows(left, right):
    return lax.dot_general(left, right, (((0,), (0,)), ((), ())), preferred_element_type=F32)


def over_columns(left, right):
    return lax.dot_general(left, right, (((1,), (1,)), ((), ())), preferred_element_type=F32)


def attend_kernel(blocks, begin_ref, q_ref, k_ref, v_ref, o_ref, l_ref):
    step = pl.program_id(1)
    factor = HD**-0.5 * LOG2E

    def one(first, count):
        bias = allowed_bias(begin_ref[...], first, count, step)
        rows = pl.ds(first, count)
        parts = []
        for head in range(2):
            lanes = slice(head * HD, (head + 1) * HD)
            scores = over_columns(k_ref[rows, lanes], q_ref[:, lanes]) * factor + bias
            top = jnp.max(scores, axis=0, keepdims=True)
            probs = jnp.exp2(scores - top)
            total = jnp.sum(probs, axis=0, keepdims=True)
            got = over_rows(v_ref[rows, lanes], probs.astype(BF16))
            parts.append(got * (1.0 / total))
            l_ref[head] = top + jnp.log2(total)
        o_ref[...] = jnp.concatenate(parts, axis=0).T.astype(BF16)

    for condition, first, count in spans(step, blocks):
        pl.when(condition)(functools.partial(one, first, count))


def attend(begins, queries, keys, values):
    rows, width = queries.shape
    blocks = rows // BQ
    return pl.pallas_call(
        functools.partial(attend_kernel, blocks),
        grid=(width // 128, blocks),
        in_specs=[
            pl.BlockSpec((1, BQ), lambda h, i: (0, i)),
            pl.BlockSpec((BQ, 128), lambda h, i: (i, h)),
            pl.BlockSpec((rows, 128), lambda h, i: (0, h)),
            pl.BlockSpec((rows, 128), lambda h, i: (0, h)),
        ],
        out_specs=[
            pl.BlockSpec((BQ, 128), lambda h, i: (i, h)),
            pl.BlockSpec((2, 1, BQ), lambda h, i: (h, 0, i)),
        ],
        out_shape=[
            jax.ShapeDtypeStruct((rows, width), BF16),
            jax.ShapeDtypeStruct((width // HD, 1, rows), F32),
        ],
        compiler_params=pltpu.CompilerParams(vmem_limit_bytes=VMEM_LIMIT),
        cost_estimate=pl.CostEstimate(
            flops=8 * rows * 768 * width, bytes_accessed=8 * rows * width, transcendentals=rows * 768 * width // HD
        ),
    )(begins[None], queries, keys, values)


def attend_back_kernel(
    blocks, begin_ref, q_ref, k_ref, v_ref, g_ref, l_ref, cq_ref, aq_ref, hq_ref, c_ref, a_ref, h_ref,
    dq_ref, dk_ref, dv_ref, sum_k, sum_v,
):
    step = pl.program_id(1)
    scale = HD**-0.5
    factor = scale * LOG2E

    @pl.when(step == 0)
    def _():
        sum_k[...] = jnp.zeros_like(sum_k)
        sum_v[...] = jnp.zeros_like(sum_v)

    def one(first, count):
        bias = allowed_bias(begin_ref[...], first, count, step)
        rows = pl.ds(first, count)
        dq, dk, dv = [], [], []
        for head in range(2):
            lanes = slice(head * HD, (head + 1) * HD)
            query, key, value, grad = q_ref[:, lanes], k_ref[rows, lanes], v_ref[rows, lanes], g_ref[:, lanes]
            probs = jnp.exp2(over_columns(key, query) * factor + bias - l_ref[head])
            weighed = probs * over_columns(value, grad)
            inner = jnp.sum(weighed, axis=0, keepdims=True)
            score_grad = (weighed - probs * inner).astype(BF16)
            dv.append(jnp.dot(probs.astype(BF16), grad, preferred_element_type=F32))
            dk.append(jnp.dot(score_grad, query, preferred_element_type=F32))
            dq.append(over_rows(key, score_grad))
        sum_k[rows, :] += jnp.concatenate(dk, axis=1)
        sum_v[rows, :] += jnp.concatenate(dv, axis=1)
        query_grad = jnp.concatenate(dq, axis=0).T * scale
        dq_ref[...] = turned(query_grad, cq_ref[...], -aq_ref[...], -hq_ref[...]).astype(BF16)

    for condition, first, count in spans(step, blocks):
        pl.when(condition)(functools.partial(one, first, count))

    @pl.when(step == blocks - 1)
    def _():
        dk_ref[...] = turned(sum_k[...] * scale, c_ref[...], -a_ref[...], -h_ref[...]).astype(BF16)
        dv_ref[...] = sum_v[...].astype(BF16)


def attend_back(begins, queries, keys, values, grads, logs, tables):
    rows, width = queries.shape
    blocks = rows // BQ
    part = pl.BlockSpec((BQ, 128), lambda h, i: (i, h))
    column = pl.BlockSpec((rows, 128), lambda h, i: (0, h))
    return pl.pallas_call(
        functools.partial(attend_back_kernel, blocks),
        grid=(width // 128, blocks),
        in_specs=[
            pl.BlockSpec((1, BQ), lambda h, i: (0, i)),
            part,
            column,
            column,
            part,
            pl.BlockSpec((2, 1, BQ), lambda h, i: (h, 0, i)),
        ]
        + [pl.BlockSpec((BQ, 128), lambda h, i: (i, 0))] * 3
        + [pl.BlockSpec((rows, 128), lambda h, i: (0, 0))] * 3,
        out_specs=[part, column, column],
        out_shape=[jax.ShapeDtypeStruct((rows, width), BF16)] * 3,
        scratch_shapes=[pltpu.VMEM((rows, 128), F32)] * 2,
        compiler_params=pltpu.CompilerParams(vmem_limit_bytes=VMEM_LIMIT),
        cost_estimate=pl.CostEstimate(
            flops=20 * rows * 768 * width, bytes_accessed=16 * rows * width, transcendentals=rows * 768 * width // HD
        ),
    )(begins[None], queries, keys, values, grads, logs, *tables, *tables)


def dot(left, right):
    return jnp.dot(left, right, preferred_element_type=F32)


def pick(values, at, axis):
    return lax.dynamic_index_in_dim(values, at, axis, keepdims=False)


def swap(values, axis, bit):
    size = lax.axis_size(axis)
    return lax.ppermute(values, axis, [(i, i ^ (1 << bit)) for i in range(size)])


def sum_rows(left, times):
    size = lax.axis_size("tensor")
    me = lax.axis_index("tensor")
    bits = size.bit_length() - 1
    rows = left.shape[0] // size
    core = me & 1
    by_core = left.reshape(size // 2, 2, rows, left.shape[1])

    def product(of):
        taken = pick(by_core, of, 1)
        got = times(taken.reshape(-1, left.shape[1]))
        return got.reshape(size // 2, rows, got.shape[-1])

    arrived = swap(product(1 - core).astype(BF16), "tensor", 0)
    total = product(core) + arrived.astype(F32)
    for bit in range(1, bits):
        mine = (me >> bit) & 1
        total = total.reshape(-1, 2, *total.shape[1:])
        arrived = swap(pick(total, 1 - mine, 1).astype(BF16), "tensor", bit)
        total = pick(total, mine, 1) + arrived.astype(F32)
    return total[0]


def spread_rows(own):
    size = lax.axis_size("tensor")
    me = lax.axis_index("tensor")
    bits = size.bit_length() - 1
    rows, columns = own.shape
    held = own[None]
    for bit in reversed(range(bits)):
        other = swap(held, "tensor", bit)
        mine = ((me >> bit) & 1) == 0
        held = jnp.stack([jnp.where(mine, held, other), jnp.where(mine, other, held)], axis=1)
        held = held.reshape(-1, rows, columns)
    return held.reshape(-1, columns)


def sum_parts(send, keep, shape_back):
    size = lax.axis_size("dp")
    me = lax.axis_index("dp")
    bits = size.bit_length() - 1
    arrived = swap(send, "dp", 0)
    total = keep + arrived.astype(F32)
    for bit in range(1, bits):
        mine = (me >> bit) & 1
        total = total.reshape(-1, 2, *total.shape[1:])
        arrived = swap(pick(total, 1 - mine, 1).astype(BF16), "dp", bit)
        total = pick(total, mine, 1) + arrived.astype(F32)
    return total[0]


def halves(values):
    size = lax.axis_size("dp")
    me = lax.axis_index("dp") & 1
    cut = values.reshape(values.shape[0], size // 2, 2, values.shape[1] // size)
    return pick(cut, 1 - me, 2), pick(cut, me, 2)


def body(
    tokens,
    seq_lengths,
    qkv_weight,
    qkv_bias,
    out_weight,
    gate_up_weight,
    down_weight,
    norm_gains,
    norm_shifts,
    cotangent,
):
    row_count, full_width = tokens.shape
    share = row_count // lax.axis_size("tensor")
    first_row = lax.axis_index("tensor") * share
    local_width = qkv_weight.shape[2]

    def own_rows(values):
        return lax.dynamic_slice_in_dim(values, first_row, share, 0)

    begins, *tables = positions(seq_lengths[0], row_count)
    normed, queries, keys, values = project(
        tokens, qkv_weight, qkv_bias, norm_gains[0], norm_shifts[0], tables
    )
    heads_out, logs = attend(begins, queries, keys, values)
    inputs_own = own_rows(tokens).astype(F32)
    cotangent_own = own_rows(cotangent).astype(F32)
    residual_own = inputs_own + sum_rows(heads_out, lambda left: dot(left, out_weight))
    unit_second, inverse_second = norm_parts(residual_own)
    second = spread_rows((unit_second * norm_gains[1] + norm_shifts[1]).astype(BF16))
    gate = dot(second, gate_up_weight[0])
    upper = dot(second, gate_up_weight[1])
    hidden_grad = jnp.einsum("td,fd->tf", cotangent, down_weight, preferred_element_type=F32)
    sigmoid_gate = jax.nn.sigmoid(gate)
    activated = gate * sigmoid_gate
    hidden = (activated * upper).astype(BF16)
    gate_grad = (
        hidden_grad * upper * (sigmoid_gate * (1.0 + gate * (1.0 - sigmoid_gate)))
    ).astype(BF16)
    upper_grad = (hidden_grad * activated).astype(BF16)

    cotangent_send, cotangent_keep = halves(cotangent)
    down_part = sum_parts(
        jnp.einsum("tf,tbc->bfc", hidden, cotangent_send, preferred_element_type=F32).astype(BF16),
        jnp.einsum("tf,tbc->bfc", hidden, cotangent_keep, preferred_element_type=F32),
        None,
    )
    second_send, second_keep = halves(second)

    def weight_part(send, keep, grads):
        return sum_parts(
            jnp.einsum("tbd,tf->bdf", send, grads, preferred_element_type=F32).astype(BF16),
            jnp.einsum("tbd,tf->bdf", keep, grads, preferred_element_type=F32),
            None,
        )

    gate_up_part = jnp.stack(
        [
            weight_part(second_send, second_keep, gate_grad),
            weight_part(second_send, second_keep, upper_grad),
        ]
    )
    branch_own = sum_rows(hidden, lambda left: dot(left, down_weight))
    block_out = (residual_own + branch_own).astype(BF16)

    def second_back(left):
        gates, uppers = jnp.split(left, 2, axis=1)
        return jnp.einsum(
            "tf,df->td", gates, gate_up_weight[0], preferred_element_type=F32
        ) + jnp.einsum("tf,df->td", uppers, gate_up_weight[1], preferred_element_type=F32)

    second_grad_own = sum_rows(jnp.concatenate([gate_grad, upper_grad], axis=1), second_back)
    residual_grad_own = cotangent_own + norm_back(
        unit_second, inverse_second, norm_gains[1], second_grad_own
    )
    residual_low = spread_rows(residual_grad_own.astype(BF16))
    gain_second = jnp.sum(second_grad_own * unit_second, axis=0)
    shift_second = jnp.sum(second_grad_own, axis=0)
    heads_grad = jnp.einsum(
        "td,ed->te", residual_low, out_weight, preferred_element_type=F32
    ).astype(BF16)
    low_send, low_keep = halves(residual_low)
    out_part = sum_parts(
        jnp.einsum("tf,tbc->bfc", heads_out, low_send, preferred_element_type=F32).astype(BF16),
        jnp.einsum("tf,tbc->bfc", heads_out, low_keep, preferred_element_type=F32),
        None,
    )
    projected_low = attend_back(begins, queries, keys, values, heads_grad, logs, tables)
    normed_send, normed_keep = halves(normed)
    qkv_part = jnp.stack([weight_part(normed_send, normed_keep, g) for g in projected_low])
    bias_local = jnp.stack([jnp.sum(g, axis=0, dtype=F32) for g in projected_low])

    def normed_back(left):
        return sum(
            jnp.einsum("te,de->td", piece, qkv_weight[j], preferred_element_type=F32)
            for j, piece in enumerate(jnp.split(left, 3, axis=1))
        )

    normed_grad_own = sum_rows(jnp.concatenate(projected_low, axis=1), normed_back)
    unit_first, inverse_first = norm_parts(inputs_own)
    input_grad = residual_grad_own + norm_back(
        unit_first, inverse_first, norm_gains[0], normed_grad_own
    )
    gain_first = jnp.sum(normed_grad_own * unit_first, axis=0)
    shift_first = jnp.sum(normed_grad_own, axis=0)
    bias_placed = lax.dynamic_update_slice(
        jnp.zeros((3, full_width), F32),
        bias_local,
        (0, lax.axis_index("tensor") * local_width),
    )
    gains_grad, shifts_grad, bias_grad = lax.psum(
        (jnp.stack([gain_first, gain_second]), jnp.stack([shift_first, shift_second]), bias_placed),
        ("dp", "tensor"),
    )
    return (
        block_out,
        input_grad,
        qkv_part,
        bias_grad,
        out_part,
        gate_up_part,
        down_part,
        gains_grad,
        shifts_grad,
    )


def solution(mesh):
    return jax.shard_map(
        body,
        mesh=mesh,
        in_specs=(
            P("dp", None),
            P("dp", None),
            P(None, None, "tensor"),
            P(None, "tensor"),
            P("tensor", None),
            P(None, None, "tensor"),
            P("tensor", None),
            P(),
            P(),
            P("dp", None),
        ),
        out_specs=(
            P(("dp", "tensor"), None),
            P(("dp", "tensor"), None),
            P(None, "dp", "tensor"),
            P(),
            P("tensor", "dp"),
            P(None, "dp", "tensor"),
            P("tensor", "dp"),
            P(),
            P(),
        ),
        check_vma=False,
    )
```

```python
import functools

import jax
import jax.numpy as jnp
from jax import lax
from jax.experimental import pallas as pl
from jax.experimental.pallas import tpu as pltpu
from jax.sharding import PartitionSpec as P

HD = 64
SEQ_MAX = 512
BQ = 256
F32 = jnp.float32
BF16 = jnp.bfloat16
LOG2E = 1.4426950408889634
VMEM_LIMIT = 60 * 1024 * 1024


def norm_parts(values):
    centred = values - jnp.mean(values, axis=-1, keepdims=True)
    inverse = lax.rsqrt(jnp.mean(centred * centred, axis=-1, keepdims=True) + 1e-05)
    return (centred * inverse, inverse)


def norm_back(unit, inverse, gain_row, grad_rows):
    scaled = grad_rows * gain_row
    return inverse * (
        scaled
        - jnp.mean(scaled, axis=-1, keepdims=True)
        - unit * jnp.mean(scaled * unit, axis=-1, keepdims=True)
    )


def positions(lengths, row_count):
    indices = jnp.arange(row_count, dtype=jnp.int32)
    count = lengths.shape[0]
    order = jnp.arange(count, dtype=jnp.int32)
    ends_at = jnp.sum(jnp.where(order[:, None] <= order[None, :], lengths[:, None], 0), axis=0)
    passed = indices[:, None] >= ends_at[None, :]
    begins = jnp.sum(jnp.where(passed, lengths[None, :], 0), axis=1, dtype=jnp.int32)
    places = (indices - begins).astype(F32)
    half = HD // 8
    lane = jnp.arange(128, dtype=jnp.int32) % HD
    rates = 10000.0 ** (-((lane % half).astype(F32) / half))
    angles = places[:, None] * rates[None, :]
    cosine, sine = jnp.cos(angles), jnp.sin(angles)
    turn = jnp.where(lane < 2 * half, cosine, 1.0)
    ahead = jnp.where(lane < half, -sine, 0.0)
    behind = jnp.where((lane >= half) & (lane < 2 * half), sine, 0.0)
    return begins, turn, ahead, behind


def turned(values, turn, ahead, behind):
    half = HD // 8
    width = values.shape[1]
    times = width // turn.shape[1]

    def wide(table):
        return jnp.concatenate([table] * times, axis=1) if times > 1 else table

    return (
        values * wide(turn)
        + pltpu.roll(values, width - half, 1) * wide(ahead)
        + pltpu.roll(values, half, 1) * wide(behind)
    )


def qkv_kernel(x_ref, w_ref, b_ref, g_ref, s_ref, c_ref, a_ref, h_ref, n_ref, q_ref, k_ref, v_ref):
    unit, _ = norm_parts(x_ref[...].astype(F32))
    normed = (unit * g_ref[...] + s_ref[...]).astype(BF16)
    n_ref[...] = normed
    for j, out in enumerate((q_ref, k_ref, v_ref)):
        got = jnp.dot(normed, w_ref[j], preferred_element_type=F32) + b_ref[j : j + 1, :]
        if j < 2:
            got = turned(got, c_ref[...], a_ref[...], h_ref[...])
        out[...] = got.astype(BF16)


def project(tokens, weight, bias, gain, shift, tables):
    rows, full = tokens.shape
    width = weight.shape[2]
    block = min(256, rows)

    def whole(*dims):
        return pl.BlockSpec(dims, lambda i: (0,) * len(dims))

    def by_row(columns):
        return pl.BlockSpec((block, columns), lambda i: (i, 0))

    return pl.pallas_call(
        qkv_kernel,
        name="project",
        grid=(rows // block,),
        in_specs=[
            by_row(full),
            whole(3, full, width),
            whole(3, width),
            whole(1, full),
            whole(1, full),
            by_row(128),
            by_row(128),
            by_row(128),
        ],
        out_specs=[by_row(full), by_row(width), by_row(width), by_row(width)],
        out_shape=[jax.ShapeDtypeStruct((rows, full), BF16)]
        + [jax.ShapeDtypeStruct((rows, width), BF16)] * 3,
        compiler_params=pltpu.CompilerParams(vmem_limit_bytes=VMEM_LIMIT),
        cost_estimate=pl.CostEstimate(flops=0, bytes_accessed=0, transcendentals=0),
    )(tokens, weight, bias.astype(F32), gain[None], shift[None], *tables)


def spans(step, blocks):
    most = SEQ_MAX // BQ + 1
    forms = []
    for at in range(min(most - 1, blocks)):
        forms.append((step == at, 0, (at + 1) * BQ))
    if blocks >= most:
        first = pl.multiple_of((step - (most - 1)) * BQ, BQ)
        forms.append((step >= most - 1, first, most * BQ))
    return forms


def allowed_bias(begin_row, first, count, step):
    key_at = first + lax.broadcasted_iota(jnp.int32, (count, BQ), 0)
    query_at = step * BQ + lax.broadcasted_iota(jnp.int32, (count, BQ), 1)
    return jnp.where((key_at >= begin_row) & (key_at <= query_at), 0.0, -1e30)


def over_rows(left, right):
    return lax.dot_general(left, right, (((0,), (0,)), ((), ())), preferred_element_type=F32)


def over_columns(left, right):
    return lax.dot_general(left, right, (((1,), (1,)), ((), ())), preferred_element_type=F32)


def attend_kernel(blocks, begin_ref, q_ref, k_ref, v_ref, o_ref, l_ref):
    step = pl.program_id(1)
    factor = HD**-0.5 * LOG2E

    def one(first, count):
        bias = allowed_bias(begin_ref[...], first, count, step)
        rows = pl.ds(first, count)
        parts = []
        for head in range(2):
            lanes = slice(head * HD, (head + 1) * HD)
            scores = over_columns(k_ref[rows, lanes], q_ref[:, lanes]) * factor + bias
            top = jnp.max(scores, axis=0, keepdims=True)
            probs = jnp.exp2(scores - top)
            total = jnp.sum(probs, axis=0, keepdims=True)
            got = over_rows(v_ref[rows, lanes], probs.astype(BF16))
            parts.append(got * (1.0 / total))
            l_ref[head] = top + jnp.log2(total)
        o_ref[...] = jnp.concatenate(parts, axis=0).T.astype(BF16)

    for condition, first, count in spans(step, blocks):
        pl.when(condition)(functools.partial(one, first, count))


def attend(begins, queries, keys, values):
    rows, width = queries.shape
    blocks = rows // BQ
    return pl.pallas_call(
        functools.partial(attend_kernel, blocks),
        name="attend",
        grid=(width // 128, blocks),
        in_specs=[
            pl.BlockSpec((1, BQ), lambda h, i: (0, i)),
            pl.BlockSpec((BQ, 128), lambda h, i: (i, h)),
            pl.BlockSpec((rows, 128), lambda h, i: (0, h)),
            pl.BlockSpec((rows, 128), lambda h, i: (0, h)),
        ],
        out_specs=[
            pl.BlockSpec((BQ, 128), lambda h, i: (i, h)),
            pl.BlockSpec((2, 1, BQ), lambda h, i: (h, 0, i)),
        ],
        out_shape=[
            jax.ShapeDtypeStruct((rows, width), BF16),
            jax.ShapeDtypeStruct((width // HD, 1, rows), F32),
        ],
        compiler_params=pltpu.CompilerParams(vmem_limit_bytes=VMEM_LIMIT),
        cost_estimate=pl.CostEstimate(flops=0, bytes_accessed=0, transcendentals=0),
    )(begins[None], queries, keys, values)


def attend_back_kernel(
    blocks, begin_ref, q_ref, k_ref, v_ref, g_ref, l_ref, cq_ref, aq_ref, hq_ref, c_ref, a_ref, h_ref,
    dq_ref, dk_ref, dv_ref, sum_k, sum_v,
):
    step = pl.program_id(1)
    scale = HD**-0.5
    factor = scale * LOG2E

    @pl.when(step == 0)
    def _():
        sum_k[...] = jnp.zeros_like(sum_k)
        sum_v[...] = jnp.zeros_like(sum_v)

    def one(first, count):
        bias = allowed_bias(begin_ref[...], first, count, step)
        rows = pl.ds(first, count)
        dq, dk, dv = [], [], []
        for head in range(2):
            lanes = slice(head * HD, (head + 1) * HD)
            query, key, value, grad = q_ref[:, lanes], k_ref[rows, lanes], v_ref[rows, lanes], g_ref[:, lanes]
            probs = jnp.exp2(over_columns(key, query) * factor + bias - l_ref[head])
            weighed = probs * over_columns(value, grad)
            inner = jnp.sum(weighed, axis=0, keepdims=True)
            score_grad = (weighed - probs * inner).astype(BF16)
            dv.append(jnp.dot(probs.astype(BF16), grad, preferred_element_type=F32))
            dk.append(jnp.dot(score_grad, query, preferred_element_type=F32))
            dq.append(over_rows(key, score_grad))
        sum_k[rows, :] += jnp.concatenate(dk, axis=1)
        sum_v[rows, :] += jnp.concatenate(dv, axis=1)
        query_grad = jnp.concatenate(dq, axis=0).T * scale
        dq_ref[...] = turned(query_grad, cq_ref[...], -aq_ref[...], -hq_ref[...]).astype(BF16)

    for condition, first, count in spans(step, blocks):
        pl.when(condition)(functools.partial(one, first, count))

    @pl.when(step == blocks - 1)
    def _():
        dk_ref[...] = turned(sum_k[...] * scale, c_ref[...], -a_ref[...], -h_ref[...]).astype(BF16)
        dv_ref[...] = sum_v[...].astype(BF16)


def attend_back(begins, queries, keys, values, grads, logs, tables):
    rows, width = queries.shape
    blocks = rows // BQ
    part = pl.BlockSpec((BQ, 128), lambda h, i: (i, h))
    column = pl.BlockSpec((rows, 128), lambda h, i: (0, h))
    return pl.pallas_call(
        functools.partial(attend_back_kernel, blocks),
        name="attend_back",
        grid=(width // 128, blocks),
        in_specs=[
            pl.BlockSpec((1, BQ), lambda h, i: (0, i)),
            part,
            column,
            column,
            part,
            pl.BlockSpec((2, 1, BQ), lambda h, i: (h, 0, i)),
        ]
        + [pl.BlockSpec((BQ, 128), lambda h, i: (i, 0))] * 3
        + [pl.BlockSpec((rows, 128), lambda h, i: (0, 0))] * 3,
        out_specs=[part, column, column],
        out_shape=[jax.ShapeDtypeStruct((rows, width), BF16)] * 3,
        scratch_shapes=[pltpu.VMEM((rows, 128), F32)] * 2,
        compiler_params=pltpu.CompilerParams(vmem_limit_bytes=VMEM_LIMIT),
        cost_estimate=pl.CostEstimate(flops=0, bytes_accessed=0, transcendentals=0),
    )(begins[None], queries, keys, values, grads, logs, *tables, *tables)


ANY = pl.BlockSpec(memory_space=pl.ANY)


def call(name, kernel, marks, grid, ins, in_specs, outs, out_specs, after=(), flops=0, moved=0, scratch=()):
    given, waits = len(ins), len(after)

    def inner(mark, *refs):
        kernel(mark, *refs[:given], *refs[given + waits :])

    return pl.pallas_call(
        inner,
        grid_spec=pltpu.PrefetchScalarGridSpec(
            num_scalar_prefetch=1,
            grid=grid,
            in_specs=list(in_specs) + [ANY] * waits,
            out_specs=out_specs,
            scratch_shapes=scratch,
        ),
        out_shape=outs,
        name=name,
        compiler_params=pltpu.CompilerParams(vmem_limit_bytes=VMEM_LIMIT),
        cost_estimate=pl.CostEstimate(flops=0, bytes_accessed=0, transcendentals=0),
    )(marks, *ins, *after)


def fixed(*dims):
    return pl.BlockSpec(dims, lambda *_: (0,) * len(dims))


def shape(dims, kind):
    return jax.ShapeDtypeStruct(dims, kind)


def pick(values, at, axis):
    return lax.dynamic_index_in_dim(values, at, axis, keepdims=False)


def swap(values, axis, bit):
    size = lax.axis_size(axis)
    return lax.ppermute(values, axis, [(i, i ^ (1 << bit)) for i in range(size)])


CORE, CHIP, DP = 0, 1, 2


def rows_product(marks, lefts, weight, flipped, arrived=None, after=()):
    rows, depth = lefts[0].shape
    share = rows // 4
    width = weight.shape[-2] if flipped else weight.shape[-1]
    tile = 256
    count = len(lefts)
    keep = arrived is not None

    def kernel(mark, *refs):
        total = 0.0
        for j in range(count):
            left = refs[j][...].reshape(2 * share, depth)
            if flipped:
                total += over_columns(left, refs[count][j])
            else:
                total += jnp.dot(left, refs[count][...], preferred_element_type=F32)
        total = total.reshape(2, share, tile)
        if keep:
            total = total + refs[count + 1][...].astype(F32)
            first = mark[CHIP] == 0
            refs[-2][...] = jnp.where(first, total[1], total[0]).astype(BF16)
            refs[-1][...] = jnp.where(first, total[0], total[1])
        else:
            refs[-1][...] = total.astype(BF16)

    def of_core(i, mark):
        return (0, mark[CORE] if keep else 1 - mark[CORE], 0, 0)

    in_specs = [pl.BlockSpec((2, 1, share, depth), of_core)] * count
    if flipped:
        in_specs.append(pl.BlockSpec((count, tile, depth), lambda i, mark: (0, i, 0)))
    else:
        in_specs.append(pl.BlockSpec((depth, tile), lambda i, mark: (0, i)))
    ins = [left.reshape(2, 2, share, depth) for left in lefts] + [weight]
    pair = pl.BlockSpec((2, share, tile), lambda i, mark: (0, 0, i))
    one = pl.BlockSpec((share, tile), lambda i, mark: (0, i))
    if keep:
        ins.append(arrived)
        in_specs.append(pair)
        outs, out_specs = [shape((share, width), BF16), shape((share, width), F32)], [one, one]
    else:
        outs, out_specs = shape((2, share, width), BF16), pair
    return call(
        "rows_keep" if keep else "rows_send", kernel, marks, (width // tile,), ins, in_specs, outs, out_specs, after,
        flops=4 * share * depth * width * count, moved=2 * depth * width * count,
    )


def norm_rows(marks, tokens, kept, arrived, gain, shift, after=()):
    share, full = kept.shape
    block = min(128, share)
    steps = share // block

    def kernel(mark, x_ref, k_ref, a_ref, g_ref, s_ref, r_ref, n_ref):
        residual = x_ref[...].astype(F32) + (k_ref[...] + a_ref[...].astype(F32))
        unit, _ = norm_parts(residual)
        r_ref[...] = residual
        n_ref[...] = (unit * g_ref[...] + s_ref[...]).astype(BF16)

    rows = pl.BlockSpec((block, full), lambda i, mark: (i, 0))
    mine = pl.BlockSpec((block, full), lambda i, mark: ((2 * mark[CHIP] + mark[CORE]) * steps + i, 0))
    return call(
        "norm_rows", kernel, marks, (steps,), [tokens, kept, arrived, gain[None], shift[None]],
        [mine, rows, rows, fixed(1, full), fixed(1, full)],
        [shape((share, full), F32), shape((share, full), BF16)], [rows, rows], after,
        flops=10 * share * full, moved=14 * share * full,
    )


def norm_back_rows(marks, values, base, kept, arrived, gain, after=()):
    share, full = kept.shape
    block = min(128, share)
    steps = share // block

    def kernel(mark, x_ref, b_ref, k_ref, a_ref, g_ref, o_ref, l_ref, s_ref):
        unit, inverse = norm_parts(x_ref[...].astype(F32))
        grad = k_ref[...] + a_ref[...].astype(F32)
        out = b_ref[...].astype(F32) + norm_back(unit, inverse, g_ref[...], grad)
        o_ref[...] = out
        l_ref[...] = out.astype(BF16)

        @pl.when(pl.program_id(0) == 0)
        def _():
            s_ref[...] = jnp.zeros_like(s_ref)

        s_ref[0:1, :] += jnp.sum(grad * unit, axis=0, keepdims=True)
        s_ref[1:2, :] += jnp.sum(grad, axis=0, keepdims=True)

    rows = pl.BlockSpec((block, full), lambda i, mark: (i, 0))
    mine = pl.BlockSpec((block, full), lambda i, mark: ((2 * mark[CHIP] + mark[CORE]) * steps + i, 0))

    def where(of):
        return rows if of.shape[0] == share else mine

    return call(
        "norm_back_rows", kernel, marks, (steps,), [values, base, kept, arrived, gain[None]],
        [where(values), where(base), rows, rows, fixed(1, full)],
        [shape((share, full), F32), shape((share, full), BF16), shape((2, full), F32)],
        [rows, rows, fixed(2, full)], after,
        flops=20 * share * full, moved=18 * share * full,
    )


def spread(own):
    chip = swap(own, "tensor", 1)
    core = swap(own, "tensor", 0)
    return own, core, chip, swap(chip, "tensor", 0)


def gather_into(mark, parts, whole):
    share = parts[0].shape[0]
    for at, part in enumerate(parts):
        core = mark[CORE] if at % 2 == 0 else 1 - mark[CORE]
        chip = mark[CHIP] if at < 2 else 1 - mark[CHIP]
        first = pl.multiple_of((2 * chip + core) * share, share)
        whole[pl.ds(first, share), :] = part[...]


def hidden_back(marks, cotangent, weight, after=()):
    rows, full = cotangent.shape
    inner = weight.shape[0]
    block = min(256, rows)

    def kernel(mark, c_ref, w_ref, o_ref):
        o_ref[...] = over_columns(c_ref[...], w_ref[...]).astype(BF16)

    return call(
        "hidden_back", kernel, marks, (rows // block,), [cotangent, weight],
        [pl.BlockSpec((block, full), lambda i, mark: (i, 0)), fixed(inner, full)],
        shape((rows, inner), BF16), pl.BlockSpec((block, inner), lambda i, mark: (i, 0)), after,
        flops=2 * rows * full * inner, moved=2 * (rows * full + inner * full + rows * inner),
    )


def gate_up(marks, parts, weight, hidden_grad, after=()):
    share, full = parts[0].shape
    rows = 4 * share
    inner = weight.shape[2]
    tile = 128
    block = min(256, rows)

    def kernel(mark, p0, p1, p2, p3, w_ref, h_ref, second, hidden, hidden_t, gate_grad, up_grad):
        @pl.when(pl.program_id(0) == 0)
        def _():
            gather_into(mark, (p0, p1, p2, p3), second)

        both = jnp.concatenate([w_ref[0], w_ref[1]], axis=1)
        for first in range(0, rows, block):
            at = pl.ds(first, block)
            got = jnp.dot(second[at, :], both, preferred_element_type=F32)
            gate, up = got[:, :tile], got[:, tile:]
            sigmoid = 1.0 / (1.0 + jnp.exp(-gate))
            active = gate * sigmoid
            made = (active * up).astype(BF16)
            hidden[at, :] = made
            hidden_t[:, at] = made.T
            grad = h_ref[at, :].astype(F32)
            gate_grad[at, :] = (grad * up * (sigmoid * (1.0 + gate * (1.0 - sigmoid)))).astype(BF16)
            up_grad[at, :] = (grad * active).astype(BF16)

    column = pl.BlockSpec((rows, tile), lambda i, mark: (0, i))
    return call(
        "gate_up", kernel, marks, (inner // tile,), [*parts, weight, hidden_grad],
        [fixed(share, full)] * 4 + [pl.BlockSpec((2, full, tile), lambda i, mark: (0, 0, i)), column],
        [
            shape((rows, full), BF16), shape((rows, inner), BF16), shape((inner, rows), BF16),
            shape((rows, inner), BF16), shape((rows, inner), BF16),
        ],
        [fixed(rows, full), column, pl.BlockSpec((tile, rows), lambda i, mark: (i, 0)), column, column],
        after,
        flops=4 * rows * full * inner, moved=2 * (4 * full * inner + 2 * rows * full + 5 * rows * inner),
    )


def heads_back(marks, parts, weight, after=()):
    share, full = parts[0].shape
    rows = 4 * share
    width = weight.shape[0]

    def kernel(mark, p0, p1, p2, p3, w_ref, low, grad):
        @pl.when(pl.program_id(0) == 0)
        def _():
            gather_into(mark, (p0, p1, p2, p3), low)

        at = pl.ds(pl.multiple_of(pl.program_id(0) * share, share), share)
        grad[...] = over_columns(low[at, :], w_ref[...]).astype(BF16)

    return call(
        "heads_back", kernel, marks, (4,), [*parts, weight], [fixed(share, full)] * 4 + [fixed(width, full)],
        [shape((rows, full), BF16), shape((rows, width), BF16)],
        [fixed(rows, full), pl.BlockSpec((share, width), lambda i, mark: (i, 0))], after,
        flops=2 * rows * full * width, moved=2 * (2 * rows * full + full * width + rows * width),
    )


def bit_of(mark, bit):
    return (mark[DP] >> bit) & 1


def block_at(mark, order, flips, j):
    rest = len(order) - len(flips)
    index = 0
    for at, bit in enumerate(order):
        if at < len(flips):
            value = bit_of(mark, bit)
            value = 1 - value if flips[at] else value
        else:
            value = (j >> (rest - 1 - (at - len(flips)))) & 1
        index = index + (value << bit)
    return index


def weight_send(marks, order, columns, other, turned_out, after=()):
    size = lax.axis_size("dp")
    rows, full = columns.shape
    block = full // size
    count = size // 2
    dims = (other.shape[0], block) if turned_out else (block, other.shape[1])

    def kernel(mark, c_ref, o_ref, out):
        if turned_out:
            got = jnp.dot(o_ref[...], c_ref[...], preferred_element_type=F32)
        else:
            got = over_rows(c_ref[...], o_ref[...])
        out[0] = got.astype(BF16)

    return call(
        "weight_send", kernel, marks, (count,), [columns, other],
        [
            pl.BlockSpec((rows, block), lambda j, mark: (0, block_at(mark, order, (True,), j))),
            fixed(*other.shape),
        ],
        shape((count, *dims), BF16), pl.BlockSpec((1, *dims), lambda j, mark: (j, 0, 0)), after,
        flops=2 * rows * dims[0] * dims[1] * count,
        moved=rows * full + 2 * other.size + 2 * count * dims[0] * dims[1],
    )


def weight_keep(marks, order, columns, other, turned_out, arrived, after=()):
    size = lax.axis_size("dp")
    rows, full = columns.shape
    block = full // size
    half = size // 4
    dims = (other.shape[0], block) if turned_out else (block, other.shape[1])

    def kernel(mark, c_ref, o_ref, a_ref, send, keep):
        if turned_out:
            got = jnp.dot(o_ref[...], c_ref[...], preferred_element_type=F32)
        else:
            got = over_rows(c_ref[...], o_ref[...])
        got = got + a_ref[0].astype(F32)

        @pl.when(pl.program_id(0) < half)
        def _():
            send[0] = got.astype(BF16)

        @pl.when(pl.program_id(0) >= half)
        def _():
            keep[0] = got

    def block_for(j, mark):
        away = block_at(mark, order, (False, True), j)
        here = block_at(mark, order, (False, False), j - half)
        return jnp.where(j < half, away, here)

    def arrived_for(j, mark):
        mine = bit_of(mark, order[1])
        return jnp.where(j < half, (1 - mine) * half + j, mine * half + j - half)

    return call(
        "weight_keep", kernel, marks, (2 * half,), [columns, other, arrived],
        [
            pl.BlockSpec((rows, block), lambda j, mark: (0, block_for(j, mark))),
            fixed(*other.shape),
            pl.BlockSpec((1, *dims), lambda j, mark: (arrived_for(j, mark), 0, 0)),
        ],
        [shape((half, *dims), BF16), shape((half, *dims), F32)],
        [
            pl.BlockSpec((1, *dims), lambda j, mark: (jnp.minimum(j, half - 1), 0, 0)),
            pl.BlockSpec((1, *dims), lambda j, mark: (jnp.maximum(j - half, 0), 0, 0)),
        ],
        after,
        flops=2 * rows * dims[0] * dims[1] * 2 * half,
        moved=rows * full + 2 * other.size + 8 * half * dims[0] * dims[1],
    )


def finish(order, keep, arrived):
    me = lax.axis_index("dp")
    total = keep + arrived.astype(F32)
    for bit in order[2:]:
        mine = (me >> bit) & 1
        total = total.reshape(2, -1, *total.shape[1:])
        arrived = swap(pick(total, 1 - mine, 0).astype(BF16), "dp", bit)
        total = pick(total, mine, 0) + arrived.astype(F32)
    return total[0]


def plain_weight(columns, other, turned_out):
    if turned_out:
        got = jnp.einsum("fr,rd->fd", other, columns, preferred_element_type=F32)
    else:
        got = jnp.einsum("rd,rf->df", columns, other, preferred_element_type=F32)
    return lax.psum_scatter(
        got.astype(BF16), "dp", scatter_dimension=1 if turned_out else 0, tiled=True
    ).astype(F32)


def everywhere(values):
    for axis in ("dp", "tensor"):
        for bit in range(lax.axis_size(axis).bit_length() - 1):
            values = values + swap(values, axis, bit)
    return values


def body(
    tokens,
    seq_lengths,
    qkv_weight,
    qkv_bias,
    out_weight,
    gate_up_weight,
    down_weight,
    norm_gains,
    norm_shifts,
    cotangent,
):
    row_count, full_width = tokens.shape
    local_width = qkv_weight.shape[2]
    tensor_at, dp_at, dp_size = lax.axis_index("tensor"), lax.axis_index("dp"), lax.axis_size("dp")
    marks = jnp.stack([tensor_at & 1, tensor_at >> 1, dp_at]).astype(jnp.int32)
    bits = dp_size.bit_length() - 1
    x_first = tuple(range(bits))
    z_first = (1, 0) + x_first[2:]
    fine = (full_width // dp_size) % 128 == 0

    def send(order, columns, other, turned_out, after):
        if not fine:
            return columns
        return weight_send(marks, order, columns, other, turned_out, after)

    def keep(order, columns, other, turned_out, sent, after):
        if not fine:
            return columns, None
        return weight_keep(
            marks, order, columns, other, turned_out, swap(sent, "dp", order[0]), after
        )

    def total(order, columns, other, turned_out, kept):
        if not fine:
            return plain_weight(columns, other, turned_out)
        return finish(order, kept[1], swap(kept[0], "dp", order[1]))

    begins, *tables = positions(seq_lengths[0], row_count)
    normed, queries, keys, values = project(
        tokens, qkv_weight, qkv_bias, norm_gains[0], norm_shifts[0], tables
    )
    heads_out, logs = attend(begins, queries, keys, values)
    sent = rows_product(marks, [heads_out], out_weight, False)
    to_chip, own = rows_product(marks, [heads_out], out_weight, False, swap(sent, "tensor", 0))
    hidden_grad = hidden_back(marks, cotangent, down_weight, [own])
    residual, second_own = norm_rows(
        marks, tokens, own, swap(to_chip, "tensor", 1), norm_gains[1], norm_shifts[1], [hidden_grad]
    )
    second, hidden, hidden_t, gate_grad, up_grad = gate_up(
        marks, spread(second_own), gate_up_weight, hidden_grad
    )
    down_sent = send(x_first, cotangent, hidden_t, True, [])
    second_sent = rows_product(marks, [gate_grad, up_grad], gate_up_weight, True, None, [down_sent])
    up_sent = send(x_first, second, up_grad, False, [second_sent])
    to_chip, own = rows_product(
        marks, [gate_grad, up_grad], gate_up_weight, True, swap(second_sent, "tensor", 0), [up_sent]
    )
    gate_sent = send(z_first, second, gate_grad, False, [own])
    branch_sent = rows_product(marks, [hidden], down_weight, False, None, [gate_sent])
    branch_to_chip, branch_own = rows_product(
        marks, [hidden], down_weight, False, swap(branch_sent, "tensor", 0), [gate_sent]
    )
    residual_grad, residual_low_own, second_sums = norm_back_rows(
        marks, residual, cotangent, own, swap(to_chip, "tensor", 1), norm_gains[1], [branch_own]
    )
    block_out = (
        residual + branch_own + swap(branch_to_chip, "tensor", 1).astype(F32)
    ).astype(BF16)
    down_kept = keep(x_first, cotangent, hidden_t, True, down_sent, [residual_low_own])
    residual_low, heads_grad = heads_back(
        marks, spread(residual_low_own), out_weight, [down_kept[0]]
    )
    heads_t = heads_out.T
    out_sent = send(x_first, residual_low, heads_t, True, [heads_grad])
    projected_low = attend_back(begins, queries, keys, values, heads_grad, logs, tables)
    gate_kept = keep(z_first, second, gate_grad, False, gate_sent, [projected_low[0]])
    qkv_sent = []
    before = gate_kept[0]
    for grads in projected_low:
        before = send(x_first, normed, grads, False, [before])
        qkv_sent.append(before)
    normed_sent = rows_product(marks, projected_low, qkv_weight, True, None, [before])
    up_kept = keep(x_first, second, up_grad, False, up_sent, [normed_sent])
    to_chip, own = rows_product(
        marks, projected_low, qkv_weight, True, swap(normed_sent, "tensor", 0), [normed_sent]
    )
    input_grad, _, first_sums = norm_back_rows(
        marks, tokens, residual_grad, own, swap(to_chip, "tensor", 1), norm_gains[0], [up_kept[0]]
    )
    bias_local = jnp.stack([jnp.sum(g, axis=0, dtype=F32) for g in projected_low])
    bias_placed = lax.dynamic_update_slice(
        jnp.zeros((3, full_width), F32), bias_local, (0, tensor_at * local_width)
    )
    sums = everywhere(jnp.concatenate([first_sums, second_sums, bias_placed], axis=0))
    out_kept = keep(x_first, residual_low, heads_t, True, out_sent, [input_grad])
    qkv_kept = []
    before = out_kept[0]
    for grads, sent in zip(projected_low, qkv_sent):
        kept = keep(x_first, normed, grads, False, sent, [before])
        before = kept[0]
        qkv_kept.append(kept)
    return (
        block_out,
        input_grad,
        jnp.stack(
            [total(x_first, normed, g, False, k) for g, k in zip(projected_low, qkv_kept)]
        ),
        sums[4:7],
        total(x_first, residual_low, heads_t, True, out_kept),
        jnp.stack(
            [
                total(z_first, second, gate_grad, False, gate_kept),
                total(x_first, second, up_grad, False, up_kept),
            ]
        ),
        total(x_first, cotangent, hidden_t, True, down_kept),
        jnp.stack([sums[0], sums[2]]),
        jnp.stack([sums[1], sums[3]]),
    )


def solution(mesh):
    return jax.shard_map(
        body,
        mesh=mesh,
        in_specs=(
            P("dp", None),
            P("dp", None),
            P(None, None, "tensor"),
            P(None, "tensor"),
            P("tensor", None),
            P(None, None, "tensor"),
            P("tensor", None),
            P(),
            P(),
            P("dp", None),
        ),
        out_specs=(
            P(("dp", "tensor"), None),
            P(("dp", "tensor"), None),
            P(None, "dp", "tensor"),
            P(),
            P("tensor", "dp"),
            P(None, "dp", "tensor"),
            P("tensor", "dp"),
            P(),
            P(),
        ),
        check_vma=False,
    )
```

```python
import functools

import jax
import jax.numpy as jnp
from jax import lax
from jax.experimental import pallas as pl
from jax.experimental.pallas import tpu as pltpu
from jax.sharding import PartitionSpec as P

HD = 64
SEQ_MAX = 512
BQ = 256
F32 = jnp.float32
BF16 = jnp.bfloat16
LOG2E = 1.4426950408889634
VMEM_LIMIT = 60 * 1024 * 1024


def norm_parts(values):
    centred = values - jnp.mean(values, axis=-1, keepdims=True)
    inverse = lax.rsqrt(jnp.mean(centred * centred, axis=-1, keepdims=True) + 1e-05)
    return (centred * inverse, inverse)


def norm_back(unit, inverse, gain_row, grad_rows):
    scaled = grad_rows * gain_row
    return inverse * (
        scaled
        - jnp.mean(scaled, axis=-1, keepdims=True)
        - unit * jnp.mean(scaled * unit, axis=-1, keepdims=True)
    )


def positions(lengths, row_count):
    indices = jnp.arange(row_count, dtype=jnp.int32)
    count = lengths.shape[0]
    order = jnp.arange(count, dtype=jnp.int32)
    ends_at = jnp.sum(jnp.where(order[:, None] <= order[None, :], lengths[:, None], 0), axis=0)
    passed = indices[:, None] >= ends_at[None, :]
    begins = jnp.sum(jnp.where(passed, lengths[None, :], 0), axis=1, dtype=jnp.int32)
    places = (indices - begins).astype(F32)
    half = HD // 8
    lane = jnp.arange(128, dtype=jnp.int32) % HD
    rates = 10000.0 ** (-((lane % half).astype(F32) / half))
    angles = places[:, None] * rates[None, :]
    cosine, sine = jnp.cos(angles), jnp.sin(angles)
    turn = jnp.where(lane < 2 * half, cosine, 1.0)
    ahead = jnp.where(lane < half, -sine, 0.0)
    behind = jnp.where((lane >= half) & (lane < 2 * half), sine, 0.0)
    return begins, turn, ahead, behind


def turned(values, turn, ahead, behind):
    half = HD // 8
    width = values.shape[1]
    times = width // turn.shape[1]

    def wide(table):
        return jnp.concatenate([table] * times, axis=1) if times > 1 else table

    return (
        values * wide(turn)
        + pltpu.roll(values, width - half, 1) * wide(ahead)
        + pltpu.roll(values, half, 1) * wide(behind)
    )


def qkv_kernel(x_ref, w_ref, b_ref, g_ref, s_ref, c_ref, a_ref, h_ref, n_ref, q_ref, k_ref, v_ref):
    unit, _ = norm_parts(x_ref[...].astype(F32))
    normed = (unit * g_ref[...] + s_ref[...]).astype(BF16)
    n_ref[...] = normed
    for j, out in enumerate((q_ref, k_ref, v_ref)):
        got = jnp.dot(normed, w_ref[j], preferred_element_type=F32) + b_ref[j : j + 1, :]
        if j < 2:
            got = turned(got, c_ref[...], a_ref[...], h_ref[...])
        out[...] = got.astype(BF16)


def project(tokens, weight, bias, gain, shift, tables):
    rows, full = tokens.shape
    width = weight.shape[2]
    block = min(256, rows)

    def whole(*dims):
        return pl.BlockSpec(dims, lambda i: (0,) * len(dims))

    def by_row(columns):
        return pl.BlockSpec((block, columns), lambda i: (i, 0))

    return pl.pallas_call(
        qkv_kernel,
        name="project",
        grid=(rows // block,),
        in_specs=[
            by_row(full),
            whole(3, full, width),
            whole(3, width),
            whole(1, full),
            whole(1, full),
            by_row(128),
            by_row(128),
            by_row(128),
        ],
        out_specs=[by_row(full), by_row(width), by_row(width), by_row(width)],
        out_shape=[jax.ShapeDtypeStruct((rows, full), BF16)]
        + [jax.ShapeDtypeStruct((rows, width), BF16)] * 3,
        compiler_params=pltpu.CompilerParams(vmem_limit_bytes=VMEM_LIMIT),
        cost_estimate=pl.CostEstimate(flops=0, bytes_accessed=0, transcendentals=0),
    )(tokens, weight, bias.astype(F32), gain[None], shift[None], *tables)


def spans(step, blocks):
    most = SEQ_MAX // BQ + 1
    forms = []
    for at in range(min(most - 1, blocks)):
        forms.append((step == at, 0, (at + 1) * BQ))
    if blocks >= most:
        first = pl.multiple_of((step - (most - 1)) * BQ, BQ)
        forms.append((step >= most - 1, first, most * BQ))
    return forms


def allowed_bias(begin_row, first, count, step):
    key_at = first + lax.broadcasted_iota(jnp.int32, (count, BQ), 0)
    query_at = step * BQ + lax.broadcasted_iota(jnp.int32, (count, BQ), 1)
    return jnp.where((key_at >= begin_row) & (key_at <= query_at), 0.0, -1e30)


def over_rows(left, right):
    return lax.dot_general(left, right, (((0,), (0,)), ((), ())), preferred_element_type=F32)


def over_columns(left, right):
    return lax.dot_general(left, right, (((1,), (1,)), ((), ())), preferred_element_type=F32)


def attend_kernel(blocks, begin_ref, q_ref, k_ref, v_ref, o_ref, l_ref):
    step = pl.program_id(1)
    factor = HD**-0.5 * LOG2E

    def one(first, count):
        bias = allowed_bias(begin_ref[...], first, count, step)
        rows = pl.ds(first, count)
        parts = []
        for head in range(2):
            lanes = slice(head * HD, (head + 1) * HD)
            scores = over_columns(k_ref[rows, lanes], q_ref[:, lanes]) * factor + bias
            top = jnp.max(scores, axis=0, keepdims=True)
            probs = jnp.exp2(scores - top)
            total = jnp.sum(probs, axis=0, keepdims=True)
            got = over_rows(v_ref[rows, lanes], probs.astype(BF16))
            parts.append(got * (1.0 / total))
            l_ref[head] = top + jnp.log2(total)
        o_ref[...] = jnp.concatenate(parts, axis=0).T.astype(BF16)

    for condition, first, count in spans(step, blocks):
        pl.when(condition)(functools.partial(one, first, count))


def attend(begins, queries, keys, values):
    rows, width = queries.shape
    blocks = rows // BQ
    return pl.pallas_call(
        functools.partial(attend_kernel, blocks),
        name="attend",
        grid=(width // 128, blocks),
        in_specs=[
            pl.BlockSpec((1, BQ), lambda h, i: (0, i)),
            pl.BlockSpec((BQ, 128), lambda h, i: (i, h)),
            pl.BlockSpec((rows, 128), lambda h, i: (0, h)),
            pl.BlockSpec((rows, 128), lambda h, i: (0, h)),
        ],
        out_specs=[
            pl.BlockSpec((BQ, 128), lambda h, i: (i, h)),
            pl.BlockSpec((2, 1, BQ), lambda h, i: (h, 0, i)),
        ],
        out_shape=[
            jax.ShapeDtypeStruct((rows, width), BF16),
            jax.ShapeDtypeStruct((width // HD, 1, rows), F32),
        ],
        compiler_params=pltpu.CompilerParams(vmem_limit_bytes=VMEM_LIMIT),
        cost_estimate=pl.CostEstimate(flops=0, bytes_accessed=0, transcendentals=0),
    )(begins[None], queries, keys, values)


def attend_back_kernel(
    blocks, begin_ref, q_ref, k_ref, v_ref, g_ref, l_ref, cq_ref, aq_ref, hq_ref, c_ref, a_ref, h_ref,
    dq_ref, dk_ref, dv_ref, sum_k, sum_v,
):
    step = pl.program_id(1)
    scale = HD**-0.5
    factor = scale * LOG2E

    @pl.when(step == 0)
    def _():
        sum_k[...] = jnp.zeros_like(sum_k)
        sum_v[...] = jnp.zeros_like(sum_v)

    def one(first, count):
        bias = allowed_bias(begin_ref[...], first, count, step)
        rows = pl.ds(first, count)
        dq, dk, dv = [], [], []
        for head in range(2):
            lanes = slice(head * HD, (head + 1) * HD)
            query, key, value, grad = q_ref[:, lanes], k_ref[rows, lanes], v_ref[rows, lanes], g_ref[:, lanes]
            probs = jnp.exp2(over_columns(key, query) * factor + bias - l_ref[head])
            weighed = probs * over_columns(value, grad)
            inner = jnp.sum(weighed, axis=0, keepdims=True)
            score_grad = (weighed - probs * inner).astype(BF16)
            dv.append(jnp.dot(probs.astype(BF16), grad, preferred_element_type=F32))
            dk.append(jnp.dot(score_grad, query, preferred_element_type=F32))
            dq.append(over_rows(key, score_grad))
        sum_k[rows, :] += jnp.concatenate(dk, axis=1)
        sum_v[rows, :] += jnp.concatenate(dv, axis=1)
        query_grad = jnp.concatenate(dq, axis=0).T * scale
        dq_ref[...] = turned(query_grad, cq_ref[...], -aq_ref[...], -hq_ref[...]).astype(BF16)

    for condition, first, count in spans(step, blocks):
        pl.when(condition)(functools.partial(one, first, count))

    @pl.when(step == blocks - 1)
    def _():
        dk_ref[...] = turned(sum_k[...] * scale, c_ref[...], -a_ref[...], -h_ref[...]).astype(BF16)
        dv_ref[...] = sum_v[...].astype(BF16)


def attend_back(begins, queries, keys, values, grads, logs, tables):
    rows, width = queries.shape
    blocks = rows // BQ
    part = pl.BlockSpec((BQ, 128), lambda h, i: (i, h))
    column = pl.BlockSpec((rows, 128), lambda h, i: (0, h))
    return pl.pallas_call(
        functools.partial(attend_back_kernel, blocks),
        name="attend_back",
        grid=(width // 128, blocks),
        in_specs=[
            pl.BlockSpec((1, BQ), lambda h, i: (0, i)),
            part,
            column,
            column,
            part,
            pl.BlockSpec((2, 1, BQ), lambda h, i: (h, 0, i)),
        ]
        + [pl.BlockSpec((BQ, 128), lambda h, i: (i, 0))] * 3
        + [pl.BlockSpec((rows, 128), lambda h, i: (0, 0))] * 3,
        out_specs=[part, column, column],
        out_shape=[jax.ShapeDtypeStruct((rows, width), BF16)] * 3,
        scratch_shapes=[pltpu.VMEM((rows, 128), F32)] * 2,
        compiler_params=pltpu.CompilerParams(vmem_limit_bytes=VMEM_LIMIT),
        cost_estimate=pl.CostEstimate(flops=0, bytes_accessed=0, transcendentals=0),
    )(begins[None], queries, keys, values, grads, logs, *tables, *tables)


ANY = pl.BlockSpec(memory_space=pl.ANY)


def call(name, kernel, marks, grid, ins, in_specs, outs, out_specs, after=(), flops=0, moved=0, scratch=()):
    given, waits = len(ins), len(after)

    def inner(mark, *refs):
        kernel(mark, *refs[:given], *refs[given + waits :])

    return pl.pallas_call(
        inner,
        grid_spec=pltpu.PrefetchScalarGridSpec(
            num_scalar_prefetch=1,
            grid=grid,
            in_specs=list(in_specs) + [ANY] * waits,
            out_specs=out_specs,
            scratch_shapes=scratch,
        ),
        out_shape=outs,
        name=name,
        compiler_params=pltpu.CompilerParams(vmem_limit_bytes=VMEM_LIMIT),
        cost_estimate=pl.CostEstimate(flops=0, bytes_accessed=0, transcendentals=0),
    )(marks, *ins, *after)


def fixed(*dims):
    return pl.BlockSpec(dims, lambda *_: (0,) * len(dims))


def shape(dims, kind):
    return jax.ShapeDtypeStruct(dims, kind)


def pick(values, at, axis):
    return lax.dynamic_index_in_dim(values, at, axis, keepdims=False)


def swap(values, axis, bit):
    size = lax.axis_size(axis)
    return lax.ppermute(values, axis, [(i, i ^ (1 << bit)) for i in range(size)])


CORE, CHIP, DP = 0, 1, 2


def rows_product(marks, lefts, weight, flipped, arrived=None, after=()):
    rows, depth = lefts[0].shape
    share = rows // 4
    width = weight.shape[-2] if flipped else weight.shape[-1]
    tile = 256
    count = len(lefts)
    keep = arrived is not None

    def kernel(mark, *refs):
        total = 0.0
        for j in range(count):
            left = refs[j][...].reshape(2 * share, depth)
            if flipped:
                total += over_columns(left, refs[count][j])
            else:
                total += jnp.dot(left, refs[count][...], preferred_element_type=F32)
        total = total.reshape(2, share, tile)
        if keep:
            total = total + refs[count + 1][...].astype(F32)
            first = mark[CHIP] == 0
            refs[-2][...] = jnp.where(first, total[1], total[0]).astype(BF16)
            refs[-1][...] = jnp.where(first, total[0], total[1])
        else:
            refs[-1][...] = total.astype(BF16)

    def of_core(i, mark):
        return (0, mark[CORE] if keep else 1 - mark[CORE], 0, 0)

    in_specs = [pl.BlockSpec((2, 1, share, depth), of_core)] * count
    if flipped:
        in_specs.append(pl.BlockSpec((count, tile, depth), lambda i, mark: (0, i, 0)))
    else:
        in_specs.append(pl.BlockSpec((depth, tile), lambda i, mark: (0, i)))
    ins = [left.reshape(2, 2, share, depth) for left in lefts] + [weight]
    pair = pl.BlockSpec((2, share, tile), lambda i, mark: (0, 0, i))
    one = pl.BlockSpec((share, tile), lambda i, mark: (0, i))
    if keep:
        ins.append(arrived)
        in_specs.append(pair)
        outs, out_specs = [shape((share, width), BF16), shape((share, width), F32)], [one, one]
    else:
        outs, out_specs = shape((2, share, width), BF16), pair
    return call(
        "rows_keep" if keep else "rows_send", kernel, marks, (width // tile,), ins, in_specs, outs, out_specs, after,
        flops=4 * share * depth * width * count, moved=2 * depth * width * count,
    )


def norm_rows(marks, tokens, kept, arrived, gain, shift, after=()):
    share, full = kept.shape
    block = min(128, share)
    steps = share // block

    def kernel(mark, x_ref, k_ref, a_ref, g_ref, s_ref, r_ref, n_ref):
        residual = x_ref[...].astype(F32) + (k_ref[...] + a_ref[...].astype(F32))
        unit, _ = norm_parts(residual)
        r_ref[...] = residual
        n_ref[...] = (unit * g_ref[...] + s_ref[...]).astype(BF16)

    rows = pl.BlockSpec((block, full), lambda i, mark: (i, 0))
    mine = pl.BlockSpec((block, full), lambda i, mark: ((2 * mark[CHIP] + mark[CORE]) * steps + i, 0))
    return call(
        "norm_rows", kernel, marks, (steps,), [tokens, kept, arrived, gain[None], shift[None]],
        [mine, rows, rows, fixed(1, full), fixed(1, full)],
        [shape((share, full), F32), shape((share, full), BF16)], [rows, rows], after,
        flops=10 * share * full, moved=14 * share * full,
    )


def norm_back_rows(marks, values, base, kept, arrived, gain, after=()):
    share, full = kept.shape
    block = min(128, share)
    steps = share // block

    def kernel(mark, x_ref, b_ref, k_ref, a_ref, g_ref, o_ref, l_ref, s_ref):
        unit, inverse = norm_parts(x_ref[...].astype(F32))
        grad = k_ref[...] + a_ref[...].astype(F32)
        out = b_ref[...].astype(F32) + norm_back(unit, inverse, g_ref[...], grad)
        o_ref[...] = out
        l_ref[...] = out.astype(BF16)

        @pl.when(pl.program_id(0) == 0)
        def _():
            s_ref[...] = jnp.zeros_like(s_ref)

        s_ref[0:1, :] += jnp.sum(grad * unit, axis=0, keepdims=True)
        s_ref[1:2, :] += jnp.sum(grad, axis=0, keepdims=True)

    rows = pl.BlockSpec((block, full), lambda i, mark: (i, 0))
    mine = pl.BlockSpec((block, full), lambda i, mark: ((2 * mark[CHIP] + mark[CORE]) * steps + i, 0))

    def where(of):
        return rows if of.shape[0] == share else mine

    return call(
        "norm_back_rows", kernel, marks, (steps,), [values, base, kept, arrived, gain[None]],
        [where(values), where(base), rows, rows, fixed(1, full)],
        [shape((share, full), F32), shape((share, full), BF16), shape((2, full), F32)],
        [rows, rows, fixed(2, full)], after,
        flops=20 * share * full, moved=18 * share * full,
    )


def spread(own):
    chip = swap(own, "tensor", 1)
    core = swap(own, "tensor", 0)
    return own, core, chip, swap(chip, "tensor", 0)


def gather_into(mark, parts, whole):
    share = parts[0].shape[0]
    for at, part in enumerate(parts):
        core = mark[CORE] if at % 2 == 0 else 1 - mark[CORE]
        chip = mark[CHIP] if at < 2 else 1 - mark[CHIP]
        first = pl.multiple_of((2 * chip + core) * share, share)
        whole[pl.ds(first, share), :] = part[...]


def hidden_back(marks, cotangent, weight, after=()):
    rows, full = cotangent.shape
    inner = weight.shape[0]
    block = min(256, rows)

    def kernel(mark, c_ref, w_ref, o_ref):
        o_ref[...] = over_columns(c_ref[...], w_ref[...]).astype(BF16)

    return call(
        "hidden_back", kernel, marks, (rows // block,), [cotangent, weight],
        [pl.BlockSpec((block, full), lambda i, mark: (i, 0)), fixed(inner, full)],
        shape((rows, inner), BF16), pl.BlockSpec((block, inner), lambda i, mark: (i, 0)), after,
        flops=2 * rows * full * inner, moved=2 * (rows * full + inner * full + rows * inner),
    )


def gate_up(marks, parts, weight, hidden_grad, after=()):
    share, full = parts[0].shape
    rows = 4 * share
    inner = weight.shape[2]
    tile = 128
    block = min(256, rows)

    def kernel(mark, p0, p1, p2, p3, w_ref, h_ref, second, hidden, hidden_t, gate_grad, up_grad):
        @pl.when(pl.program_id(0) == 0)
        def _():
            gather_into(mark, (p0, p1, p2, p3), second)

        both = jnp.concatenate([w_ref[0], w_ref[1]], axis=1)
        for first in range(0, rows, block):
            at = pl.ds(first, block)
            got = jnp.dot(second[at, :], both, preferred_element_type=F32)
            gate, up = got[:, :tile], got[:, tile:]
            sigmoid = 1.0 / (1.0 + jnp.exp(-gate))
            active = gate * sigmoid
            made = (active * up).astype(BF16)
            hidden[at, :] = made
            hidden_t[:, at] = made.T
            grad = h_ref[at, :].astype(F32)
            gate_grad[at, :] = (grad * up * (sigmoid * (1.0 + gate * (1.0 - sigmoid)))).astype(BF16)
            up_grad[at, :] = (grad * active).astype(BF16)

    column = pl.BlockSpec((rows, tile), lambda i, mark: (0, i))
    return call(
        "gate_up", kernel, marks, (inner // tile,), [*parts, weight, hidden_grad],
        [fixed(share, full)] * 4 + [pl.BlockSpec((2, full, tile), lambda i, mark: (0, 0, i)), column],
        [
            shape((rows, full), BF16), shape((rows, inner), BF16), shape((inner, rows), BF16),
            shape((rows, inner), BF16), shape((rows, inner), BF16),
        ],
        [fixed(rows, full), column, pl.BlockSpec((tile, rows), lambda i, mark: (i, 0)), column, column],
        after,
        flops=4 * rows * full * inner, moved=2 * (4 * full * inner + 2 * rows * full + 5 * rows * inner),
    )


def heads_back(marks, parts, weight, after=()):
    share, full = parts[0].shape
    rows = 4 * share
    width = weight.shape[0]

    def kernel(mark, p0, p1, p2, p3, w_ref, low, grad):
        @pl.when(pl.program_id(0) == 0)
        def _():
            gather_into(mark, (p0, p1, p2, p3), low)

        at = pl.ds(pl.multiple_of(pl.program_id(0) * share, share), share)
        grad[...] = over_columns(low[at, :], w_ref[...]).astype(BF16)

    return call(
        "heads_back", kernel, marks, (4,), [*parts, weight], [fixed(share, full)] * 4 + [fixed(width, full)],
        [shape((rows, full), BF16), shape((rows, width), BF16)],
        [fixed(rows, full), pl.BlockSpec((share, width), lambda i, mark: (i, 0))], after,
        flops=2 * rows * full * width, moved=2 * (2 * rows * full + full * width + rows * width),
    )


def bit_of(mark, bit):
    return (mark[DP] >> bit) & 1


def block_at(mark, order, flips, j):
    rest = len(order) - len(flips)
    index = 0
    for at, bit in enumerate(order):
        if at < len(flips):
            value = bit_of(mark, bit)
            value = 1 - value if flips[at] else value
        else:
            value = (j >> (rest - 1 - (at - len(flips)))) & 1
        index = index + (value << bit)
    return index


def weight_send(marks, order, columns, other, turned_out, after=()):
    size = lax.axis_size("dp")
    rows, full = columns.shape
    block = full // size
    count = size // 2
    dims = (other.shape[0], block) if turned_out else (block, other.shape[1])

    def kernel(mark, c_ref, o_ref, out):
        if turned_out:
            got = jnp.dot(o_ref[...], c_ref[...], preferred_element_type=F32)
        else:
            got = over_rows(c_ref[...], o_ref[...])
        out[0] = got.astype(BF16)

    return call(
        "weight_send", kernel, marks, (count,), [columns, other],
        [
            pl.BlockSpec((rows, block), lambda j, mark: (0, block_at(mark, order, (True,), j))),
            fixed(*other.shape),
        ],
        shape((count, *dims), BF16), pl.BlockSpec((1, *dims), lambda j, mark: (j, 0, 0)), after,
        flops=2 * rows * dims[0] * dims[1] * count,
        moved=rows * full + 2 * other.size + 2 * count * dims[0] * dims[1],
    )


def weight_keep(marks, order, columns, other, turned_out, arrived, after=()):
    size = lax.axis_size("dp")
    rows, full = columns.shape
    block = full // size
    half = size // 4
    dims = (other.shape[0], block) if turned_out else (block, other.shape[1])

    def kernel(mark, c_ref, o_ref, a_ref, send, keep):
        if turned_out:
            got = jnp.dot(o_ref[...], c_ref[...], preferred_element_type=F32)
        else:
            got = over_rows(c_ref[...], o_ref[...])
        got = got + a_ref[0].astype(F32)

        @pl.when(pl.program_id(0) < half)
        def _():
            send[0] = got.astype(BF16)

        @pl.when(pl.program_id(0) >= half)
        def _():
            keep[0] = got

    def block_for(j, mark):
        away = block_at(mark, order, (False, True), j)
        here = block_at(mark, order, (False, False), j - half)
        return jnp.where(j < half, away, here)

    def arrived_for(j, mark):
        mine = bit_of(mark, order[1])
        return jnp.where(j < half, (1 - mine) * half + j, mine * half + j - half)

    return call(
        "weight_keep", kernel, marks, (2 * half,), [columns, other, arrived],
        [
            pl.BlockSpec((rows, block), lambda j, mark: (0, block_for(j, mark))),
            fixed(*other.shape),
            pl.BlockSpec((1, *dims), lambda j, mark: (arrived_for(j, mark), 0, 0)),
        ],
        [shape((half, *dims), BF16), shape((half, *dims), F32)],
        [
            pl.BlockSpec((1, *dims), lambda j, mark: (jnp.minimum(j, half - 1), 0, 0)),
            pl.BlockSpec((1, *dims), lambda j, mark: (jnp.maximum(j - half, 0), 0, 0)),
        ],
        after,
        flops=2 * rows * dims[0] * dims[1] * 2 * half,
        moved=rows * full + 2 * other.size + 8 * half * dims[0] * dims[1],
    )


def finish(order, keep, arrived):
    me = lax.axis_index("dp")
    total = keep + arrived.astype(F32)
    for bit in order[2:]:
        mine = (me >> bit) & 1
        total = total.reshape(2, -1, *total.shape[1:])
        arrived = swap(pick(total, 1 - mine, 0).astype(BF16), "dp", bit)
        total = pick(total, mine, 0) + arrived.astype(F32)
    return total[0]


def plain_weight(columns, other, turned_out):
    if turned_out:
        got = jnp.einsum("fr,rd->fd", other, columns, preferred_element_type=F32)
    else:
        got = jnp.einsum("rd,rf->df", columns, other, preferred_element_type=F32)
    return lax.psum_scatter(
        got.astype(BF16), "dp", scatter_dimension=1 if turned_out else 0, tiled=True
    ).astype(F32)


def everywhere(values):
    for axis in ("dp", "tensor"):
        for bit in range(lax.axis_size(axis).bit_length() - 1):
            values = values + swap(values, axis, bit)
    return values


MESH = pl.DeviceIdType.MESH
QB = 128
SPAN = SEQ_MAX + QB
X_FIRST, Z_FIRST = (0, 1, 2), (1, 0, 2)


class Place:
    def __init__(self):
        self.dp, self.tensor = lax.axis_index("dp"), lax.axis_index("tensor")
        self.core, self.chip = lax.rem(self.tensor, 2), lax.div(self.tensor, 2)
        self.by_bit = [self.dp_partner(at) for at in range(3)]
        self.to_core = (self.dp, self.tensor + 1 - 2 * self.core)
        self.to_chip = (self.dp, self.tensor + 2 * (1 - 2 * self.chip))

    def bit(self, at):
        return lax.rem(lax.div(self.dp, 1 << at), 2)

    def dp_partner(self, at):
        return (self.dp + (1 - 2 * self.bit(at)) * (1 << at), self.tensor)

    def block(self, order, first, j):
        lead = self.bit(order[0])
        index = ((1 - lead) if first else lead) * (1 << order[0])
        rest = order[1:]
        for at, bit in enumerate(rest):
            index = index + lax.rem(lax.div(j, 1 << (len(rest) - 1 - at)), 2) * (1 << bit)
        return index


class Wires:
    def __init__(self, send, receive):
        self.send, self.receive, self.used, self.count = send, receive, [], 0

    def start(self, source, target, partner):
        at, self.count = self.count, self.count + 1
        copy = pltpu.make_async_remote_copy(
            src_ref=source,
            dst_ref=target,
            send_sem=self.send.at[at],
            recv_sem=self.receive.at[at],
            device_id=partner,
            device_id_type=MESH,
        )
        copy.start()
        self.used.append(copy)
        return copy

    def sent(self, copy):
        copy.wait_send()
        self.used = [other for other in self.used if other is not copy]

    def close(self):
        for copy in self.used:
            copy.wait_send()


class Arrays:
    def __init__(self):
        self.shapes = []

    def add(self, kind, *dims):
        self.shapes.append((dims, kind))
        return len(self.shapes) - 1


class Piece:
    def __init__(self, outs, order, block, width):
        self.order = order
        self.first = (outs.add(BF16, 4, block, width), outs.add(BF16, 4, block, width))
        self.kept = outs.add(BF16, 4, block, width)
        self.second = (outs.add(BF16, 2, block, width), outs.add(BF16, 2, block, width))
        self.third = (outs.add(BF16, block, width), outs.add(BF16, block, width))
        self.own = outs.add(F32, block, width)
        self.flying = None


def paired(values):
    lane = lax.broadcasted_iota(jnp.int32, (1, 2 * HD), 1)
    left = (lane < HD).astype(F32).astype(BF16)
    right = (lane >= HD).astype(F32).astype(BF16)
    return jnp.concatenate([values * left, values * right], axis=0)


def unpaired(values):
    return jnp.concatenate([values[:HD, :QB], values[HD:, QB:]], axis=0).T


def reach(row):
    first = max(0, row + QB - SPAN)
    return first, row + QB - first


def pair_bias(begins, row):
    first, count = reach(row)
    key_at = first + lax.broadcasted_iota(jnp.int32, (count, QB), 0)
    query_at = row + lax.broadcasted_iota(jnp.int32, (count, QB), 1)
    seen = (key_at >= begins[:, row : row + QB]) & (key_at <= query_at)
    bias = jnp.where(seen, 0.0, -1e30)
    return jnp.concatenate([bias, bias], axis=1)


FACTOR = HD**-0.5 * LOG2E


def attend_part(begins, qkv, heads_out, logs, part):
    rows, width = heads_out.shape
    for at in range(part, rows // QB, 2):
        row = at * QB
        first, count = reach(row)
        bias = pair_bias(begins, row)

        def pair(h, _):
            lanes = pl.ds(pl.multiple_of(h * 2 * HD, 2 * HD), 2 * HD)
            query = paired(qkv[0, row : row + QB, lanes])
            scores = over_columns(qkv[1, first : first + count, lanes], query) * FACTOR + bias
            top = jnp.max(scores, axis=0, keepdims=True)
            probs = jnp.exp2(scores - top)
            total = jnp.sum(probs, axis=0, keepdims=True)
            got = over_rows(qkv[2, first : first + count, lanes], probs.astype(BF16))
            heads_out[row : row + QB, lanes] = unpaired(got * (1.0 / total)).astype(BF16)
            logs[h, at] = top + jnp.log2(total)
            return _

        lax.fori_loop(0, width // (2 * HD), pair, 0)


def attend_grads(begins, qkv, grads, logs, turn, ahead, behind, out, sum_k, sum_v, sum_b):
    rows, width = grads.shape
    scale = HD**-0.5

    def pair(h, _):
        lanes = pl.ds(pl.multiple_of(h * 2 * HD, 2 * HD), 2 * HD)
        sum_k[...] = jnp.zeros_like(sum_k)
        sum_v[...] = jnp.zeros_like(sum_v)
        bias_q = jnp.zeros((1, 2 * HD), F32)
        for at in range(rows // QB):
            row = at * QB
            first, count = reach(row)
            own, seen = slice(row, row + QB), slice(first, first + count)
            query, grad = paired(qkv[0, own, lanes]), paired(grads[own, lanes])
            key, value = qkv[1, seen, lanes], qkv[2, seen, lanes]
            scores = over_columns(key, query) * FACTOR + pair_bias(begins, row)
            probs = jnp.exp2(scores - logs[h, at])
            weighed = probs * over_columns(value, grad)
            inner = jnp.sum(weighed, axis=0, keepdims=True)
            score_grad = (weighed - probs * inner).astype(BF16)
            sum_v[seen, :] += jnp.dot(probs.astype(BF16), grad, preferred_element_type=F32)
            sum_k[seen, :] += jnp.dot(score_grad, query, preferred_element_type=F32)
            got = unpaired(over_rows(key, score_grad)) * scale
            got = turned(got, turn[own, :], -ahead[own, :], -behind[own, :]).astype(BF16)
            out[0, own, lanes] = got
            bias_q += jnp.sum(got.astype(F32), axis=0, keepdims=True)
        key_grad = turned(sum_k[...] * scale, turn[...], -ahead[...], -behind[...]).astype(BF16)
        value_grad = sum_v[...].astype(BF16)
        out[1, :, lanes] = key_grad
        out[2, :, lanes] = value_grad
        sum_b[0:1, lanes] = bias_q
        sum_b[1:2, lanes] = jnp.sum(key_grad.astype(F32), axis=0, keepdims=True)
        sum_b[2:3, lanes] = jnp.sum(value_grad.astype(F32), axis=0, keepdims=True)
        return _

    lax.fori_loop(0, width // (2 * HD), pair, 0)


def pipe_rows(place, lefts, weight, flipped, send, arrived=None, kept=None):
    rows, depth = lefts[0].shape
    share = rows // 4
    width = weight.shape[-2] if flipped else weight.shape[-1]
    tile = 512
    count = len(lefts)
    keep = arrived is not None
    core = place.core if keep else 1 - place.core

    def left_rows(ref):
        return jnp.concatenate(
            [ref[pl.ds(pl.multiple_of((2 * y + core) * share, share), share), :] for y in range(2)], axis=0
        )

    def body(w_ref, *refs):
        total = 0.0
        for j in range(count):
            if flipped:
                total += over_columns(left_rows(lefts[j]), w_ref[j])
            else:
                total += jnp.dot(left_rows(lefts[j]), w_ref[...], preferred_element_type=F32)
        if keep:
            low = total[:share] + refs[0][0].astype(F32)
            high = total[share:] + refs[0][1].astype(F32)
            first = place.chip == 0
            refs[-1][...] = jnp.where(first, high, low).astype(BF16)
            at = pl.ds(pl.multiple_of(pl.program_id(0) * tile, tile), tile)
            kept[:, at] = jnp.where(first, low, high)
        else:
            refs[-1][...] = total.reshape(2, share, tile).astype(BF16)

    if flipped:
        in_specs = [pl.BlockSpec((count, tile, depth), lambda i: (0, i, 0))]
    else:
        in_specs = [pl.BlockSpec((depth, tile), lambda i: (0, i))]
    pair = pl.BlockSpec((2, share, tile), lambda i: (0, 0, i))
    one = pl.BlockSpec((share, tile), lambda i: (0, i))
    pltpu.emit_pipeline(
        body,
        grid=(width // tile,),
        in_specs=in_specs + ([pair] if keep else []),
        out_specs=[one if keep else pair],
    )(weight, *([arrived] if keep else []), send)


def pipe_weight(place, order, first, columns, others, outs):
    block = outs[0].shape[1]

    def body(*refs):
        for z in range(2):
            at = place.block(order, first, 2 * pl.program_id(0) + z)
            taken = columns[:, pl.ds(pl.multiple_of(at * block, block), block)]
            for other, ref in zip(others, refs):
                ref[z] = over_rows(taken, other[...]).astype(BF16)

    pltpu.emit_pipeline(
        body,
        grid=(2,),
        out_specs=[pl.BlockSpec((2, block, out.shape[2]), lambda j: (j, 0, 0)) for out in outs],
    )(*outs)


def pipe_second(mine, kept, arrived, send):
    _, rows, width = kept.shape
    tile = min(128, rows)
    spec = pl.BlockSpec((2, tile, width), lambda i: (1 - mine, i, 0))

    def body(k_ref, a_ref, o_ref):
        o_ref[...] = (k_ref[...].astype(F32) + a_ref[...].astype(F32)).astype(BF16)

    pltpu.emit_pipeline(
        body,
        grid=(rows // tile,),
        in_specs=[spec, spec],
        out_specs=[pl.BlockSpec((2, tile, width), lambda i: (0, i, 0))],
    )(kept, arrived, send)


def pipe_third(mine, first, kept, arrived, second, send, own):
    _, rows, width = kept.shape
    tile = min(128, rows)
    spec = pl.BlockSpec((2, tile, width), lambda i: (mine, i, 0))
    one = pl.BlockSpec((tile, width), lambda i: (i, 0))

    def body(k_ref, a_ref, b_ref, s_ref, o_ref):
        low, high = (
            k_ref[at].astype(F32) + a_ref[at].astype(F32) + b_ref[at].astype(F32) for at in range(2)
        )
        s_ref[...] = jnp.where(first, high, low).astype(BF16)
        o_ref[...] = jnp.where(first, low, high)

    pltpu.emit_pipeline(
        body,
        grid=(rows // tile,),
        in_specs=[spec, spec, pl.BlockSpec((2, tile, width), lambda i: (0, i, 0))],
        out_specs=[one, one],
    )(kept, arrived, second, send, own)


def finished(results, qkv, out, gate_up, down, block_at, input_at, sums_at):
    wide, tall = [*gate_up, *qkv], [out, down]
    steps = 4
    block = results[qkv[0].own].shape[0]
    part = block // steps

    def kernel(*refs):
        given, made = refs[: 2 * len(wide + tall) + 3], refs[2 * len(wide + tall) + 3 :]

        def total(at):
            return given[2 * at][...] + given[2 * at + 1][...].astype(F32)

        for at in range(len(gate_up)):
            made[0][at] = total(at)
        for at in range(len(qkv)):
            made[1][at] = total(len(gate_up) + at)
        for at in range(len(tall)):

            @pl.when(pl.program_id(0) == 0)
            def _():
                made[2 + at][...] = total(len(wide) + at).T

        made[4][...] = given[-3][...]
        made[5][...] = given[-2][...]
        made[6][...] = given[-1][4:7, :]
        made[7][0:1, :], made[7][1:2, :] = given[-1][0:1, :], given[-1][2:3, :]
        made[8][0:1, :], made[8][1:2, :] = given[-1][1:2, :], given[-1][3:4, :]

    ins, in_specs = [], []
    for p in wide:
        for at in (p.own, p.third[1]):
            ins.append(results[at])
            in_specs.append(pl.BlockSpec((part, results[at].shape[1]), lambda i: (i, 0)))
    for p in tall:
        for at in (p.own, p.third[1]):
            ins.append(results[at])
            in_specs.append(at_zero(*results[at].shape))
    inner, width = results[down.own].shape[1], results[out.own].shape[1]
    share, full = results[block_at].shape
    by_row = pl.BlockSpec((share // steps, full), lambda i: (i, 0))
    got = pl.pallas_call(
        kernel,
        name="finished",
        grid=(steps,),
        in_specs=in_specs + [by_row, by_row, at_zero(8, full)],
        out_specs=[
            pl.BlockSpec((2, part, inner), lambda i: (0, i, 0)),
            pl.BlockSpec((3, part, width), lambda i: (0, i, 0)),
            at_zero(width, block), at_zero(inner, block), by_row, by_row,
            at_zero(3, full), at_zero(2, full), at_zero(2, full),
        ],
        out_shape=[
            shape((2, block, inner), F32), shape((3, block, width), F32), shape((width, block), F32),
            shape((inner, block), F32), shape((share, full), BF16), shape((share, full), F32),
            shape((3, full), F32), shape((2, full), F32), shape((2, full), F32),
        ],
        compiler_params=pltpu.CompilerParams(vmem_limit_bytes=VMEM_LIMIT),
    )(*ins, results[block_at], results[input_at], results[sums_at])
    return got[4], got[5], got[1], got[6], got[2], got[0], got[3], got[7], got[8]


def at_zero(*dims):
    return pl.BlockSpec(dims, lambda *_: (0,) * len(dims))


def forward(tokens, cotangent, qkv_weight, bias, out_weight, gate_up_weight, down_weight, gains, shifts, begins, tables):
    rows, full = tokens.shape
    width, inner = out_weight.shape[0], down_weight.shape[0]
    share = rows // 4
    half = share // 2
    ins = [
        tokens, cotangent, qkv_weight, bias[:, None, :], out_weight, gate_up_weight, down_weight,
        gains, shifts, begins, *tables,
    ]
    outs = Arrays()
    for dims in ((rows, full), (rows, full), (rows, inner), (rows, inner), (rows, inner), (rows, width), (3, rows, width)):
        outs.add(BF16, *dims)
    outs.add(F32, width // 128, rows // QB, 1, 2 * QB)
    outs.add(F32, share, full)
    given, made = len(ins), len(outs.shapes)
    scratch = Arrays()
    for _, dims in enumerate(outs.shapes[1:]):
        scratch.add(dims[1], *dims[0])
    cot_at, out_weight_at = scratch.add(BF16, rows, full), scratch.add(BF16, width, full)
    tables_at = [scratch.add(F32, rows, 128) for _ in range(3)]
    begins_at = scratch.add(jnp.int32, 1, rows)
    gains_at, shifts_at = scratch.add(F32, 2, full), scratch.add(F32, 2, full)
    own_at, kept_at = scratch.add(BF16, share, full), scratch.add(F32, share, full)
    to_core_at = scratch.add(BF16, 2, half, full)
    fore = [
        [to_core_at, scratch.add(BF16, 2, half, full), scratch.add(BF16, half, full), scratch.add(BF16, half, full)]
        for _ in range(2)
    ]
    kinds = [pltpu.VMEM(dims, kind) for dims, kind in scratch.shapes]
    kinds += [pltpu.SemaphoreType.DMA((16,)), pltpu.SemaphoreType.DMA((16,)), pltpu.SemaphoreType.DMA((24,))]

    def kernel(*refs):
        tok, cot, w_qkv, b_qkv, w_out, w_gate_up, w_down, gain_in, shift_in, begin_in, *tables_in = refs[:given]
        o, s = refs[given : given + made], refs[given + made :]
        sends, receives, locals_ = s[-3:]
        sec_v, hidden, gate_grad, up_grad, heads, qkv_v, logs, residual = s[: made - 1]
        cot_v, w_out_v, kept = s[cot_at], s[out_weight_at], s[kept_at]
        turn, ahead, behind = (s[at] for at in tables_at)
        begin, gain, shift, own = s[begins_at], s[gains_at], s[shifts_at], s[own_at]
        place = Place()
        partners = [place.to_core, place.to_chip]
        wires = Wires(sends, receives)
        stays = []

        def load(source, target):
            copy = pltpu.make_async_copy(source, target, locals_.at[len(stays)])
            copy.start()
            stays.append(copy)
            return copy

        def quarter(at, tensor, part=None):
            if part is None:
                return at.at[pl.ds(pl.multiple_of(tensor * share, share), share), :]
            return at.at[pl.ds(pl.multiple_of(tensor * share + part * half, half), half), :]

        mine, beyond = place.tensor, place.core + 2 * (1 - place.chip)
        barrier = pltpu.get_barrier_semaphore()
        for partner in partners:
            pl.semaphore_signal(barrier, inc=1, device_id=partner, device_id_type=MESH)
        early = [load(gain_in, gain), load(shift_in, shift)]
        soon = [
            load(tables_in[0], turn), load(tables_in[1], ahead), load(tables_in[2], behind),
            load(begin_in, begin),
        ]
        later = [load(quarter(tok, mine), own), load(w_out, w_out_v), load(cot, cot_v)]
        for copy in early:
            copy.wait()

        for copy in soon:
            copy.wait()
        def norm_first(t_ref):
            unit, _ = norm_parts(t_ref[...].astype(F32))
            at = pl.ds(pl.multiple_of(pl.program_id(0) * half, half), half)
            sec_v[at, :] = (unit * gain[0:1, :] + shift[0:1, :]).astype(BF16)

        pltpu.emit_pipeline(
            norm_first, grid=(rows // half,), in_specs=[pl.BlockSpec((half, full), lambda i: (i, 0))]
        )(tok)
        keep_normed = load(sec_v, o[0])

        def project_tile(w_ref, b_ref):
            j = pl.program_id(0)
            lanes = pl.ds(pl.multiple_of(pl.program_id(1) * 256, 256), 256)
            for first in range(0, rows, 256):
                at = slice(first, first + 256)
                got = jnp.dot(sec_v[at, :], w_ref[0], preferred_element_type=F32) + b_ref[0]

                @pl.when(j < 2)
                def _():
                    qkv_v[j, at, lanes] = turned(got, turn[at, :], ahead[at, :], behind[at, :]).astype(BF16)

                @pl.when(j == 2)
                def _():
                    qkv_v[j, at, lanes] = got.astype(BF16)

        pltpu.emit_pipeline(
            project_tile,
            grid=(3, width // 256),
            in_specs=[
                pl.BlockSpec((1, full, 256), lambda j, i: (j, 0, i)),
                pl.BlockSpec((1, 1, 256), lambda j, i: (j, 0, i)),
            ],
        )(w_qkv, b_qkv)

        def project_out(part):
            to_core, from_core = s[fore[part][0]], s[fore[part][1]]
            places = [(2 * y + c) * share + part * half for c in (1 - place.core, place.core) for y in range(2)]
            left = jnp.concatenate([heads[pl.ds(pl.multiple_of(at, half), half), :] for at in places], axis=0)
            for first in range(0, full, 512):
                at = slice(first, first + 512)
                got = jnp.dot(left, w_out_v[:, at], preferred_element_type=F32)
                to_core[:, :, at] = got[:share].reshape(2, half, 512).astype(BF16)
                kept[:, at] = got[share:]
            return wires.start(to_core, from_core, place.to_core)

        def add_core(part, flying):
            from_core, to_chip, from_chip = (s[at] for at in fore[part][1:])
            flying.wait_recv()
            wires.sent(flying)
            low = kept[:half, :] + from_core[0].astype(F32)
            high = kept[half:, :] + from_core[1].astype(F32)
            first = place.chip == 0
            at = slice(part * half, (part + 1) * half)
            residual[at, :] = own[at, :].astype(F32) + jnp.where(first, low, high)
            to_chip[...] = jnp.where(first, high, low).astype(BF16)
            return wires.start(to_chip, from_chip, place.to_chip)

        def norm_second(part, flying):
            flying.wait_recv()
            at = slice(part * half, (part + 1) * half)
            got = residual[at, :] + s[fore[part][3]][...].astype(F32)
            residual[at, :] = got
            unit, _ = norm_parts(got)
            rows_at = quarter(sec_v, mine, part)
            rows_at[...] = (unit * gain[1:2, :] + shift[1:2, :]).astype(BF16)
            return (
                wires.start(rows_at, rows_at, place.to_chip),
                wires.start(rows_at, rows_at, place.to_core),
            )

        def pass_on(part, chip_flying):
            chip_flying.wait_recv()
            rows_at = quarter(sec_v, beyond, part)
            return wires.start(rows_at, rows_at, place.to_core)

        def hidden_back(first, count):
            def body(w_ref):
                lanes = pl.ds(pl.multiple_of((first + pl.program_id(0)) * 128, 128), 128)
                up_grad[:, lanes] = over_columns(cot_v[...], w_ref[...]).astype(BF16)

            pltpu.emit_pipeline(
                body, grid=(count,), in_specs=[pl.BlockSpec((128, full), lambda i: (first + i, 0))]
            )(w_down)

        def gate_up(part):
            def body(w_ref):
                lanes = pl.ds(pl.multiple_of(pl.program_id(0) * 128, 128), 128)
                both = jnp.concatenate([w_ref[0], w_ref[1]], axis=1)
                for q in range(0, 4, 2):
                    spots = [slice((q + z) * share + part * half, (q + z) * share + (part + 1) * half) for z in range(2)]
                    left = jnp.concatenate([sec_v[at, :] for at in spots], axis=0)
                    got = jnp.dot(left, both, preferred_element_type=F32)
                    for z, at in enumerate(spots):
                        gates, ups = got[z * half : (z + 1) * half, :128], got[z * half : (z + 1) * half, 128:]
                        sigmoid = 1.0 / (1.0 + jnp.exp(-gates))
                        active = gates * sigmoid
                        grad = up_grad[at, lanes].astype(F32)
                        hidden[at, lanes] = (active * ups).astype(BF16)
                        gate_grad[at, lanes] = (
                            grad * ups * (sigmoid * (1.0 + gates * (1.0 - sigmoid)))
                        ).astype(BF16)
                        up_grad[at, lanes] = (grad * active).astype(BF16)

            pltpu.emit_pipeline(
                body, grid=(inner // 128,), in_specs=[pl.BlockSpec((2, full, 128), lambda i: (0, 0, i))]
            )(w_gate_up)

        tiles = inner // 128
        attend_part(begin, qkv_v, heads, logs, 0)
        keep_normed.wait()
        for copy in later:
            copy.wait()
        pl.semaphore_wait(barrier, len(partners))
        flying = project_out(0)
        hidden_back(0, tiles // 2)
        chip0 = add_core(0, flying)
        attend_part(begin, qkv_v, heads, logs, 1)
        flying = project_out(1)
        kept_early = [load(heads, o[5]), load(qkv_v, o[6]), load(logs, o[7])]
        hidden_back(tiles // 2, 2)
        chip1 = add_core(1, flying)
        hidden_back(tiles // 2 + 2, tiles - tiles // 2 - 2)
        chip0, core0 = norm_second(0, chip0)
        chip1, core1 = norm_second(1, chip1)
        both0 = pass_on(0, chip0)
        core0.wait_recv()
        both0.wait_recv()
        gate_up(0)
        both1 = pass_on(1, chip1)
        core1.wait_recv()
        both1.wait_recv()
        kept_early += [load(sec_v, o[1]), load(residual, o[8])]
        gate_up(1)

        late = [load(hidden, o[2]), load(gate_grad, o[3]), load(up_grad, o[4])]
        for copy in [*kept_early, *late]:
            copy.wait()
        wires.close()

    return pl.pallas_call(
        kernel,
        name="forward",
        in_specs=[ANY] * given,
        out_specs=[ANY] * made,
        out_shape=[shape(dims, kind) for dims, kind in outs.shapes],
        scratch_shapes=kinds,
        compiler_params=pltpu.CompilerParams(
            vmem_limit_bytes=62 << 20, collective_id=1, has_side_effects=True
        ),
    )(*ins)


def backward(
    tokens, cotangent, qkv_weight, out_weight, gate_up_weight, down_weight, gains, begins, tables, saved
):
    rows, full = tokens.shape
    width, inner = out_weight.shape[0], down_weight.shape[0]
    share, block = rows // 4, full // 8
    half = share // 2
    ins = [
        tokens, cotangent, qkv_weight, out_weight, gate_up_weight, down_weight, gains, begins, *tables, *saved,
    ]
    outs = Arrays()
    down, up = Piece(outs, X_FIRST, block, inner), Piece(outs, X_FIRST, block, inner)
    gate = Piece(outs, Z_FIRST, block, inner)
    out = Piece(outs, X_FIRST, block, width)
    qkv = [Piece(outs, X_FIRST, block, width) for _ in range(3)]
    pieces = [down, gate, up, out, *qkv]
    rows_out = [[outs.add(BF16, 2, share, full) for _ in range(2)] + [outs.add(BF16, share, full)] for _ in range(3)]
    block_at, input_at, sums_at = outs.add(BF16, share, full), outs.add(F32, share, full), outs.add(F32, 8, full)
    given, made = len(ins), len(outs.shapes)

    scratch = Arrays()
    for array in saved[1:]:
        scratch.add(array.dtype, *array.shape)
    cot_at, low_rows, out_weight_at = scratch.add(BF16, rows, full), scratch.add(BF16, rows, full), scratch.add(BF16, width, full)
    heads_grad_at, qkv_grad_at = scratch.add(BF16, rows, width), scratch.add(BF16, 3, rows, width)
    tables_at = [scratch.add(F32, rows, 128) for _ in range(3)]
    begins_at, gains_at = scratch.add(jnp.int32, 1, rows), scratch.add(F32, 2, full)
    own_at = scratch.add(BF16, share, full)
    residual_grad_at, kept_at = (scratch.add(F32, share, full) for _ in range(2))
    chip_in = [scratch.add(BF16, share, full) for _ in range(3)]
    sum_k_at, sum_v_at = scratch.add(F32, rows, 128), scratch.add(F32, rows, 128)
    sum_b_at = scratch.add(F32, 8, width)
    held_at, came_at = scratch.add(F32, 6, 8, full), scratch.add(F32, 5, 8, full)
    kinds = [pltpu.VMEM(dims, kind) for dims, kind in scratch.shapes]
    kinds += [pltpu.SemaphoreType.DMA((48,)), pltpu.SemaphoreType.DMA((48,)), pltpu.SemaphoreType.DMA((24,))]

    def kernel(*refs):
        tok, cot, w_qkv, w_out, w_gate_up, w_down, gain_in, begin_in = refs[:8]
        tables_in, saved_in = refs[8:11], refs[11:given]
        o, s = refs[given : given + made], refs[given + made :]
        sends, receives, locals_ = s[-3:]
        sec_v, hidden, gate_grad, up_grad, heads, qkv_v, logs, residual = s[: len(saved) - 1]
        cot_v, low_v, w_out_v = s[cot_at], s[low_rows], s[out_weight_at]
        heads_grad, qkv_grad = s[heads_grad_at], s[qkv_grad_at]
        turn, ahead, behind = (s[at] for at in tables_at)
        begin, gain, own = s[begins_at], s[gains_at], s[own_at]
        residual_grad, kept = s[residual_grad_at], s[kept_at]
        held, came, sum_b = s[held_at], s[came_at], s[sum_b_at]
        place = Place()
        partners = [*place.by_bit, place.to_core, place.to_chip]
        wires = Wires(sends, receives)
        stays = []

        def load(source, target):
            copy = pltpu.make_async_copy(source, target, locals_.at[len(stays)])
            copy.start()
            stays.append(copy)
            return copy

        def quarter(at, tensor, part=None):
            if part is None:
                return at.at[pl.ds(pl.multiple_of(tensor * share, share), share), :]
            return at.at[pl.ds(pl.multiple_of(tensor * share + part * half, half), half), :]

        mine, beyond = place.tensor, place.core + 2 * (1 - place.chip)
        barrier = pltpu.get_barrier_semaphore()
        for partner in partners:
            pl.semaphore_signal(barrier, inc=1, device_id=partner, device_id_type=MESH)
        loads = [load(cot, cot_v), load(saved_in[2], hidden)]
        loads_second = [load(saved_in[1], sec_v), load(saved_in[3], gate_grad), load(saved_in[4], up_grad)]
        loads_rest = [
            load(saved_in[5], heads), load(saved_in[6], qkv_v), load(saved_in[7], logs), load(saved_in[8], residual),
            load(w_out, w_out_v), load(gain_in, gain), load(begin_in, begin),
            load(tables_in[0], turn), load(tables_in[1], ahead), load(tables_in[2], behind),
        ]
        pl.semaphore_wait(barrier, len(partners))

        def first_half(those, columns, others):
            order = those[0].order
            pipe_weight(place, order, True, columns, others, [o[p.first[0]] for p in those])
            for p in those:
                p.flying = wires.start(o[p.first[0]], o[p.first[1]], place.by_bit[order[0]])

        def second_half(those, columns, others):
            pipe_weight(place, those[0].order, False, columns, others, [o[p.kept] for p in those])

        def then(p):
            p.flying.wait_recv()
            pipe_second(place.bit(p.order[1]), o[p.kept], o[p.first[1]], o[p.second[0]])
            p.flying = wires.start(o[p.second[0]], o[p.second[1]], place.by_bit[p.order[1]])

        def last(p):
            p.flying.wait_recv()
            pipe_third(
                place.bit(p.order[1]), place.bit(p.order[2]) == 0, o[p.kept], o[p.first[1]], o[p.second[1]],
                o[p.third[0]], o[p.own],
            )
            p.flying = wires.start(o[p.third[0]], o[p.third[1]], place.by_bit[p.order[2]])

        def rows_first(at, lefts, weight, flipped):
            pipe_rows(place, lefts, weight, flipped, o[rows_out[at][0]])
            return wires.start(o[rows_out[at][0]], o[rows_out[at][1]], place.to_core)

        def rows_then(at, lefts, weight, flipped, flying, into):
            flying.wait_recv()
            pipe_rows(place, lefts, weight, flipped, o[rows_out[at][2]], o[rows_out[at][1]], into)
            return wires.start(o[rows_out[at][2]], s[chip_in[at]], place.to_chip)

        def norm_grads(values, base, arrived, row, result, low):
            for part in range(2):
                at = slice(part * half, (part + 1) * half)
                unit, inverse = norm_parts(values[at, :].astype(F32))
                grad = kept[at, :] + arrived[at, :].astype(F32)
                got = base[at, :].astype(F32) + norm_back(unit, inverse, gain[row : row + 1, :], grad)
                result[at, :] = got
                if low is not None:
                    low[at, :] = got.astype(BF16)
                held[0, 2 * row : 2 * row + 1, :] += jnp.sum(grad * unit, axis=0, keepdims=True)
                held[0, 2 * row + 1 : 2 * row + 2, :] += jnp.sum(grad, axis=0, keepdims=True)

        def add_everywhere(step):
            order = [place.to_core, place.to_chip, place.by_bit[1], place.by_bit[2], place.by_bit[0]]
            return wires.start(held.at[step], came.at[step], order[step])

        def added(step, flying):
            flying.wait_recv()
            held[step + 1] = held[step] + came[step]

        grads = [gate_grad, up_grad]
        lows = [qkv_grad.at[j] for j in range(3)]
        for copy in loads:
            copy.wait()
        first_half([down], cot_v, [hidden])
        for copy in loads_second:
            copy.wait()
        first_half([gate], sec_v, [gate_grad])
        second_half([down], cot_v, [hidden])
        flying = rows_first(0, grads, w_gate_up, True)
        first_half([up], sec_v, [up_grad])
        chip = rows_then(0, grads, w_gate_up, True, flying, kept)
        second_half([gate], sec_v, [gate_grad])
        second_half([up], sec_v, [up_grad])
        renormed = load(saved_in[0], sec_v)
        for copy in loads_rest:
            copy.wait()
        held[0] = jnp.zeros_like(held[0])
        chip.wait_recv()
        norm_grads(residual, quarter(cot_v, mine), s[chip_in[0]], 1, residual_grad, quarter(low_v, mine))
        mine_v, beyond_v = quarter(low_v, mine), quarter(low_v, beyond)
        chip = wires.start(mine_v, mine_v, place.to_chip)
        core = wires.start(mine_v, mine_v, place.to_core)
        flying = rows_first(1, [hidden], w_down, False)
        branch_chip = rows_then(1, [hidden], w_down, False, flying, kept)
        then(down)
        chip.wait_recv()
        both = wires.start(beyond_v, beyond_v, place.to_core)
        core.wait_recv()
        both.wait_recv()
        for first in range(0, rows, 256):
            at = slice(first, first + 256)
            heads_grad[at, :] = over_columns(low_v[at, :], w_out_v[...]).astype(BF16)
        first_half([out], low_v, [heads])
        then(gate)
        attend_grads(
            begin, qkv_v, heads_grad, logs, turn, ahead, behind, qkv_grad, s[sum_k_at], s[sum_v_at], sum_b
        )
        renormed.wait()
        first_half(qkv, sec_v, lows)
        flying = rows_first(2, lows, w_qkv, True)
        branch_chip.wait_recv()
        own[...] = (residual[...] + kept[...] + s[chip_in[1]][...].astype(F32)).astype(BF16)
        keep_block = load(own, o[block_at])
        last(down)
        chip = rows_then(2, lows, w_qkv, True, flying, kept)
        second_half([out], low_v, [heads])
        second_half(qkv, sec_v, lows)
        then(up)
        chip.wait_recv()
        keep_block.wait()
        back = load(quarter(tok, mine), own)
        back.wait()
        norm_grads(own, residual_grad, s[chip_in[2]], 0, residual, None)
        keep_input = load(residual, o[input_at])
        held[0, 4:7, pl.ds(pl.multiple_of(place.tensor * width, 128), width)] = sum_b[0:3, :]
        flying = add_everywhere(0)
        then(out)
        added(0, flying)
        flying = add_everywhere(1)
        last(gate)
        added(1, flying)
        last(up)
        last(out)
        flying = add_everywhere(2)
        then(qkv[0])
        added(2, flying)
        flying = add_everywhere(3)
        then(qkv[1])
        last(qkv[0])
        added(3, flying)
        flying = add_everywhere(4)
        then(qkv[2])
        last(qkv[1])
        added(4, flying)
        keep_sums = load(held.at[5], o[sums_at])
        last(qkv[2])
        for p in pieces:
            p.flying.wait_recv()
        keep_input.wait()
        keep_sums.wait()
        wires.close()

    results = pl.pallas_call(
        kernel,
        name="backward",
        in_specs=[ANY] * given,
        out_specs=[ANY] * made,
        out_shape=[shape(dims, kind) for dims, kind in outs.shapes],
        scratch_shapes=kinds,
        compiler_params=pltpu.CompilerParams(
            vmem_limit_bytes=62 << 20, collective_id=2, has_side_effects=True
        ),
    )(*ins)
    return finished(results, qkv, out, [gate, up], down, block_at, input_at, sums_at)


def body(
    tokens,
    seq_lengths,
    qkv_weight,
    qkv_bias,
    out_weight,
    gate_up_weight,
    down_weight,
    norm_gains,
    norm_shifts,
    cotangent,
):
    row_count, full_width = tokens.shape
    local_width = qkv_weight.shape[2]
    tensor_at, dp_at, dp_size = lax.axis_index("tensor"), lax.axis_index("dp"), lax.axis_size("dp")
    marks = jnp.stack([tensor_at & 1, tensor_at >> 1, dp_at]).astype(jnp.int32)
    bits = dp_size.bit_length() - 1
    x_first = tuple(range(bits))
    z_first = (1, 0) + x_first[2:]
    fine = (full_width // dp_size) % 128 == 0

    def send(order, columns, other, turned_out, after):
        if not fine:
            return columns
        return weight_send(marks, order, columns, other, turned_out, after)

    def keep(order, columns, other, turned_out, sent, after):
        if not fine:
            return columns, None
        return weight_keep(
            marks, order, columns, other, turned_out, swap(sent, "dp", order[0]), after
        )

    def total(order, columns, other, turned_out, kept):
        if not fine:
            return plain_weight(columns, other, turned_out)
        return finish(order, kept[1], swap(kept[0], "dp", order[1]))

    begins, *tables = positions(seq_lengths[0], row_count)
    if dp_size == 8 and lax.axis_size("tensor") == 4:
        saved = forward(
            tokens, cotangent, qkv_weight, qkv_bias.astype(F32), out_weight, gate_up_weight, down_weight,
            norm_gains, norm_shifts, begins[None], tables,
        )
        return backward(
            tokens, cotangent, qkv_weight, out_weight, gate_up_weight, down_weight, norm_gains, begins[None],
            tables, saved,
        )
    normed, queries, keys, values = project(
        tokens, qkv_weight, qkv_bias, norm_gains[0], norm_shifts[0], tables
    )
    heads_out, logs = attend(begins, queries, keys, values)
    sent = rows_product(marks, [heads_out], out_weight, False)
    to_chip, own = rows_product(marks, [heads_out], out_weight, False, swap(sent, "tensor", 0))
    hidden_grad = hidden_back(marks, cotangent, down_weight, [own])
    residual, second_own = norm_rows(
        marks, tokens, own, swap(to_chip, "tensor", 1), norm_gains[1], norm_shifts[1], [hidden_grad]
    )
    second, hidden, hidden_t, gate_grad, up_grad = gate_up(
        marks, spread(second_own), gate_up_weight, hidden_grad
    )
    down_sent = send(x_first, cotangent, hidden_t, True, [])
    second_sent = rows_product(marks, [gate_grad, up_grad], gate_up_weight, True, None, [down_sent])
    up_sent = send(x_first, second, up_grad, False, [second_sent])
    to_chip, own = rows_product(
        marks, [gate_grad, up_grad], gate_up_weight, True, swap(second_sent, "tensor", 0), [up_sent]
    )
    gate_sent = send(z_first, second, gate_grad, False, [own])
    branch_sent = rows_product(marks, [hidden], down_weight, False, None, [gate_sent])
    branch_to_chip, branch_own = rows_product(
        marks, [hidden], down_weight, False, swap(branch_sent, "tensor", 0), [gate_sent]
    )
    residual_grad, residual_low_own, second_sums = norm_back_rows(
        marks, residual, cotangent, own, swap(to_chip, "tensor", 1), norm_gains[1], [branch_own]
    )
    block_out = (
        residual + branch_own + swap(branch_to_chip, "tensor", 1).astype(F32)
    ).astype(BF16)
    down_kept = keep(x_first, cotangent, hidden_t, True, down_sent, [residual_low_own])
    residual_low, heads_grad = heads_back(
        marks, spread(residual_low_own), out_weight, [down_kept[0]]
    )
    heads_t = heads_out.T
    out_sent = send(x_first, residual_low, heads_t, True, [heads_grad])
    projected_low = attend_back(begins, queries, keys, values, heads_grad, logs, tables)
    gate_kept = keep(z_first, second, gate_grad, False, gate_sent, [projected_low[0]])
    qkv_sent = []
    before = gate_kept[0]
    for grads in projected_low:
        before = send(x_first, normed, grads, False, [before])
        qkv_sent.append(before)
    normed_sent = rows_product(marks, projected_low, qkv_weight, True, None, [before])
    up_kept = keep(x_first, second, up_grad, False, up_sent, [normed_sent])
    to_chip, own = rows_product(
        marks, projected_low, qkv_weight, True, swap(normed_sent, "tensor", 0), [normed_sent]
    )
    input_grad, _, first_sums = norm_back_rows(
        marks, tokens, residual_grad, own, swap(to_chip, "tensor", 1), norm_gains[0], [up_kept[0]]
    )
    bias_local = jnp.stack([jnp.sum(g, axis=0, dtype=F32) for g in projected_low])
    bias_placed = lax.dynamic_update_slice(
        jnp.zeros((3, full_width), F32), bias_local, (0, tensor_at * local_width)
    )
    sums = everywhere(jnp.concatenate([first_sums, second_sums, bias_placed], axis=0))
    out_kept = keep(x_first, residual_low, heads_t, True, out_sent, [input_grad])
    qkv_kept = []
    before = out_kept[0]
    for grads, sent in zip(projected_low, qkv_sent):
        kept = keep(x_first, normed, grads, False, sent, [before])
        before = kept[0]
        qkv_kept.append(kept)
    return (
        block_out,
        input_grad,
        jnp.stack(
            [total(x_first, normed, g, False, k) for g, k in zip(projected_low, qkv_kept)]
        ),
        sums[4:7],
        total(x_first, residual_low, heads_t, True, out_kept),
        jnp.stack(
            [
                total(z_first, second, gate_grad, False, gate_kept),
                total(x_first, second, up_grad, False, up_kept),
            ]
        ),
        total(x_first, cotangent, hidden_t, True, down_kept),
        jnp.stack([sums[0], sums[2]]),
        jnp.stack([sums[1], sums[3]]),
    )


def solution(mesh):
    return jax.shard_map(
        body,
        mesh=mesh,
        in_specs=(
            P("dp", None),
            P("dp", None),
            P(None, None, "tensor"),
            P(None, "tensor"),
            P("tensor", None),
            P(None, None, "tensor"),
            P("tensor", None),
            P(),
            P(),
            P("dp", None),
        ),
        out_specs=(
            P(("dp", "tensor"), None),
            P(("dp", "tensor"), None),
            P(None, "dp", "tensor"),
            P(),
            P("tensor", "dp"),
            P(None, "dp", "tensor"),
            P("tensor", "dp"),
            P(),
            P(),
        ),
        check_vma=False,
    )
```

```python
import functools

import jax
import jax.numpy as jnp
from jax import lax
from jax.experimental import pallas as pl
from jax.experimental.pallas import tpu as pltpu
from jax.sharding import PartitionSpec as P

HD = 64
SEQ_MAX = 512
BQ = 256
F32 = jnp.float32
BF16 = jnp.bfloat16
LOG2E = 1.4426950408889634
VMEM_LIMIT = 60 * 1024 * 1024


def norm_parts(values):
    centred = values - jnp.mean(values, axis=-1, keepdims=True)
    inverse = lax.rsqrt(jnp.mean(centred * centred, axis=-1, keepdims=True) + 1e-05)
    return (centred * inverse, inverse)


def norm_back(unit, inverse, gain_row, grad_rows):
    scaled = grad_rows * gain_row
    return inverse * (
        scaled
        - jnp.mean(scaled, axis=-1, keepdims=True)
        - unit * jnp.mean(scaled * unit, axis=-1, keepdims=True)
    )


def positions(lengths, row_count):
    indices = jnp.arange(row_count, dtype=jnp.int32)
    count = lengths.shape[0]
    order = jnp.arange(count, dtype=jnp.int32)
    ends_at = jnp.sum(jnp.where(order[:, None] <= order[None, :], lengths[:, None], 0), axis=0)
    passed = indices[:, None] >= ends_at[None, :]
    begins = jnp.sum(jnp.where(passed, lengths[None, :], 0), axis=1, dtype=jnp.int32)
    places = (indices - begins).astype(F32)
    half = HD // 8
    lane = jnp.arange(128, dtype=jnp.int32) % HD
    rates = 10000.0 ** (-((lane % half).astype(F32) / half))
    angles = places[:, None] * rates[None, :]
    cosine, sine = jnp.cos(angles), jnp.sin(angles)
    turn = jnp.where(lane < 2 * half, cosine, 1.0)
    ahead = jnp.where(lane < half, -sine, 0.0)
    behind = jnp.where((lane >= half) & (lane < 2 * half), sine, 0.0)
    return begins, turn, ahead, behind


def turned(values, turn, ahead, behind):
    half = HD // 8
    width = values.shape[1]
    times = width // turn.shape[1]

    def wide(table):
        return jnp.concatenate([table] * times, axis=1) if times > 1 else table

    return (
        values * wide(turn)
        + pltpu.roll(values, width - half, 1) * wide(ahead)
        + pltpu.roll(values, half, 1) * wide(behind)
    )


def qkv_kernel(x_ref, w_ref, b_ref, g_ref, s_ref, c_ref, a_ref, h_ref, n_ref, q_ref, k_ref, v_ref):
    unit, _ = norm_parts(x_ref[...].astype(F32))
    normed = (unit * g_ref[...] + s_ref[...]).astype(BF16)
    n_ref[...] = normed
    for j, out in enumerate((q_ref, k_ref, v_ref)):
        got = jnp.dot(normed, w_ref[j], preferred_element_type=F32) + b_ref[j : j + 1, :]
        if j < 2:
            got = turned(got, c_ref[...], a_ref[...], h_ref[...])
        out[...] = got.astype(BF16)


def project(tokens, weight, bias, gain, shift, tables):
    rows, full = tokens.shape
    width = weight.shape[2]
    block = min(256, rows)

    def whole(*dims):
        return pl.BlockSpec(dims, lambda i: (0,) * len(dims))

    def by_row(columns):
        return pl.BlockSpec((block, columns), lambda i: (i, 0))

    return pl.pallas_call(
        qkv_kernel,
        name="project",
        grid=(rows // block,),
        in_specs=[
            by_row(full),
            whole(3, full, width),
            whole(3, width),
            whole(1, full),
            whole(1, full),
            by_row(128),
            by_row(128),
            by_row(128),
        ],
        out_specs=[by_row(full), by_row(width), by_row(width), by_row(width)],
        out_shape=[jax.ShapeDtypeStruct((rows, full), BF16)]
        + [jax.ShapeDtypeStruct((rows, width), BF16)] * 3,
        compiler_params=pltpu.CompilerParams(vmem_limit_bytes=VMEM_LIMIT),
        cost_estimate=pl.CostEstimate(flops=0, bytes_accessed=0, transcendentals=0),
    )(tokens, weight, bias.astype(F32), gain[None], shift[None], *tables)


def spans(step, blocks):
    most = SEQ_MAX // BQ + 1
    forms = []
    for at in range(min(most - 1, blocks)):
        forms.append((step == at, 0, (at + 1) * BQ))
    if blocks >= most:
        first = pl.multiple_of((step - (most - 1)) * BQ, BQ)
        forms.append((step >= most - 1, first, most * BQ))
    return forms


def allowed_bias(begin_row, first, count, step):
    key_at = first + lax.broadcasted_iota(jnp.int32, (count, BQ), 0)
    query_at = step * BQ + lax.broadcasted_iota(jnp.int32, (count, BQ), 1)
    return jnp.where((key_at >= begin_row) & (key_at <= query_at), 0.0, -1e30)


def over_rows(left, right):
    return lax.dot_general(left, right, (((0,), (0,)), ((), ())), preferred_element_type=F32)


def over_columns(left, right):
    return lax.dot_general(left, right, (((1,), (1,)), ((), ())), preferred_element_type=F32)


def attend_kernel(blocks, begin_ref, q_ref, k_ref, v_ref, o_ref, l_ref):
    step = pl.program_id(1)
    factor = HD**-0.5 * LOG2E

    def one(first, count):
        bias = allowed_bias(begin_ref[...], first, count, step)
        rows = pl.ds(first, count)
        parts = []
        for head in range(2):
            lanes = slice(head * HD, (head + 1) * HD)
            scores = over_columns(k_ref[rows, lanes], q_ref[:, lanes]) * factor + bias
            top = jnp.max(scores, axis=0, keepdims=True)
            probs = jnp.exp2(scores - top)
            total = jnp.sum(probs, axis=0, keepdims=True)
            got = over_rows(v_ref[rows, lanes], probs.astype(BF16))
            parts.append(got * (1.0 / total))
            l_ref[head] = top + jnp.log2(total)
        o_ref[...] = jnp.concatenate(parts, axis=0).T.astype(BF16)

    for condition, first, count in spans(step, blocks):
        pl.when(condition)(functools.partial(one, first, count))


def attend(begins, queries, keys, values):
    rows, width = queries.shape
    blocks = rows // BQ
    return pl.pallas_call(
        functools.partial(attend_kernel, blocks),
        name="attend",
        grid=(width // 128, blocks),
        in_specs=[
            pl.BlockSpec((1, BQ), lambda h, i: (0, i)),
            pl.BlockSpec((BQ, 128), lambda h, i: (i, h)),
            pl.BlockSpec((rows, 128), lambda h, i: (0, h)),
            pl.BlockSpec((rows, 128), lambda h, i: (0, h)),
        ],
        out_specs=[
            pl.BlockSpec((BQ, 128), lambda h, i: (i, h)),
            pl.BlockSpec((2, 1, BQ), lambda h, i: (h, 0, i)),
        ],
        out_shape=[
            jax.ShapeDtypeStruct((rows, width), BF16),
            jax.ShapeDtypeStruct((width // HD, 1, rows), F32),
        ],
        compiler_params=pltpu.CompilerParams(vmem_limit_bytes=VMEM_LIMIT),
        cost_estimate=pl.CostEstimate(flops=0, bytes_accessed=0, transcendentals=0),
    )(begins[None], queries, keys, values)


def attend_back_kernel(
    blocks, begin_ref, q_ref, k_ref, v_ref, g_ref, l_ref, cq_ref, aq_ref, hq_ref, c_ref, a_ref, h_ref,
    dq_ref, dk_ref, dv_ref, sum_k, sum_v,
):
    step = pl.program_id(1)
    scale = HD**-0.5
    factor = scale * LOG2E

    @pl.when(step == 0)
    def _():
        sum_k[...] = jnp.zeros_like(sum_k)
        sum_v[...] = jnp.zeros_like(sum_v)

    def one(first, count):
        bias = allowed_bias(begin_ref[...], first, count, step)
        rows = pl.ds(first, count)
        dq, dk, dv = [], [], []
        for head in range(2):
            lanes = slice(head * HD, (head + 1) * HD)
            query, key, value, grad = q_ref[:, lanes], k_ref[rows, lanes], v_ref[rows, lanes], g_ref[:, lanes]
            probs = jnp.exp2(over_columns(key, query) * factor + bias - l_ref[head])
            weighed = probs * over_columns(value, grad)
            inner = jnp.sum(weighed, axis=0, keepdims=True)
            score_grad = (weighed - probs * inner).astype(BF16)
            dv.append(jnp.dot(probs.astype(BF16), grad, preferred_element_type=F32))
            dk.append(jnp.dot(score_grad, query, preferred_element_type=F32))
            dq.append(over_rows(key, score_grad))
        sum_k[rows, :] += jnp.concatenate(dk, axis=1)
        sum_v[rows, :] += jnp.concatenate(dv, axis=1)
        query_grad = jnp.concatenate(dq, axis=0).T * scale
        dq_ref[...] = turned(query_grad, cq_ref[...], -aq_ref[...], -hq_ref[...]).astype(BF16)

    for condition, first, count in spans(step, blocks):
        pl.when(condition)(functools.partial(one, first, count))

    @pl.when(step == blocks - 1)
    def _():
        dk_ref[...] = turned(sum_k[...] * scale, c_ref[...], -a_ref[...], -h_ref[...]).astype(BF16)
        dv_ref[...] = sum_v[...].astype(BF16)


def attend_back(begins, queries, keys, values, grads, logs, tables):
    rows, width = queries.shape
    blocks = rows // BQ
    part = pl.BlockSpec((BQ, 128), lambda h, i: (i, h))
    column = pl.BlockSpec((rows, 128), lambda h, i: (0, h))
    return pl.pallas_call(
        functools.partial(attend_back_kernel, blocks),
        name="attend_back",
        grid=(width // 128, blocks),
        in_specs=[
            pl.BlockSpec((1, BQ), lambda h, i: (0, i)),
            part,
            column,
            column,
            part,
            pl.BlockSpec((2, 1, BQ), lambda h, i: (h, 0, i)),
        ]
        + [pl.BlockSpec((BQ, 128), lambda h, i: (i, 0))] * 3
        + [pl.BlockSpec((rows, 128), lambda h, i: (0, 0))] * 3,
        out_specs=[part, column, column],
        out_shape=[jax.ShapeDtypeStruct((rows, width), BF16)] * 3,
        scratch_shapes=[pltpu.VMEM((rows, 128), F32)] * 2,
        compiler_params=pltpu.CompilerParams(vmem_limit_bytes=VMEM_LIMIT),
        cost_estimate=pl.CostEstimate(flops=0, bytes_accessed=0, transcendentals=0),
    )(begins[None], queries, keys, values, grads, logs, *tables, *tables)


ANY = pl.BlockSpec(memory_space=pl.ANY)


def call(name, kernel, marks, grid, ins, in_specs, outs, out_specs, after=(), flops=0, moved=0, scratch=()):
    given, waits = len(ins), len(after)

    def inner(mark, *refs):
        kernel(mark, *refs[:given], *refs[given + waits :])

    return pl.pallas_call(
        inner,
        grid_spec=pltpu.PrefetchScalarGridSpec(
            num_scalar_prefetch=1,
            grid=grid,
            in_specs=list(in_specs) + [ANY] * waits,
            out_specs=out_specs,
            scratch_shapes=scratch,
        ),
        out_shape=outs,
        name=name,
        compiler_params=pltpu.CompilerParams(vmem_limit_bytes=VMEM_LIMIT),
        cost_estimate=pl.CostEstimate(flops=0, bytes_accessed=0, transcendentals=0),
    )(marks, *ins, *after)


def fixed(*dims):
    return pl.BlockSpec(dims, lambda *_: (0,) * len(dims))


def shape(dims, kind):
    return jax.ShapeDtypeStruct(dims, kind)


def pick(values, at, axis):
    return lax.dynamic_index_in_dim(values, at, axis, keepdims=False)


def swap(values, axis, bit):
    size = lax.axis_size(axis)
    return lax.ppermute(values, axis, [(i, i ^ (1 << bit)) for i in range(size)])


CORE, CHIP, DP = 0, 1, 2


def rows_product(marks, lefts, weight, flipped, arrived=None, after=()):
    rows, depth = lefts[0].shape
    share = rows // 4
    width = weight.shape[-2] if flipped else weight.shape[-1]
    tile = 256
    count = len(lefts)
    keep = arrived is not None

    def kernel(mark, *refs):
        total = 0.0
        for j in range(count):
            left = refs[j][...].reshape(2 * share, depth)
            if flipped:
                total += over_columns(left, refs[count][j])
            else:
                total += jnp.dot(left, refs[count][...], preferred_element_type=F32)
        total = total.reshape(2, share, tile)
        if keep:
            total = total + refs[count + 1][...].astype(F32)
            first = mark[CHIP] == 0
            refs[-2][...] = jnp.where(first, total[1], total[0]).astype(BF16)
            refs[-1][...] = jnp.where(first, total[0], total[1])
        else:
            refs[-1][...] = total.astype(BF16)

    def of_core(i, mark):
        return (0, mark[CORE] if keep else 1 - mark[CORE], 0, 0)

    in_specs = [pl.BlockSpec((2, 1, share, depth), of_core)] * count
    if flipped:
        in_specs.append(pl.BlockSpec((count, tile, depth), lambda i, mark: (0, i, 0)))
    else:
        in_specs.append(pl.BlockSpec((depth, tile), lambda i, mark: (0, i)))
    ins = [left.reshape(2, 2, share, depth) for left in lefts] + [weight]
    pair = pl.BlockSpec((2, share, tile), lambda i, mark: (0, 0, i))
    one = pl.BlockSpec((share, tile), lambda i, mark: (0, i))
    if keep:
        ins.append(arrived)
        in_specs.append(pair)
        outs, out_specs = [shape((share, width), BF16), shape((share, width), F32)], [one, one]
    else:
        outs, out_specs = shape((2, share, width), BF16), pair
    return call(
        "rows_keep" if keep else "rows_send", kernel, marks, (width // tile,), ins, in_specs, outs, out_specs, after,
        flops=4 * share * depth * width * count, moved=2 * depth * width * count,
    )


def norm_rows(marks, tokens, kept, arrived, gain, shift, after=()):
    share, full = kept.shape
    block = min(128, share)
    steps = share // block

    def kernel(mark, x_ref, k_ref, a_ref, g_ref, s_ref, r_ref, n_ref):
        residual = x_ref[...].astype(F32) + (k_ref[...] + a_ref[...].astype(F32))
        unit, _ = norm_parts(residual)
        r_ref[...] = residual
        n_ref[...] = (unit * g_ref[...] + s_ref[...]).astype(BF16)

    rows = pl.BlockSpec((block, full), lambda i, mark: (i, 0))
    mine = pl.BlockSpec((block, full), lambda i, mark: ((2 * mark[CHIP] + mark[CORE]) * steps + i, 0))
    return call(
        "norm_rows", kernel, marks, (steps,), [tokens, kept, arrived, gain[None], shift[None]],
        [mine, rows, rows, fixed(1, full), fixed(1, full)],
        [shape((share, full), F32), shape((share, full), BF16)], [rows, rows], after,
        flops=10 * share * full, moved=14 * share * full,
    )


def norm_back_rows(marks, values, base, kept, arrived, gain, after=()):
    share, full = kept.shape
    block = min(128, share)
    steps = share // block

    def kernel(mark, x_ref, b_ref, k_ref, a_ref, g_ref, o_ref, l_ref, s_ref):
        unit, inverse = norm_parts(x_ref[...].astype(F32))
        grad = k_ref[...] + a_ref[...].astype(F32)
        out = b_ref[...].astype(F32) + norm_back(unit, inverse, g_ref[...], grad)
        o_ref[...] = out
        l_ref[...] = out.astype(BF16)

        @pl.when(pl.program_id(0) == 0)
        def _():
            s_ref[...] = jnp.zeros_like(s_ref)

        s_ref[0:1, :] += jnp.sum(grad * unit, axis=0, keepdims=True)
        s_ref[1:2, :] += jnp.sum(grad, axis=0, keepdims=True)

    rows = pl.BlockSpec((block, full), lambda i, mark: (i, 0))
    mine = pl.BlockSpec((block, full), lambda i, mark: ((2 * mark[CHIP] + mark[CORE]) * steps + i, 0))

    def where(of):
        return rows if of.shape[0] == share else mine

    return call(
        "norm_back_rows", kernel, marks, (steps,), [values, base, kept, arrived, gain[None]],
        [where(values), where(base), rows, rows, fixed(1, full)],
        [shape((share, full), F32), shape((share, full), BF16), shape((2, full), F32)],
        [rows, rows, fixed(2, full)], after,
        flops=20 * share * full, moved=18 * share * full,
    )


def spread(own):
    chip = swap(own, "tensor", 1)
    core = swap(own, "tensor", 0)
    return own, core, chip, swap(chip, "tensor", 0)


def gather_into(mark, parts, whole):
    share = parts[0].shape[0]
    for at, part in enumerate(parts):
        core = mark[CORE] if at % 2 == 0 else 1 - mark[CORE]
        chip = mark[CHIP] if at < 2 else 1 - mark[CHIP]
        first = pl.multiple_of((2 * chip + core) * share, share)
        whole[pl.ds(first, share), :] = part[...]


def hidden_back(marks, cotangent, weight, after=()):
    rows, full = cotangent.shape
    inner = weight.shape[0]
    block = min(256, rows)

    def kernel(mark, c_ref, w_ref, o_ref):
        o_ref[...] = over_columns(c_ref[...], w_ref[...]).astype(BF16)

    return call(
        "hidden_back", kernel, marks, (rows // block,), [cotangent, weight],
        [pl.BlockSpec((block, full), lambda i, mark: (i, 0)), fixed(inner, full)],
        shape((rows, inner), BF16), pl.BlockSpec((block, inner), lambda i, mark: (i, 0)), after,
        flops=2 * rows * full * inner, moved=2 * (rows * full + inner * full + rows * inner),
    )


def gate_up(marks, parts, weight, hidden_grad, after=()):
    share, full = parts[0].shape
    rows = 4 * share
    inner = weight.shape[2]
    tile = 128
    block = min(256, rows)

    def kernel(mark, p0, p1, p2, p3, w_ref, h_ref, second, hidden, hidden_t, gate_grad, up_grad):
        @pl.when(pl.program_id(0) == 0)
        def _():
            gather_into(mark, (p0, p1, p2, p3), second)

        both = jnp.concatenate([w_ref[0], w_ref[1]], axis=1)
        for first in range(0, rows, block):
            at = pl.ds(first, block)
            got = jnp.dot(second[at, :], both, preferred_element_type=F32)
            gate, up = got[:, :tile], got[:, tile:]
            sigmoid = 1.0 / (1.0 + jnp.exp(-gate))
            active = gate * sigmoid
            made = (active * up).astype(BF16)
            hidden[at, :] = made
            hidden_t[:, at] = made.T
            grad = h_ref[at, :].astype(F32)
            gate_grad[at, :] = (grad * up * (sigmoid * (1.0 + gate * (1.0 - sigmoid)))).astype(BF16)
            up_grad[at, :] = (grad * active).astype(BF16)

    column = pl.BlockSpec((rows, tile), lambda i, mark: (0, i))
    return call(
        "gate_up", kernel, marks, (inner // tile,), [*parts, weight, hidden_grad],
        [fixed(share, full)] * 4 + [pl.BlockSpec((2, full, tile), lambda i, mark: (0, 0, i)), column],
        [
            shape((rows, full), BF16), shape((rows, inner), BF16), shape((inner, rows), BF16),
            shape((rows, inner), BF16), shape((rows, inner), BF16),
        ],
        [fixed(rows, full), column, pl.BlockSpec((tile, rows), lambda i, mark: (i, 0)), column, column],
        after,
        flops=4 * rows * full * inner, moved=2 * (4 * full * inner + 2 * rows * full + 5 * rows * inner),
    )


def heads_back(marks, parts, weight, after=()):
    share, full = parts[0].shape
    rows = 4 * share
    width = weight.shape[0]

    def kernel(mark, p0, p1, p2, p3, w_ref, low, grad):
        @pl.when(pl.program_id(0) == 0)
        def _():
            gather_into(mark, (p0, p1, p2, p3), low)

        at = pl.ds(pl.multiple_of(pl.program_id(0) * share, share), share)
        grad[...] = over_columns(low[at, :], w_ref[...]).astype(BF16)

    return call(
        "heads_back", kernel, marks, (4,), [*parts, weight], [fixed(share, full)] * 4 + [fixed(width, full)],
        [shape((rows, full), BF16), shape((rows, width), BF16)],
        [fixed(rows, full), pl.BlockSpec((share, width), lambda i, mark: (i, 0))], after,
        flops=2 * rows * full * width, moved=2 * (2 * rows * full + full * width + rows * width),
    )


def bit_of(mark, bit):
    return (mark[DP] >> bit) & 1


def block_at(mark, order, flips, j):
    rest = len(order) - len(flips)
    index = 0
    for at, bit in enumerate(order):
        if at < len(flips):
            value = bit_of(mark, bit)
            value = 1 - value if flips[at] else value
        else:
            value = (j >> (rest - 1 - (at - len(flips)))) & 1
        index = index + (value << bit)
    return index


def weight_send(marks, order, columns, other, turned_out, after=()):
    size = lax.axis_size("dp")
    rows, full = columns.shape
    block = full // size
    count = size // 2
    dims = (other.shape[0], block) if turned_out else (block, other.shape[1])

    def kernel(mark, c_ref, o_ref, out):
        if turned_out:
            got = jnp.dot(o_ref[...], c_ref[...], preferred_element_type=F32)
        else:
            got = over_rows(c_ref[...], o_ref[...])
        out[0] = got.astype(BF16)

    return call(
        "weight_send", kernel, marks, (count,), [columns, other],
        [
            pl.BlockSpec((rows, block), lambda j, mark: (0, block_at(mark, order, (True,), j))),
            fixed(*other.shape),
        ],
        shape((count, *dims), BF16), pl.BlockSpec((1, *dims), lambda j, mark: (j, 0, 0)), after,
        flops=2 * rows * dims[0] * dims[1] * count,
        moved=rows * full + 2 * other.size + 2 * count * dims[0] * dims[1],
    )


def weight_keep(marks, order, columns, other, turned_out, arrived, after=()):
    size = lax.axis_size("dp")
    rows, full = columns.shape
    block = full // size
    half = size // 4
    dims = (other.shape[0], block) if turned_out else (block, other.shape[1])

    def kernel(mark, c_ref, o_ref, a_ref, send, keep):
        if turned_out:
            got = jnp.dot(o_ref[...], c_ref[...], preferred_element_type=F32)
        else:
            got = over_rows(c_ref[...], o_ref[...])
        got = got + a_ref[0].astype(F32)

        @pl.when(pl.program_id(0) < half)
        def _():
            send[0] = got.astype(BF16)

        @pl.when(pl.program_id(0) >= half)
        def _():
            keep[0] = got

    def block_for(j, mark):
        away = block_at(mark, order, (False, True), j)
        here = block_at(mark, order, (False, False), j - half)
        return jnp.where(j < half, away, here)

    def arrived_for(j, mark):
        mine = bit_of(mark, order[1])
        return jnp.where(j < half, (1 - mine) * half + j, mine * half + j - half)

    return call(
        "weight_keep", kernel, marks, (2 * half,), [columns, other, arrived],
        [
            pl.BlockSpec((rows, block), lambda j, mark: (0, block_for(j, mark))),
            fixed(*other.shape),
            pl.BlockSpec((1, *dims), lambda j, mark: (arrived_for(j, mark), 0, 0)),
        ],
        [shape((half, *dims), BF16), shape((half, *dims), F32)],
        [
            pl.BlockSpec((1, *dims), lambda j, mark: (jnp.minimum(j, half - 1), 0, 0)),
            pl.BlockSpec((1, *dims), lambda j, mark: (jnp.maximum(j - half, 0), 0, 0)),
        ],
        after,
        flops=2 * rows * dims[0] * dims[1] * 2 * half,
        moved=rows * full + 2 * other.size + 8 * half * dims[0] * dims[1],
    )


def finish(order, keep, arrived):
    me = lax.axis_index("dp")
    total = keep + arrived.astype(F32)
    for bit in order[2:]:
        mine = (me >> bit) & 1
        total = total.reshape(2, -1, *total.shape[1:])
        arrived = swap(pick(total, 1 - mine, 0).astype(BF16), "dp", bit)
        total = pick(total, mine, 0) + arrived.astype(F32)
    return total[0]


def plain_weight(columns, other, turned_out):
    if turned_out:
        got = jnp.einsum("fr,rd->fd", other, columns, preferred_element_type=F32)
    else:
        got = jnp.einsum("rd,rf->df", columns, other, preferred_element_type=F32)
    return lax.psum_scatter(
        got.astype(BF16), "dp", scatter_dimension=1 if turned_out else 0, tiled=True
    ).astype(F32)


def everywhere(values):
    for axis in ("dp", "tensor"):
        for bit in range(lax.axis_size(axis).bit_length() - 1):
            values = values + swap(values, axis, bit)
    return values


MESH = pl.DeviceIdType.MESH
QB = 128
SPAN = SEQ_MAX + QB
X_FIRST, Z_FIRST = (0, 1, 2), (1, 0, 2)


class Place:
    def __init__(self):
        self.dp, self.tensor = lax.axis_index("dp"), lax.axis_index("tensor")
        self.core, self.chip = lax.rem(self.tensor, 2), lax.div(self.tensor, 2)
        self.by_bit = [self.dp_partner(at) for at in range(3)]
        self.to_core = (self.dp, self.tensor + 1 - 2 * self.core)
        self.to_chip = (self.dp, self.tensor + 2 * (1 - 2 * self.chip))

    def bit(self, at):
        return lax.rem(lax.div(self.dp, 1 << at), 2)

    def dp_partner(self, at):
        return (self.dp + (1 - 2 * self.bit(at)) * (1 << at), self.tensor)

    def block(self, order, first, j):
        lead = self.bit(order[0])
        index = ((1 - lead) if first else lead) * (1 << order[0])
        rest = order[1:]
        for at, bit in enumerate(rest):
            index = index + lax.rem(lax.div(j, 1 << (len(rest) - 1 - at)), 2) * (1 << bit)
        return index


class Wires:
    def __init__(self, send, receive):
        self.send, self.receive, self.used, self.count = send, receive, [], 0

    def start(self, source, target, partner):
        at, self.count = self.count, self.count + 1
        copy = pltpu.make_async_remote_copy(
            src_ref=source,
            dst_ref=target,
            send_sem=self.send.at[at],
            recv_sem=self.receive.at[at],
            device_id=partner,
            device_id_type=MESH,
        )
        copy.start()
        self.used.append(copy)
        return copy

    def sent(self, copy):
        copy.wait_send()
        self.used = [other for other in self.used if other is not copy]

    def close(self):
        for copy in self.used:
            copy.wait_send()


class Arrays:
    def __init__(self):
        self.shapes = []

    def add(self, kind, *dims):
        self.shapes.append((dims, kind))
        return len(self.shapes) - 1


class Piece:
    def __init__(self, outs, order, block, width):
        self.order = order
        self.first = (outs.add(BF16, 4, block, width), outs.add(BF16, 4, block, width))
        self.kept = outs.add(BF16, 4, block, width)
        self.second = (outs.add(BF16, 2, block, width), outs.add(BF16, 2, block, width))
        self.third = (outs.add(BF16, block, width), outs.add(BF16, block, width))
        self.own = outs.add(F32, block, width)
        self.flying = None


def paired(values):
    lane = lax.broadcasted_iota(jnp.int32, (1, 2 * HD), 1)
    left = (lane < HD).astype(F32).astype(BF16)
    right = (lane >= HD).astype(F32).astype(BF16)
    return jnp.concatenate([values * left, values * right], axis=0)


def unpaired(values):
    return jnp.concatenate([values[:HD, :QB], values[HD:, QB:]], axis=0).T


def reach(row):
    first = max(0, row + QB - SPAN)
    return first, row + QB - first


def pair_bias(begins, row):
    first, count = reach(row)
    key_at = first + lax.broadcasted_iota(jnp.int32, (count, QB), 0)
    query_at = row + lax.broadcasted_iota(jnp.int32, (count, QB), 1)
    seen = (key_at >= begins[:, row : row + QB]) & (key_at <= query_at)
    bias = jnp.where(seen, 0.0, -1e30)
    return jnp.concatenate([bias, bias], axis=1)


FACTOR = HD**-0.5 * LOG2E


def attend_part(begins, qkv, heads_out, logs, part):
    rows, width = heads_out.shape

    def pair(h, _):
        lanes = pl.ds(pl.multiple_of(h * 2 * HD, 2 * HD), 2 * HD)
        for at in range(part, rows // QB, 2):
            row = at * QB
            first, count = reach(row)
            query = paired(qkv[0, row : row + QB, lanes])
            scores = over_columns(qkv[1, first : first + count, lanes], query) * FACTOR + pair_bias(begins, row)
            top = jnp.max(scores, axis=0, keepdims=True)
            probs = jnp.exp2(scores - top)
            total = jnp.sum(probs, axis=0, keepdims=True)
            got = over_rows(qkv[2, first : first + count, lanes], probs.astype(BF16))
            heads_out[row : row + QB, lanes] = unpaired(got * (1.0 / total)).astype(BF16)
            logs[h, at] = top + jnp.log2(total)
        return _

    lax.fori_loop(0, width // (2 * HD), pair, 0)


def attend_grads(begins, qkv, grads, logs, turn, ahead, behind, out, sum_k, sum_v, sum_b):
    rows, width = grads.shape
    scale = HD**-0.5

    def pair(h, _):
        lanes = pl.ds(pl.multiple_of(h * 2 * HD, 2 * HD), 2 * HD)
        sum_k[...] = jnp.zeros_like(sum_k)
        sum_v[...] = jnp.zeros_like(sum_v)
        bias_q = jnp.zeros((1, 2 * HD), F32)
        for at in range(rows // QB):
            row = at * QB
            first, count = reach(row)
            own, seen = slice(row, row + QB), slice(first, first + count)
            query, grad = paired(qkv[0, own, lanes]), paired(grads[own, lanes])
            key, value = qkv[1, seen, lanes], qkv[2, seen, lanes]
            scores = over_columns(key, query) * FACTOR + pair_bias(begins, row)
            probs = jnp.exp2(scores - logs[h, at])
            weighed = probs * over_columns(value, grad)
            inner = jnp.sum(weighed, axis=0, keepdims=True)
            score_grad = (weighed - probs * inner).astype(BF16)
            sum_v[seen, :] += jnp.dot(probs.astype(BF16), grad, preferred_element_type=F32)
            sum_k[seen, :] += jnp.dot(score_grad, query, preferred_element_type=F32)
            got = unpaired(over_rows(key, score_grad)) * scale
            got = turned(got, turn[own, :], -ahead[own, :], -behind[own, :]).astype(BF16)
            out[0, own, lanes] = got
            bias_q += jnp.sum(got.astype(F32), axis=0, keepdims=True)
        key_grad = turned(sum_k[...] * scale, turn[...], -ahead[...], -behind[...]).astype(BF16)
        value_grad = sum_v[...].astype(BF16)
        out[1, :, lanes] = key_grad
        out[2, :, lanes] = value_grad
        sum_b[0:1, lanes] = bias_q
        sum_b[1:2, lanes] = jnp.sum(key_grad.astype(F32), axis=0, keepdims=True)
        sum_b[2:3, lanes] = jnp.sum(value_grad.astype(F32), axis=0, keepdims=True)
        return _

    lax.fori_loop(0, width // (2 * HD), pair, 0)


def pipe_rows(place, lefts, weight, flipped, send, arrived=None, kept=None):
    rows, depth = lefts[0].shape
    share = rows // 4
    width = weight.shape[-2] if flipped else weight.shape[-1]
    tile = 512
    count = len(lefts)
    keep = arrived is not None
    core = place.core if keep else 1 - place.core

    def left_rows(ref):
        return jnp.concatenate(
            [ref[pl.ds(pl.multiple_of((2 * y + core) * share, share), share), :] for y in range(2)], axis=0
        )

    def body(w_ref, *refs):
        total = 0.0
        for j in range(count):
            if flipped:
                total += over_columns(left_rows(lefts[j]), w_ref[j])
            else:
                total += jnp.dot(left_rows(lefts[j]), w_ref[...], preferred_element_type=F32)
        if keep:
            low = total[:share] + refs[0][0].astype(F32)
            high = total[share:] + refs[0][1].astype(F32)
            first = place.chip == 0
            refs[-1][...] = jnp.where(first, high, low).astype(BF16)
            at = pl.ds(pl.multiple_of(pl.program_id(0) * tile, tile), tile)
            kept[:, at] = jnp.where(first, low, high)
        else:
            refs[-1][...] = total.reshape(2, share, tile).astype(BF16)

    if flipped:
        in_specs = [pl.BlockSpec((count, tile, depth), lambda i: (0, i, 0))]
    else:
        in_specs = [pl.BlockSpec((depth, tile), lambda i: (0, i))]
    pair = pl.BlockSpec((2, share, tile), lambda i: (0, 0, i))
    one = pl.BlockSpec((share, tile), lambda i: (0, i))
    pltpu.emit_pipeline(
        body,
        grid=(width // tile,),
        in_specs=in_specs + ([pair] if keep else []),
        out_specs=[one if keep else pair],
    )(weight, *([arrived] if keep else []), send)


def pipe_weight(place, order, first, columns, others, outs):
    block = outs[0].shape[1]

    def body(*refs):
        for z in range(2):
            at = place.block(order, first, 2 * pl.program_id(0) + z)
            taken = columns[:, pl.ds(pl.multiple_of(at * block, block), block)]
            for other, ref in zip(others, refs):
                ref[z] = over_rows(taken, other[...]).astype(BF16)

    pltpu.emit_pipeline(
        body,
        grid=(2,),
        out_specs=[pl.BlockSpec((2, block, out.shape[2]), lambda j: (j, 0, 0)) for out in outs],
    )(*outs)


def pipe_second(mine, kept, arrived, send):
    _, rows, width = kept.shape
    tile = min(128, rows)
    spec = pl.BlockSpec((2, tile, width), lambda i: (1 - mine, i, 0))

    def body(k_ref, a_ref, o_ref):
        o_ref[...] = (k_ref[...].astype(F32) + a_ref[...].astype(F32)).astype(BF16)

    pltpu.emit_pipeline(
        body,
        grid=(rows // tile,),
        in_specs=[spec, spec],
        out_specs=[pl.BlockSpec((2, tile, width), lambda i: (0, i, 0))],
    )(kept, arrived, send)


def pipe_third(mine, first, kept, arrived, second, send, own):
    _, rows, width = kept.shape
    tile = min(128, rows)
    spec = pl.BlockSpec((2, tile, width), lambda i: (mine, i, 0))
    one = pl.BlockSpec((tile, width), lambda i: (i, 0))

    def body(k_ref, a_ref, b_ref, s_ref, o_ref):
        low, high = (
            k_ref[at].astype(F32) + a_ref[at].astype(F32) + b_ref[at].astype(F32) for at in range(2)
        )
        s_ref[...] = jnp.where(first, high, low).astype(BF16)
        o_ref[...] = jnp.where(first, low, high)

    pltpu.emit_pipeline(
        body,
        grid=(rows // tile,),
        in_specs=[spec, spec, pl.BlockSpec((2, tile, width), lambda i: (0, i, 0))],
        out_specs=[one, one],
    )(kept, arrived, second, send, own)


def finished(results, qkv, out, gate_up, down, block_at, input_at, sums_at):
    wide, tall = [*gate_up, *qkv], [out, down]
    steps = 4
    block = results[qkv[0].own].shape[0]
    part = block // steps

    def kernel(*refs):
        given, made = refs[: 2 * len(wide + tall) + 3], refs[2 * len(wide + tall) + 3 :]

        def total(at):
            return given[2 * at][...] + given[2 * at + 1][...].astype(F32)

        for at in range(len(gate_up)):
            made[0][at] = total(at)
        for at in range(len(qkv)):
            made[1][at] = total(len(gate_up) + at)
        for at in range(len(tall)):

            @pl.when(pl.program_id(0) == 0)
            def _():
                made[2 + at][...] = total(len(wide) + at).T

        made[4][...] = given[-3][...]
        made[5][...] = given[-2][...]
        made[6][...] = given[-1][4:7, :]
        made[7][0:1, :], made[7][1:2, :] = given[-1][0:1, :], given[-1][2:3, :]
        made[8][0:1, :], made[8][1:2, :] = given[-1][1:2, :], given[-1][3:4, :]

    ins, in_specs = [], []
    for p in wide:
        for at in (p.own, p.third[1]):
            ins.append(results[at])
            in_specs.append(pl.BlockSpec((part, results[at].shape[1]), lambda i: (i, 0)))
    for p in tall:
        for at in (p.own, p.third[1]):
            ins.append(results[at])
            in_specs.append(at_zero(*results[at].shape))
    inner, width = results[down.own].shape[1], results[out.own].shape[1]
    share, full = results[block_at].shape
    by_row = pl.BlockSpec((share // steps, full), lambda i: (i, 0))
    got = pl.pallas_call(
        kernel,
        name="finished",
        grid=(steps,),
        in_specs=in_specs + [by_row, by_row, at_zero(8, full)],
        out_specs=[
            pl.BlockSpec((2, part, inner), lambda i: (0, i, 0)),
            pl.BlockSpec((3, part, width), lambda i: (0, i, 0)),
            at_zero(width, block), at_zero(inner, block), by_row, by_row,
            at_zero(3, full), at_zero(2, full), at_zero(2, full),
        ],
        out_shape=[
            shape((2, block, inner), F32), shape((3, block, width), F32), shape((width, block), F32),
            shape((inner, block), F32), shape((share, full), BF16), shape((share, full), F32),
            shape((3, full), F32), shape((2, full), F32), shape((2, full), F32),
        ],
        compiler_params=pltpu.CompilerParams(vmem_limit_bytes=VMEM_LIMIT),
    )(*ins, results[block_at], results[input_at], results[sums_at])
    return got[4], got[5], got[1], got[6], got[2], got[0], got[3], got[7], got[8]


def at_zero(*dims):
    return pl.BlockSpec(dims, lambda *_: (0,) * len(dims))


def forward(tokens, cotangent, qkv_weight, bias, out_weight, gate_up_weight, down_weight, gains, shifts, begins, tables):
    rows, full = tokens.shape
    width, inner = out_weight.shape[0], down_weight.shape[0]
    share = rows // 4
    half = share // 2
    ins = [
        tokens, cotangent, qkv_weight, bias[:, None, :], out_weight, gate_up_weight, down_weight,
        gains, shifts, begins, *tables,
    ]
    outs = Arrays()
    for dims in ((rows, full), (rows, full), (rows, inner), (rows, inner), (rows, inner), (rows, width), (3, rows, width)):
        outs.add(BF16, *dims)
    outs.add(F32, width // 128, rows // QB, 1, 2 * QB)
    outs.add(F32, share, full)
    given, made = len(ins), len(outs.shapes)
    scratch = Arrays()
    for _, dims in enumerate(outs.shapes[1:]):
        scratch.add(dims[1], *dims[0])
    cot_at, out_weight_at = scratch.add(BF16, rows, full), scratch.add(BF16, width, full)
    tables_at = [scratch.add(F32, rows, 128) for _ in range(3)]
    begins_at = scratch.add(jnp.int32, 1, rows)
    gains_at, shifts_at = scratch.add(F32, 2, full), scratch.add(F32, 2, full)
    own_at, kept_at = scratch.add(BF16, share, full), scratch.add(F32, share, full)
    to_core_at = scratch.add(BF16, 2, half, full)
    fore = [
        [to_core_at, scratch.add(BF16, 2, half, full), scratch.add(BF16, half, full), scratch.add(BF16, half, full)]
        for _ in range(2)
    ]
    kinds = [pltpu.VMEM(dims, kind) for dims, kind in scratch.shapes]
    kinds += [pltpu.SemaphoreType.DMA((16,)), pltpu.SemaphoreType.DMA((16,)), pltpu.SemaphoreType.DMA((24,))]

    def kernel(*refs):
        tok, cot, w_qkv, b_qkv, w_out, w_gate_up, w_down, gain_in, shift_in, begin_in, *tables_in = refs[:given]
        o, s = refs[given : given + made], refs[given + made :]
        sends, receives, locals_ = s[-3:]
        sec_v, hidden, gate_grad, up_grad, heads, qkv_v, logs, residual = s[: made - 1]
        cot_v, w_out_v, kept = s[cot_at], s[out_weight_at], s[kept_at]
        turn, ahead, behind = (s[at] for at in tables_at)
        begin, gain, shift, own = s[begins_at], s[gains_at], s[shifts_at], s[own_at]
        place = Place()
        partners = [place.to_core, place.to_chip]
        wires = Wires(sends, receives)
        stays = []

        def load(source, target):
            copy = pltpu.make_async_copy(source, target, locals_.at[len(stays)])
            copy.start()
            stays.append(copy)
            return copy

        def quarter(at, tensor, part=None):
            if part is None:
                return at.at[pl.ds(pl.multiple_of(tensor * share, share), share), :]
            return at.at[pl.ds(pl.multiple_of(tensor * share + part * half, half), half), :]

        mine, beyond = place.tensor, place.core + 2 * (1 - place.chip)
        barrier = pltpu.get_barrier_semaphore()
        for partner in partners:
            pl.semaphore_signal(barrier, inc=1, device_id=partner, device_id_type=MESH)
        early = [load(gain_in, gain), load(shift_in, shift)]
        soon = [
            load(tables_in[0], turn), load(tables_in[1], ahead), load(tables_in[2], behind),
            load(begin_in, begin),
        ]
        later = [load(quarter(tok, mine), own), load(w_out, w_out_v), load(cot, cot_v)]
        for copy in early:
            copy.wait()

        def norm_first(t_ref):
            unit, _ = norm_parts(t_ref[...].astype(F32))
            at = pl.ds(pl.multiple_of(pl.program_id(0) * half, half), half)
            sec_v[at, :] = (unit * gain[0:1, :] + shift[0:1, :]).astype(BF16)

        pltpu.emit_pipeline(
            norm_first, grid=(rows // half,), in_specs=[pl.BlockSpec((half, full), lambda i: (i, 0))]
        )(tok)
        keep_normed = load(sec_v, o[0])
        for copy in soon:
            copy.wait()

        def project(first_of, count, turns):
            def body(w_ref, b_ref):
                j = first_of + pl.program_id(0)
                lanes = pl.ds(pl.multiple_of(pl.program_id(1) * 256, 256), 256)
                for first in range(0, rows, 256):
                    at = slice(first, first + 256)
                    got = jnp.dot(sec_v[at, :], w_ref[0], preferred_element_type=F32) + b_ref[0]
                    if turns:
                        got = turned(got, turn[at, :], ahead[at, :], behind[at, :])
                    qkv_v[j, at, lanes] = got.astype(BF16)

            pltpu.emit_pipeline(
                body,
                grid=(count, width // 256),
                in_specs=[
                    pl.BlockSpec((1, full, 256), lambda j, i: (first_of + j, 0, i)),
                    pl.BlockSpec((1, 1, 256), lambda j, i: (first_of + j, 0, i)),
                ],
            )(w_qkv, b_qkv)

        project(0, 2, True)
        project(2, 1, False)

        def project_out(part):
            to_core, from_core = s[fore[part][0]], s[fore[part][1]]
            places = [(2 * y + c) * share + part * half for c in (1 - place.core, place.core) for y in range(2)]
            left = jnp.concatenate([heads[pl.ds(pl.multiple_of(at, half), half), :] for at in places], axis=0)
            for first in range(0, full, 512):
                at = slice(first, first + 512)
                got = jnp.dot(left, w_out_v[:, at], preferred_element_type=F32)
                to_core[:, :, at] = got[:share].reshape(2, half, 512).astype(BF16)
                kept[:, at] = got[share:]
            return wires.start(to_core, from_core, place.to_core)

        def add_core(part, flying):
            from_core, to_chip, from_chip = (s[at] for at in fore[part][1:])
            flying.wait_recv()
            wires.sent(flying)
            low = kept[:half, :] + from_core[0].astype(F32)
            high = kept[half:, :] + from_core[1].astype(F32)
            first = place.chip == 0
            at = slice(part * half, (part + 1) * half)
            residual[at, :] = own[at, :].astype(F32) + jnp.where(first, low, high)
            to_chip[...] = jnp.where(first, high, low).astype(BF16)
            return wires.start(to_chip, from_chip, place.to_chip)

        def norm_second(part, flying):
            flying.wait_recv()
            at = slice(part * half, (part + 1) * half)
            got = residual[at, :] + s[fore[part][3]][...].astype(F32)
            residual[at, :] = got
            unit, _ = norm_parts(got)
            rows_at = quarter(sec_v, mine, part)
            rows_at[...] = (unit * gain[1:2, :] + shift[1:2, :]).astype(BF16)
            return (
                wires.start(rows_at, rows_at, place.to_chip),
                wires.start(rows_at, rows_at, place.to_core),
            )

        def pass_on(part, chip_flying):
            chip_flying.wait_recv()
            rows_at = quarter(sec_v, beyond, part)
            return wires.start(rows_at, rows_at, place.to_core)

        def hidden_back(first, count, tile):
            def body(w_ref):
                lanes = pl.ds(pl.multiple_of((first + pl.program_id(0)) * tile, tile), tile)
                up_grad[:, lanes] = over_columns(cot_v[...], w_ref[...]).astype(BF16)

            pltpu.emit_pipeline(
                body, grid=(count,), in_specs=[pl.BlockSpec((tile, full), lambda i: (i, 0))]
            )(w_down.at[pl.ds(first * tile, count * tile), :])

        def gate_up(part, begin_at, count, tile):
            def body(w_ref):
                lanes = pl.ds(pl.multiple_of((begin_at + pl.program_id(0)) * tile, tile), tile)
                for q in range(0, 4, 2):
                    spots = [slice((q + z) * share + part * half, (q + z) * share + (part + 1) * half) for z in range(2)]
                    left = jnp.concatenate([sec_v[at, :] for at in spots], axis=0)
                    both = [jnp.dot(left, w_ref[j], preferred_element_type=F32) for j in range(2)]
                    for z, at in enumerate(spots):
                        gates, ups = (of[z * half : (z + 1) * half, :] for of in both)
                        sigmoid = 1.0 / (1.0 + jnp.exp(-gates))
                        active = gates * sigmoid
                        grad = up_grad[at, lanes].astype(F32)
                        hidden[at, lanes] = (active * ups).astype(BF16)
                        gate_grad[at, lanes] = (
                            grad * ups * (sigmoid * (1.0 + gates * (1.0 - sigmoid)))
                        ).astype(BF16)
                        up_grad[at, lanes] = (grad * active).astype(BF16)

            pltpu.emit_pipeline(
                body, grid=(count,), in_specs=[pl.BlockSpec((2, full, tile), lambda i: (0, 0, i))]
            )(w_gate_up.at[:, :, pl.ds(begin_at * tile, count * tile)])

        wide_tiles = inner // 256 - 1

        def gate_ups(part):
            gate_up(part, 0, wide_tiles, 256)
            gate_up(part, 2 * wide_tiles, inner // 128 - 2 * wide_tiles, 128)

        attend_part(begin, qkv_v, heads, logs, 0)
        keep_normed.wait()
        for copy in later:
            copy.wait()
        pl.semaphore_wait(barrier, len(partners))
        flying = project_out(0)
        attend_part(begin, qkv_v, heads, logs, 1)
        chip0 = add_core(0, flying)
        flying = project_out(1)
        kept_early = [load(heads, o[5]), load(qkv_v, o[6]), load(logs, o[7])]
        hidden_back(2 * wide_tiles, inner // 128 - 2 * wide_tiles, 128)
        chip1 = add_core(1, flying)
        hidden_back(0, wide_tiles, 256)
        chip0, core0 = norm_second(0, chip0)
        chip1, core1 = norm_second(1, chip1)
        both0 = pass_on(0, chip0)
        core0.wait_recv()
        both0.wait_recv()
        gate_ups(0)
        both1 = pass_on(1, chip1)
        core1.wait_recv()
        both1.wait_recv()
        kept_early += [load(sec_v, o[1]), load(residual, o[8])]
        gate_ups(1)

        late = [load(hidden, o[2]), load(gate_grad, o[3]), load(up_grad, o[4])]
        for copy in [*kept_early, *late]:
            copy.wait()
        wires.close()

    return pl.pallas_call(
        kernel,
        name="forward",
        in_specs=[ANY] * given,
        out_specs=[ANY] * made,
        out_shape=[shape(dims, kind) for dims, kind in outs.shapes],
        scratch_shapes=kinds,
        compiler_params=pltpu.CompilerParams(
            vmem_limit_bytes=62 << 20, collective_id=1, has_side_effects=True
        ),
    )(*ins)


def backward(
    tokens, cotangent, qkv_weight, out_weight, gate_up_weight, down_weight, gains, begins, tables, saved
):
    rows, full = tokens.shape
    width, inner = out_weight.shape[0], down_weight.shape[0]
    share, block = rows // 4, full // 8
    half = share // 2
    ins = [
        tokens, cotangent, qkv_weight, out_weight, gate_up_weight, down_weight, gains, begins, *tables, *saved,
    ]
    outs = Arrays()
    down, up = Piece(outs, X_FIRST, block, inner), Piece(outs, X_FIRST, block, inner)
    gate = Piece(outs, Z_FIRST, block, inner)
    out = Piece(outs, X_FIRST, block, width)
    qkv = [Piece(outs, X_FIRST, block, width) for _ in range(3)]
    pieces = [down, gate, up, out, *qkv]
    rows_out = [[outs.add(BF16, 2, share, full) for _ in range(2)] + [outs.add(BF16, share, full)] for _ in range(3)]
    block_at, input_at, sums_at = outs.add(BF16, share, full), outs.add(F32, share, full), outs.add(F32, 8, full)
    given, made = len(ins), len(outs.shapes)

    scratch = Arrays()
    for array in saved[1:]:
        scratch.add(array.dtype, *array.shape)
    cot_at, low_rows, out_weight_at = scratch.add(BF16, rows, full), scratch.add(BF16, rows, full), scratch.add(BF16, width, full)
    heads_grad_at, qkv_grad_at = scratch.add(BF16, rows, width), scratch.add(BF16, 3, rows, width)
    tables_at = [scratch.add(F32, rows, 128) for _ in range(3)]
    begins_at, gains_at = scratch.add(jnp.int32, 1, rows), scratch.add(F32, 2, full)
    own_at = scratch.add(BF16, share, full)
    residual_grad_at, kept_at = (scratch.add(F32, share, full) for _ in range(2))
    chip_in = [scratch.add(BF16, share, full) for _ in range(3)]
    sum_k_at, sum_v_at = scratch.add(F32, rows, 128), scratch.add(F32, rows, 128)
    sum_b_at = scratch.add(F32, 8, width)
    held_at, came_at = scratch.add(F32, 6, 8, full), scratch.add(F32, 5, 8, full)
    kinds = [pltpu.VMEM(dims, kind) for dims, kind in scratch.shapes]
    kinds += [pltpu.SemaphoreType.DMA((48,)), pltpu.SemaphoreType.DMA((48,)), pltpu.SemaphoreType.DMA((24,))]

    def kernel(*refs):
        tok, cot, w_qkv, w_out, w_gate_up, w_down, gain_in, begin_in = refs[:8]
        tables_in, saved_in = refs[8:11], refs[11:given]
        o, s = refs[given : given + made], refs[given + made :]
        sends, receives, locals_ = s[-3:]
        sec_v, hidden, gate_grad, up_grad, heads, qkv_v, logs, residual = s[: len(saved) - 1]
        cot_v, low_v, w_out_v = s[cot_at], s[low_rows], s[out_weight_at]
        heads_grad, qkv_grad = s[heads_grad_at], s[qkv_grad_at]
        turn, ahead, behind = (s[at] for at in tables_at)
        begin, gain, own = s[begins_at], s[gains_at], s[own_at]
        residual_grad, kept = s[residual_grad_at], s[kept_at]
        held, came, sum_b = s[held_at], s[came_at], s[sum_b_at]
        place = Place()
        partners = [*place.by_bit, place.to_core, place.to_chip]
        wires = Wires(sends, receives)
        stays = []

        def load(source, target):
            copy = pltpu.make_async_copy(source, target, locals_.at[len(stays)])
            copy.start()
            stays.append(copy)
            return copy

        def quarter(at, tensor, part=None):
            if part is None:
                return at.at[pl.ds(pl.multiple_of(tensor * share, share), share), :]
            return at.at[pl.ds(pl.multiple_of(tensor * share + part * half, half), half), :]

        mine, beyond = place.tensor, place.core + 2 * (1 - place.chip)
        barrier = pltpu.get_barrier_semaphore()
        for partner in partners:
            pl.semaphore_signal(barrier, inc=1, device_id=partner, device_id_type=MESH)
        loads = [load(cot, cot_v), load(saved_in[2], hidden)]
        loads_second = [load(saved_in[1], sec_v), load(saved_in[3], gate_grad), load(saved_in[4], up_grad)]
        loads_rest = [
            load(saved_in[5], heads), load(saved_in[6], qkv_v), load(saved_in[7], logs), load(saved_in[8], residual),
            load(w_out, w_out_v), load(gain_in, gain), load(begin_in, begin),
            load(tables_in[0], turn), load(tables_in[1], ahead), load(tables_in[2], behind),
        ]
        pl.semaphore_wait(barrier, len(partners))

        def first_half(those, columns, others):
            order = those[0].order
            pipe_weight(place, order, True, columns, others, [o[p.first[0]] for p in those])
            for p in those:
                p.flying = wires.start(o[p.first[0]], o[p.first[1]], place.by_bit[order[0]])

        def second_half(those, columns, others):
            pipe_weight(place, those[0].order, False, columns, others, [o[p.kept] for p in those])

        def then(p):
            p.flying.wait_recv()
            pipe_second(place.bit(p.order[1]), o[p.kept], o[p.first[1]], o[p.second[0]])
            p.flying = wires.start(o[p.second[0]], o[p.second[1]], place.by_bit[p.order[1]])

        def last(p):
            p.flying.wait_recv()
            pipe_third(
                place.bit(p.order[1]), place.bit(p.order[2]) == 0, o[p.kept], o[p.first[1]], o[p.second[1]],
                o[p.third[0]], o[p.own],
            )
            p.flying = wires.start(o[p.third[0]], o[p.third[1]], place.by_bit[p.order[2]])

        def rows_first(at, lefts, weight, flipped):
            pipe_rows(place, lefts, weight, flipped, o[rows_out[at][0]])
            return wires.start(o[rows_out[at][0]], o[rows_out[at][1]], place.to_core)

        def rows_then(at, lefts, weight, flipped, flying, into):
            flying.wait_recv()
            pipe_rows(place, lefts, weight, flipped, o[rows_out[at][2]], o[rows_out[at][1]], into)
            return wires.start(o[rows_out[at][2]], s[chip_in[at]], place.to_chip)

        def norm_grads(values, base, arrived, row, result, low):
            for part in range(2):
                at = slice(part * half, (part + 1) * half)
                unit, inverse = norm_parts(values[at, :].astype(F32))
                grad = kept[at, :] + arrived[at, :].astype(F32)
                got = base[at, :].astype(F32) + norm_back(unit, inverse, gain[row : row + 1, :], grad)
                result[at, :] = got
                if low is not None:
                    low[at, :] = got.astype(BF16)
                held[0, 2 * row : 2 * row + 1, :] += jnp.sum(grad * unit, axis=0, keepdims=True)
                held[0, 2 * row + 1 : 2 * row + 2, :] += jnp.sum(grad, axis=0, keepdims=True)

        def add_everywhere(step):
            order = [place.to_core, place.to_chip, place.by_bit[1], place.by_bit[2], place.by_bit[0]]
            return wires.start(held.at[step], came.at[step], order[step])

        def added(step, flying):
            flying.wait_recv()
            held[step + 1] = held[step] + came[step]

        grads = [gate_grad, up_grad]
        lows = [qkv_grad.at[j] for j in range(3)]
        for copy in loads:
            copy.wait()
        first_half([down], cot_v, [hidden])
        for copy in loads_second:
            copy.wait()
        first_half([gate], sec_v, [gate_grad])
        second_half([down], cot_v, [hidden])
        flying = rows_first(0, grads, w_gate_up, True)
        first_half([up], sec_v, [up_grad])
        chip = rows_then(0, grads, w_gate_up, True, flying, kept)
        second_half([gate], sec_v, [gate_grad])
        second_half([up], sec_v, [up_grad])
        renormed = load(saved_in[0], sec_v)
        for copy in loads_rest:
            copy.wait()
        held[0] = jnp.zeros_like(held[0])
        chip.wait_recv()
        norm_grads(residual, quarter(cot_v, mine), s[chip_in[0]], 1, residual_grad, quarter(low_v, mine))
        mine_v, beyond_v = quarter(low_v, mine), quarter(low_v, beyond)
        chip = wires.start(mine_v, mine_v, place.to_chip)
        core = wires.start(mine_v, mine_v, place.to_core)
        flying = rows_first(1, [hidden], w_down, False)
        branch_chip = rows_then(1, [hidden], w_down, False, flying, kept)
        then(down)
        chip.wait_recv()
        both = wires.start(beyond_v, beyond_v, place.to_core)
        core.wait_recv()
        both.wait_recv()
        for first in range(0, rows, 256):
            at = slice(first, first + 256)
            heads_grad[at, :] = over_columns(low_v[at, :], w_out_v[...]).astype(BF16)
        first_half([out], low_v, [heads])
        then(gate)
        attend_grads(
            begin, qkv_v, heads_grad, logs, turn, ahead, behind, qkv_grad, s[sum_k_at], s[sum_v_at], sum_b
        )
        renormed.wait()
        first_half(qkv, sec_v, lows)
        flying = rows_first(2, lows, w_qkv, True)
        branch_chip.wait_recv()
        own[...] = (residual[...] + kept[...] + s[chip_in[1]][...].astype(F32)).astype(BF16)
        keep_block = load(own, o[block_at])
        last(down)
        chip = rows_then(2, lows, w_qkv, True, flying, kept)
        second_half([out], low_v, [heads])
        second_half(qkv, sec_v, lows)
        then(up)
        chip.wait_recv()
        keep_block.wait()
        back = load(quarter(tok, mine), own)
        back.wait()
        norm_grads(own, residual_grad, s[chip_in[2]], 0, residual, None)
        keep_input = load(residual, o[input_at])
        held[0, 4:7, pl.ds(pl.multiple_of(place.tensor * width, 128), width)] = sum_b[0:3, :]
        flying = add_everywhere(0)
        then(out)
        added(0, flying)
        flying = add_everywhere(1)
        last(gate)
        added(1, flying)
        last(up)
        last(out)
        flying = add_everywhere(2)
        then(qkv[0])
        added(2, flying)
        flying = add_everywhere(3)
        then(qkv[1])
        last(qkv[0])
        added(3, flying)
        flying = add_everywhere(4)
        then(qkv[2])
        last(qkv[1])
        added(4, flying)
        keep_sums = load(held.at[5], o[sums_at])
        last(qkv[2])
        for p in pieces:
            p.flying.wait_recv()
        keep_input.wait()
        keep_sums.wait()
        wires.close()

    results = pl.pallas_call(
        kernel,
        name="backward",
        in_specs=[ANY] * given,
        out_specs=[ANY] * made,
        out_shape=[shape(dims, kind) for dims, kind in outs.shapes],
        scratch_shapes=kinds,
        compiler_params=pltpu.CompilerParams(
            vmem_limit_bytes=62 << 20, collective_id=2, has_side_effects=True
        ),
    )(*ins)
    return finished(results, qkv, out, [gate, up], down, block_at, input_at, sums_at)


def body(
    tokens,
    seq_lengths,
    qkv_weight,
    qkv_bias,
    out_weight,
    gate_up_weight,
    down_weight,
    norm_gains,
    norm_shifts,
    cotangent,
):
    row_count, full_width = tokens.shape
    local_width = qkv_weight.shape[2]
    tensor_at, dp_at, dp_size = lax.axis_index("tensor"), lax.axis_index("dp"), lax.axis_size("dp")
    marks = jnp.stack([tensor_at & 1, tensor_at >> 1, dp_at]).astype(jnp.int32)
    bits = dp_size.bit_length() - 1
    x_first = tuple(range(bits))
    z_first = (1, 0) + x_first[2:]
    fine = (full_width // dp_size) % 128 == 0

    def send(order, columns, other, turned_out, after):
        if not fine:
            return columns
        return weight_send(marks, order, columns, other, turned_out, after)

    def keep(order, columns, other, turned_out, sent, after):
        if not fine:
            return columns, None
        return weight_keep(
            marks, order, columns, other, turned_out, swap(sent, "dp", order[0]), after
        )

    def total(order, columns, other, turned_out, kept):
        if not fine:
            return plain_weight(columns, other, turned_out)
        return finish(order, kept[1], swap(kept[0], "dp", order[1]))

    begins, *tables = positions(seq_lengths[0], row_count)
    if dp_size == 8 and lax.axis_size("tensor") == 4:
        saved = forward(
            tokens, cotangent, qkv_weight, qkv_bias.astype(F32), out_weight, gate_up_weight, down_weight,
            norm_gains, norm_shifts, begins[None], tables,
        )
        return backward(
            tokens, cotangent, qkv_weight, out_weight, gate_up_weight, down_weight, norm_gains, begins[None],
            tables, saved,
        )
    normed, queries, keys, values = project(
        tokens, qkv_weight, qkv_bias, norm_gains[0], norm_shifts[0], tables
    )
    heads_out, logs = attend(begins, queries, keys, values)
    sent = rows_product(marks, [heads_out], out_weight, False)
    to_chip, own = rows_product(marks, [heads_out], out_weight, False, swap(sent, "tensor", 0))
    hidden_grad = hidden_back(marks, cotangent, down_weight, [own])
    residual, second_own = norm_rows(
        marks, tokens, own, swap(to_chip, "tensor", 1), norm_gains[1], norm_shifts[1], [hidden_grad]
    )
    second, hidden, hidden_t, gate_grad, up_grad = gate_up(
        marks, spread(second_own), gate_up_weight, hidden_grad
    )
    down_sent = send(x_first, cotangent, hidden_t, True, [])
    second_sent = rows_product(marks, [gate_grad, up_grad], gate_up_weight, True, None, [down_sent])
    up_sent = send(x_first, second, up_grad, False, [second_sent])
    to_chip, own = rows_product(
        marks, [gate_grad, up_grad], gate_up_weight, True, swap(second_sent, "tensor", 0), [up_sent]
    )
    gate_sent = send(z_first, second, gate_grad, False, [own])
    branch_sent = rows_product(marks, [hidden], down_weight, False, None, [gate_sent])
    branch_to_chip, branch_own = rows_product(
        marks, [hidden], down_weight, False, swap(branch_sent, "tensor", 0), [gate_sent]
    )
    residual_grad, residual_low_own, second_sums = norm_back_rows(
        marks, residual, cotangent, own, swap(to_chip, "tensor", 1), norm_gains[1], [branch_own]
    )
    block_out = (
        residual + branch_own + swap(branch_to_chip, "tensor", 1).astype(F32)
    ).astype(BF16)
    down_kept = keep(x_first, cotangent, hidden_t, True, down_sent, [residual_low_own])
    residual_low, heads_grad = heads_back(
        marks, spread(residual_low_own), out_weight, [down_kept[0]]
    )
    heads_t = heads_out.T
    out_sent = send(x_first, residual_low, heads_t, True, [heads_grad])
    projected_low = attend_back(begins, queries, keys, values, heads_grad, logs, tables)
    gate_kept = keep(z_first, second, gate_grad, False, gate_sent, [projected_low[0]])
    qkv_sent = []
    before = gate_kept[0]
    for grads in projected_low:
        before = send(x_first, normed, grads, False, [before])
        qkv_sent.append(before)
    normed_sent = rows_product(marks, projected_low, qkv_weight, True, None, [before])
    up_kept = keep(x_first, second, up_grad, False, up_sent, [normed_sent])
    to_chip, own = rows_product(
        marks, projected_low, qkv_weight, True, swap(normed_sent, "tensor", 0), [normed_sent]
    )
    input_grad, _, first_sums = norm_back_rows(
        marks, tokens, residual_grad, own, swap(to_chip, "tensor", 1), norm_gains[0], [up_kept[0]]
    )
    bias_local = jnp.stack([jnp.sum(g, axis=0, dtype=F32) for g in projected_low])
    bias_placed = lax.dynamic_update_slice(
        jnp.zeros((3, full_width), F32), bias_local, (0, tensor_at * local_width)
    )
    sums = everywhere(jnp.concatenate([first_sums, second_sums, bias_placed], axis=0))
    out_kept = keep(x_first, residual_low, heads_t, True, out_sent, [input_grad])
    qkv_kept = []
    before = out_kept[0]
    for grads, sent in zip(projected_low, qkv_sent):
        kept = keep(x_first, normed, grads, False, sent, [before])
        before = kept[0]
        qkv_kept.append(kept)
    return (
        block_out,
        input_grad,
        jnp.stack(
            [total(x_first, normed, g, False, k) for g, k in zip(projected_low, qkv_kept)]
        ),
        sums[4:7],
        total(x_first, residual_low, heads_t, True, out_kept),
        jnp.stack(
            [
                total(z_first, second, gate_grad, False, gate_kept),
                total(x_first, second, up_grad, False, up_kept),
            ]
        ),
        total(x_first, cotangent, hidden_t, True, down_kept),
        jnp.stack([sums[0], sums[2]]),
        jnp.stack([sums[1], sums[3]]),
    )


def solution(mesh):
    return jax.shard_map(
        body,
        mesh=mesh,
        in_specs=(
            P("dp", None),
            P("dp", None),
            P(None, None, "tensor"),
            P(None, "tensor"),
            P("tensor", None),
            P(None, None, "tensor"),
            P("tensor", None),
            P(),
            P(),
            P("dp", None),
        ),
        out_specs=(
            P(("dp", "tensor"), None),
            P(("dp", "tensor"), None),
            P(None, "dp", "tensor"),
            P(),
            P("tensor", "dp"),
            P(None, "dp", "tensor"),
            P("tensor", "dp"),
            P(),
            P(),
        ),
        check_vma=False,
    )
```

```python
import functools

import jax
import jax.numpy as jnp
from jax import lax
from jax.experimental import pallas as pl
from jax.experimental.pallas import tpu as pltpu
from jax.sharding import PartitionSpec as P

HD = 64
SEQ_MAX = 512
BQ = 256
F32 = jnp.float32
BF16 = jnp.bfloat16
LOG2E = 1.4426950408889634
VMEM_LIMIT = 60 * 1024 * 1024


def norm_parts(values):
    centred = values - jnp.mean(values, axis=-1, keepdims=True)
    inverse = lax.rsqrt(jnp.mean(centred * centred, axis=-1, keepdims=True) + 1e-05)
    return (centred * inverse, inverse)


def norm_back(unit, inverse, gain_row, grad_rows):
    scaled = grad_rows * gain_row
    return inverse * (
        scaled
        - jnp.mean(scaled, axis=-1, keepdims=True)
        - unit * jnp.mean(scaled * unit, axis=-1, keepdims=True)
    )


def positions(lengths, row_count):
    indices = jnp.arange(row_count, dtype=jnp.int32)
    count = lengths.shape[0]
    order = jnp.arange(count, dtype=jnp.int32)
    ends_at = jnp.sum(jnp.where(order[:, None] <= order[None, :], lengths[:, None], 0), axis=0)
    passed = indices[:, None] >= ends_at[None, :]
    begins = jnp.sum(jnp.where(passed, lengths[None, :], 0), axis=1, dtype=jnp.int32)
    places = (indices - begins).astype(F32)
    half = HD // 8
    lane = jnp.arange(128, dtype=jnp.int32) % HD
    rates = 10000.0 ** (-((lane % half).astype(F32) / half))
    angles = places[:, None] * rates[None, :]
    cosine, sine = jnp.cos(angles), jnp.sin(angles)
    turn = jnp.where(lane < 2 * half, cosine, 1.0)
    ahead = jnp.where(lane < half, -sine, 0.0)
    behind = jnp.where((lane >= half) & (lane < 2 * half), sine, 0.0)
    return begins, turn, ahead, behind


def turned(values, turn, ahead, behind):
    half = HD // 8
    width = values.shape[1]
    times = width // turn.shape[1]

    def wide(table):
        return jnp.concatenate([table] * times, axis=1) if times > 1 else table

    return (
        values * wide(turn)
        + pltpu.roll(values, width - half, 1) * wide(ahead)
        + pltpu.roll(values, half, 1) * wide(behind)
    )


def qkv_kernel(x_ref, w_ref, b_ref, g_ref, s_ref, c_ref, a_ref, h_ref, n_ref, q_ref, k_ref, v_ref):
    unit, _ = norm_parts(x_ref[...].astype(F32))
    normed = (unit * g_ref[...] + s_ref[...]).astype(BF16)
    n_ref[...] = normed
    for j, out in enumerate((q_ref, k_ref, v_ref)):
        got = jnp.dot(normed, w_ref[j], preferred_element_type=F32) + b_ref[j : j + 1, :]
        if j < 2:
            got = turned(got, c_ref[...], a_ref[...], h_ref[...])
        out[...] = got.astype(BF16)


def project(tokens, weight, bias, gain, shift, tables):
    rows, full = tokens.shape
    width = weight.shape[2]
    block = min(256, rows)

    def whole(*dims):
        return pl.BlockSpec(dims, lambda i: (0,) * len(dims))

    def by_row(columns):
        return pl.BlockSpec((block, columns), lambda i: (i, 0))

    return pl.pallas_call(
        qkv_kernel,
        name="project",
        grid=(rows // block,),
        in_specs=[
            by_row(full),
            whole(3, full, width),
            whole(3, width),
            whole(1, full),
            whole(1, full),
            by_row(128),
            by_row(128),
            by_row(128),
        ],
        out_specs=[by_row(full), by_row(width), by_row(width), by_row(width)],
        out_shape=[jax.ShapeDtypeStruct((rows, full), BF16)]
        + [jax.ShapeDtypeStruct((rows, width), BF16)] * 3,
        compiler_params=pltpu.CompilerParams(vmem_limit_bytes=VMEM_LIMIT),
        cost_estimate=pl.CostEstimate(flops=0, bytes_accessed=0, transcendentals=0),
    )(tokens, weight, bias.astype(F32), gain[None], shift[None], *tables)


def spans(step, blocks):
    most = SEQ_MAX // BQ + 1
    forms = []
    for at in range(min(most - 1, blocks)):
        forms.append((step == at, 0, (at + 1) * BQ))
    if blocks >= most:
        first = pl.multiple_of((step - (most - 1)) * BQ, BQ)
        forms.append((step >= most - 1, first, most * BQ))
    return forms


def allowed_bias(begin_row, first, count, step):
    key_at = first + lax.broadcasted_iota(jnp.int32, (count, BQ), 0)
    query_at = step * BQ + lax.broadcasted_iota(jnp.int32, (count, BQ), 1)
    return jnp.where((key_at >= begin_row) & (key_at <= query_at), 0.0, -1e30)


def over_rows(left, right):
    return lax.dot_general(left, right, (((0,), (0,)), ((), ())), preferred_element_type=F32)


def over_columns(left, right):
    return lax.dot_general(left, right, (((1,), (1,)), ((), ())), preferred_element_type=F32)


def attend_kernel(blocks, begin_ref, q_ref, k_ref, v_ref, o_ref, l_ref):
    step = pl.program_id(1)
    factor = HD**-0.5 * LOG2E

    def one(first, count):
        bias = allowed_bias(begin_ref[...], first, count, step)
        rows = pl.ds(first, count)
        parts = []
        for head in range(2):
            lanes = slice(head * HD, (head + 1) * HD)
            scores = over_columns(k_ref[rows, lanes], q_ref[:, lanes]) * factor + bias
            top = jnp.max(scores, axis=0, keepdims=True)
            probs = jnp.exp2(scores - top)
            total = jnp.sum(probs, axis=0, keepdims=True)
            got = over_rows(v_ref[rows, lanes], probs.astype(BF16))
            parts.append(got * (1.0 / total))
            l_ref[head] = top + jnp.log2(total)
        o_ref[...] = jnp.concatenate(parts, axis=0).T.astype(BF16)

    for condition, first, count in spans(step, blocks):
        pl.when(condition)(functools.partial(one, first, count))


def attend(begins, queries, keys, values):
    rows, width = queries.shape
    blocks = rows // BQ
    return pl.pallas_call(
        functools.partial(attend_kernel, blocks),
        name="attend",
        grid=(width // 128, blocks),
        in_specs=[
            pl.BlockSpec((1, BQ), lambda h, i: (0, i)),
            pl.BlockSpec((BQ, 128), lambda h, i: (i, h)),
            pl.BlockSpec((rows, 128), lambda h, i: (0, h)),
            pl.BlockSpec((rows, 128), lambda h, i: (0, h)),
        ],
        out_specs=[
            pl.BlockSpec((BQ, 128), lambda h, i: (i, h)),
            pl.BlockSpec((2, 1, BQ), lambda h, i: (h, 0, i)),
        ],
        out_shape=[
            jax.ShapeDtypeStruct((rows, width), BF16),
            jax.ShapeDtypeStruct((width // HD, 1, rows), F32),
        ],
        compiler_params=pltpu.CompilerParams(vmem_limit_bytes=VMEM_LIMIT),
        cost_estimate=pl.CostEstimate(flops=0, bytes_accessed=0, transcendentals=0),
    )(begins[None], queries, keys, values)


def attend_back_kernel(
    blocks, begin_ref, q_ref, k_ref, v_ref, g_ref, l_ref, cq_ref, aq_ref, hq_ref, c_ref, a_ref, h_ref,
    dq_ref, dk_ref, dv_ref, sum_k, sum_v,
):
    step = pl.program_id(1)
    scale = HD**-0.5
    factor = scale * LOG2E

    @pl.when(step == 0)
    def _():
        sum_k[...] = jnp.zeros_like(sum_k)
        sum_v[...] = jnp.zeros_like(sum_v)

    def one(first, count):
        bias = allowed_bias(begin_ref[...], first, count, step)
        rows = pl.ds(first, count)
        dq, dk, dv = [], [], []
        for head in range(2):
            lanes = slice(head * HD, (head + 1) * HD)
            query, key, value, grad = q_ref[:, lanes], k_ref[rows, lanes], v_ref[rows, lanes], g_ref[:, lanes]
            probs = jnp.exp2(over_columns(key, query) * factor + bias - l_ref[head])
            weighed = probs * over_columns(value, grad)
            inner = jnp.sum(weighed, axis=0, keepdims=True)
            score_grad = (weighed - probs * inner).astype(BF16)
            dv.append(jnp.dot(probs.astype(BF16), grad, preferred_element_type=F32))
            dk.append(jnp.dot(score_grad, query, preferred_element_type=F32))
            dq.append(over_rows(key, score_grad))
        sum_k[rows, :] += jnp.concatenate(dk, axis=1)
        sum_v[rows, :] += jnp.concatenate(dv, axis=1)
        query_grad = jnp.concatenate(dq, axis=0).T * scale
        dq_ref[...] = turned(query_grad, cq_ref[...], -aq_ref[...], -hq_ref[...]).astype(BF16)

    for condition, first, count in spans(step, blocks):
        pl.when(condition)(functools.partial(one, first, count))

    @pl.when(step == blocks - 1)
    def _():
        dk_ref[...] = turned(sum_k[...] * scale, c_ref[...], -a_ref[...], -h_ref[...]).astype(BF16)
        dv_ref[...] = sum_v[...].astype(BF16)


def attend_back(begins, queries, keys, values, grads, logs, tables):
    rows, width = queries.shape
    blocks = rows // BQ
    part = pl.BlockSpec((BQ, 128), lambda h, i: (i, h))
    column = pl.BlockSpec((rows, 128), lambda h, i: (0, h))
    return pl.pallas_call(
        functools.partial(attend_back_kernel, blocks),
        name="attend_back",
        grid=(width // 128, blocks),
        in_specs=[
            pl.BlockSpec((1, BQ), lambda h, i: (0, i)),
            part,
            column,
            column,
            part,
            pl.BlockSpec((2, 1, BQ), lambda h, i: (h, 0, i)),
        ]
        + [pl.BlockSpec((BQ, 128), lambda h, i: (i, 0))] * 3
        + [pl.BlockSpec((rows, 128), lambda h, i: (0, 0))] * 3,
        out_specs=[part, column, column],
        out_shape=[jax.ShapeDtypeStruct((rows, width), BF16)] * 3,
        scratch_shapes=[pltpu.VMEM((rows, 128), F32)] * 2,
        compiler_params=pltpu.CompilerParams(vmem_limit_bytes=VMEM_LIMIT),
        cost_estimate=pl.CostEstimate(flops=0, bytes_accessed=0, transcendentals=0),
    )(begins[None], queries, keys, values, grads, logs, *tables, *tables)


ANY = pl.BlockSpec(memory_space=pl.ANY)


def call(name, kernel, marks, grid, ins, in_specs, outs, out_specs, after=(), flops=0, moved=0, scratch=()):
    given, waits = len(ins), len(after)

    def inner(mark, *refs):
        kernel(mark, *refs[:given], *refs[given + waits :])

    return pl.pallas_call(
        inner,
        grid_spec=pltpu.PrefetchScalarGridSpec(
            num_scalar_prefetch=1,
            grid=grid,
            in_specs=list(in_specs) + [ANY] * waits,
            out_specs=out_specs,
            scratch_shapes=scratch,
        ),
        out_shape=outs,
        name=name,
        compiler_params=pltpu.CompilerParams(vmem_limit_bytes=VMEM_LIMIT),
        cost_estimate=pl.CostEstimate(flops=0, bytes_accessed=0, transcendentals=0),
    )(marks, *ins, *after)


def fixed(*dims):
    return pl.BlockSpec(dims, lambda *_: (0,) * len(dims))


def shape(dims, kind):
    return jax.ShapeDtypeStruct(dims, kind)


def pick(values, at, axis):
    return lax.dynamic_index_in_dim(values, at, axis, keepdims=False)


def swap(values, axis, bit):
    size = lax.axis_size(axis)
    return lax.ppermute(values, axis, [(i, i ^ (1 << bit)) for i in range(size)])


CORE, CHIP, DP = 0, 1, 2


def rows_product(marks, lefts, weight, flipped, arrived=None, after=()):
    rows, depth = lefts[0].shape
    share = rows // 4
    width = weight.shape[-2] if flipped else weight.shape[-1]
    tile = 256
    count = len(lefts)
    keep = arrived is not None

    def kernel(mark, *refs):
        total = 0.0
        for j in range(count):
            left = refs[j][...].reshape(2 * share, depth)
            if flipped:
                total += over_columns(left, refs[count][j])
            else:
                total += jnp.dot(left, refs[count][...], preferred_element_type=F32)
        total = total.reshape(2, share, tile)
        if keep:
            total = total + refs[count + 1][...].astype(F32)
            first = mark[CHIP] == 0
            refs[-2][...] = jnp.where(first, total[1], total[0]).astype(BF16)
            refs[-1][...] = jnp.where(first, total[0], total[1])
        else:
            refs[-1][...] = total.astype(BF16)

    def of_core(i, mark):
        return (0, mark[CORE] if keep else 1 - mark[CORE], 0, 0)

    in_specs = [pl.BlockSpec((2, 1, share, depth), of_core)] * count
    if flipped:
        in_specs.append(pl.BlockSpec((count, tile, depth), lambda i, mark: (0, i, 0)))
    else:
        in_specs.append(pl.BlockSpec((depth, tile), lambda i, mark: (0, i)))
    ins = [left.reshape(2, 2, share, depth) for left in lefts] + [weight]
    pair = pl.BlockSpec((2, share, tile), lambda i, mark: (0, 0, i))
    one = pl.BlockSpec((share, tile), lambda i, mark: (0, i))
    if keep:
        ins.append(arrived)
        in_specs.append(pair)
        outs, out_specs = [shape((share, width), BF16), shape((share, width), F32)], [one, one]
    else:
        outs, out_specs = shape((2, share, width), BF16), pair
    return call(
        "rows_keep" if keep else "rows_send", kernel, marks, (width // tile,), ins, in_specs, outs, out_specs, after,
        flops=4 * share * depth * width * count, moved=2 * depth * width * count,
    )


def norm_rows(marks, tokens, kept, arrived, gain, shift, after=()):
    share, full = kept.shape
    block = min(128, share)
    steps = share // block

    def kernel(mark, x_ref, k_ref, a_ref, g_ref, s_ref, r_ref, n_ref):
        residual = x_ref[...].astype(F32) + (k_ref[...] + a_ref[...].astype(F32))
        unit, _ = norm_parts(residual)
        r_ref[...] = residual
        n_ref[...] = (unit * g_ref[...] + s_ref[...]).astype(BF16)

    rows = pl.BlockSpec((block, full), lambda i, mark: (i, 0))
    mine = pl.BlockSpec((block, full), lambda i, mark: ((2 * mark[CHIP] + mark[CORE]) * steps + i, 0))
    return call(
        "norm_rows", kernel, marks, (steps,), [tokens, kept, arrived, gain[None], shift[None]],
        [mine, rows, rows, fixed(1, full), fixed(1, full)],
        [shape((share, full), F32), shape((share, full), BF16)], [rows, rows], after,
        flops=10 * share * full, moved=14 * share * full,
    )


def norm_back_rows(marks, values, base, kept, arrived, gain, after=()):
    share, full = kept.shape
    block = min(128, share)
    steps = share // block

    def kernel(mark, x_ref, b_ref, k_ref, a_ref, g_ref, o_ref, l_ref, s_ref):
        unit, inverse = norm_parts(x_ref[...].astype(F32))
        grad = k_ref[...] + a_ref[...].astype(F32)
        out = b_ref[...].astype(F32) + norm_back(unit, inverse, g_ref[...], grad)
        o_ref[...] = out
        l_ref[...] = out.astype(BF16)

        @pl.when(pl.program_id(0) == 0)
        def _():
            s_ref[...] = jnp.zeros_like(s_ref)

        s_ref[0:1, :] += jnp.sum(grad * unit, axis=0, keepdims=True)
        s_ref[1:2, :] += jnp.sum(grad, axis=0, keepdims=True)

    rows = pl.BlockSpec((block, full), lambda i, mark: (i, 0))
    mine = pl.BlockSpec((block, full), lambda i, mark: ((2 * mark[CHIP] + mark[CORE]) * steps + i, 0))

    def where(of):
        return rows if of.shape[0] == share else mine

    return call(
        "norm_back_rows", kernel, marks, (steps,), [values, base, kept, arrived, gain[None]],
        [where(values), where(base), rows, rows, fixed(1, full)],
        [shape((share, full), F32), shape((share, full), BF16), shape((2, full), F32)],
        [rows, rows, fixed(2, full)], after,
        flops=20 * share * full, moved=18 * share * full,
    )


def spread(own):
    chip = swap(own, "tensor", 1)
    core = swap(own, "tensor", 0)
    return own, core, chip, swap(chip, "tensor", 0)


def gather_into(mark, parts, whole):
    share = parts[0].shape[0]
    for at, part in enumerate(parts):
        core = mark[CORE] if at % 2 == 0 else 1 - mark[CORE]
        chip = mark[CHIP] if at < 2 else 1 - mark[CHIP]
        first = pl.multiple_of((2 * chip + core) * share, share)
        whole[pl.ds(first, share), :] = part[...]


def hidden_back(marks, cotangent, weight, after=()):
    rows, full = cotangent.shape
    inner = weight.shape[0]
    block = min(256, rows)

    def kernel(mark, c_ref, w_ref, o_ref):
        o_ref[...] = over_columns(c_ref[...], w_ref[...]).astype(BF16)

    return call(
        "hidden_back", kernel, marks, (rows // block,), [cotangent, weight],
        [pl.BlockSpec((block, full), lambda i, mark: (i, 0)), fixed(inner, full)],
        shape((rows, inner), BF16), pl.BlockSpec((block, inner), lambda i, mark: (i, 0)), after,
        flops=2 * rows * full * inner, moved=2 * (rows * full + inner * full + rows * inner),
    )


def gate_up(marks, parts, weight, hidden_grad, after=()):
    share, full = parts[0].shape
    rows = 4 * share
    inner = weight.shape[2]
    tile = 128
    block = min(256, rows)

    def kernel(mark, p0, p1, p2, p3, w_ref, h_ref, second, hidden, hidden_t, gate_grad, up_grad):
        @pl.when(pl.program_id(0) == 0)
        def _():
            gather_into(mark, (p0, p1, p2, p3), second)

        both = jnp.concatenate([w_ref[0], w_ref[1]], axis=1)
        for first in range(0, rows, block):
            at = pl.ds(first, block)
            got = jnp.dot(second[at, :], both, preferred_element_type=F32)
            gate, up = got[:, :tile], got[:, tile:]
            sigmoid = 1.0 / (1.0 + jnp.exp(-gate))
            active = gate * sigmoid
            made = (active * up).astype(BF16)
            hidden[at, :] = made
            hidden_t[:, at] = made.T
            grad = h_ref[at, :].astype(F32)
            gate_grad[at, :] = (grad * up * (sigmoid * (1.0 + gate * (1.0 - sigmoid)))).astype(BF16)
            up_grad[at, :] = (grad * active).astype(BF16)

    column = pl.BlockSpec((rows, tile), lambda i, mark: (0, i))
    return call(
        "gate_up", kernel, marks, (inner // tile,), [*parts, weight, hidden_grad],
        [fixed(share, full)] * 4 + [pl.BlockSpec((2, full, tile), lambda i, mark: (0, 0, i)), column],
        [
            shape((rows, full), BF16), shape((rows, inner), BF16), shape((inner, rows), BF16),
            shape((rows, inner), BF16), shape((rows, inner), BF16),
        ],
        [fixed(rows, full), column, pl.BlockSpec((tile, rows), lambda i, mark: (i, 0)), column, column],
        after,
        flops=4 * rows * full * inner, moved=2 * (4 * full * inner + 2 * rows * full + 5 * rows * inner),
    )


def heads_back(marks, parts, weight, after=()):
    share, full = parts[0].shape
    rows = 4 * share
    width = weight.shape[0]

    def kernel(mark, p0, p1, p2, p3, w_ref, low, grad):
        @pl.when(pl.program_id(0) == 0)
        def _():
            gather_into(mark, (p0, p1, p2, p3), low)

        at = pl.ds(pl.multiple_of(pl.program_id(0) * share, share), share)
        grad[...] = over_columns(low[at, :], w_ref[...]).astype(BF16)

    return call(
        "heads_back", kernel, marks, (4,), [*parts, weight], [fixed(share, full)] * 4 + [fixed(width, full)],
        [shape((rows, full), BF16), shape((rows, width), BF16)],
        [fixed(rows, full), pl.BlockSpec((share, width), lambda i, mark: (i, 0))], after,
        flops=2 * rows * full * width, moved=2 * (2 * rows * full + full * width + rows * width),
    )


def bit_of(mark, bit):
    return (mark[DP] >> bit) & 1


def block_at(mark, order, flips, j):
    rest = len(order) - len(flips)
    index = 0
    for at, bit in enumerate(order):
        if at < len(flips):
            value = bit_of(mark, bit)
            value = 1 - value if flips[at] else value
        else:
            value = (j >> (rest - 1 - (at - len(flips)))) & 1
        index = index + (value << bit)
    return index


def weight_send(marks, order, columns, other, turned_out, after=()):
    size = lax.axis_size("dp")
    rows, full = columns.shape
    block = full // size
    count = size // 2
    dims = (other.shape[0], block) if turned_out else (block, other.shape[1])

    def kernel(mark, c_ref, o_ref, out):
        if turned_out:
            got = jnp.dot(o_ref[...], c_ref[...], preferred_element_type=F32)
        else:
            got = over_rows(c_ref[...], o_ref[...])
        out[0] = got.astype(BF16)

    return call(
        "weight_send", kernel, marks, (count,), [columns, other],
        [
            pl.BlockSpec((rows, block), lambda j, mark: (0, block_at(mark, order, (True,), j))),
            fixed(*other.shape),
        ],
        shape((count, *dims), BF16), pl.BlockSpec((1, *dims), lambda j, mark: (j, 0, 0)), after,
        flops=2 * rows * dims[0] * dims[1] * count,
        moved=rows * full + 2 * other.size + 2 * count * dims[0] * dims[1],
    )


def weight_keep(marks, order, columns, other, turned_out, arrived, after=()):
    size = lax.axis_size("dp")
    rows, full = columns.shape
    block = full // size
    half = size // 4
    dims = (other.shape[0], block) if turned_out else (block, other.shape[1])

    def kernel(mark, c_ref, o_ref, a_ref, send, keep):
        if turned_out:
            got = jnp.dot(o_ref[...], c_ref[...], preferred_element_type=F32)
        else:
            got = over_rows(c_ref[...], o_ref[...])
        got = got + a_ref[0].astype(F32)

        @pl.when(pl.program_id(0) < half)
        def _():
            send[0] = got.astype(BF16)

        @pl.when(pl.program_id(0) >= half)
        def _():
            keep[0] = got

    def block_for(j, mark):
        away = block_at(mark, order, (False, True), j)
        here = block_at(mark, order, (False, False), j - half)
        return jnp.where(j < half, away, here)

    def arrived_for(j, mark):
        mine = bit_of(mark, order[1])
        return jnp.where(j < half, (1 - mine) * half + j, mine * half + j - half)

    return call(
        "weight_keep", kernel, marks, (2 * half,), [columns, other, arrived],
        [
            pl.BlockSpec((rows, block), lambda j, mark: (0, block_for(j, mark))),
            fixed(*other.shape),
            pl.BlockSpec((1, *dims), lambda j, mark: (arrived_for(j, mark), 0, 0)),
        ],
        [shape((half, *dims), BF16), shape((half, *dims), F32)],
        [
            pl.BlockSpec((1, *dims), lambda j, mark: (jnp.minimum(j, half - 1), 0, 0)),
            pl.BlockSpec((1, *dims), lambda j, mark: (jnp.maximum(j - half, 0), 0, 0)),
        ],
        after,
        flops=2 * rows * dims[0] * dims[1] * 2 * half,
        moved=rows * full + 2 * other.size + 8 * half * dims[0] * dims[1],
    )


def finish(order, keep, arrived):
    me = lax.axis_index("dp")
    total = keep + arrived.astype(F32)
    for bit in order[2:]:
        mine = (me >> bit) & 1
        total = total.reshape(2, -1, *total.shape[1:])
        arrived = swap(pick(total, 1 - mine, 0).astype(BF16), "dp", bit)
        total = pick(total, mine, 0) + arrived.astype(F32)
    return total[0]


def plain_weight(columns, other, turned_out):
    if turned_out:
        got = jnp.einsum("fr,rd->fd", other, columns, preferred_element_type=F32)
    else:
        got = jnp.einsum("rd,rf->df", columns, other, preferred_element_type=F32)
    return lax.psum_scatter(
        got.astype(BF16), "dp", scatter_dimension=1 if turned_out else 0, tiled=True
    ).astype(F32)


def everywhere(values):
    for axis in ("dp", "tensor"):
        for bit in range(lax.axis_size(axis).bit_length() - 1):
            values = values + swap(values, axis, bit)
    return values


MESH = pl.DeviceIdType.MESH
QB = 128
SPAN = SEQ_MAX + QB
X_FIRST, Z_FIRST = (0, 1, 2), (1, 0, 2)


class Place:
    def __init__(self):
        self.dp, self.tensor = lax.axis_index("dp"), lax.axis_index("tensor")
        self.core, self.chip = lax.rem(self.tensor, 2), lax.div(self.tensor, 2)
        self.by_bit = [self.dp_partner(at) for at in range(3)]
        self.to_core = (self.dp, self.tensor + 1 - 2 * self.core)
        self.to_chip = (self.dp, self.tensor + 2 * (1 - 2 * self.chip))

    def bit(self, at):
        return lax.rem(lax.div(self.dp, 1 << at), 2)

    def dp_partner(self, at):
        return (self.dp + (1 - 2 * self.bit(at)) * (1 << at), self.tensor)

    def block(self, order, first, j):
        lead = self.bit(order[0])
        index = ((1 - lead) if first else lead) * (1 << order[0])
        rest = order[1:]
        for at, bit in enumerate(rest):
            index = index + lax.rem(lax.div(j, 1 << (len(rest) - 1 - at)), 2) * (1 << bit)
        return index


class Wires:
    def __init__(self, send, receive):
        self.send, self.receive, self.used, self.count = send, receive, [], 0

    def start(self, source, target, partner):
        at, self.count = self.count, self.count + 1
        copy = pltpu.make_async_remote_copy(
            src_ref=source,
            dst_ref=target,
            send_sem=self.send.at[at],
            recv_sem=self.receive.at[at],
            device_id=partner,
            device_id_type=MESH,
        )
        copy.start()
        self.used.append(copy)
        return copy

    def sent(self, copy):
        copy.wait_send()
        self.used = [other for other in self.used if other is not copy]

    def close(self):
        for copy in self.used:
            copy.wait_send()


class Arrays:
    def __init__(self):
        self.shapes = []

    def add(self, kind, *dims):
        self.shapes.append((dims, kind))
        return len(self.shapes) - 1


class Piece:
    def __init__(self, outs, order, block, width):
        self.order = order
        self.first = (outs.add(BF16, 4, block, width), outs.add(BF16, 4, block, width))
        self.kept = outs.add(BF16, 4, block, width)
        self.second = (outs.add(BF16, 2, block, width), outs.add(BF16, 2, block, width))
        self.third = (outs.add(BF16, block, width), outs.add(BF16, block, width))
        self.own = outs.add(F32, block, width)
        self.flying = None


def paired(values):
    lane = lax.broadcasted_iota(jnp.int32, (1, 2 * HD), 1)
    left = (lane < HD).astype(F32).astype(BF16)
    right = (lane >= HD).astype(F32).astype(BF16)
    return jnp.concatenate([values * left, values * right], axis=0)


def unpaired(values):
    return jnp.concatenate([values[:HD, :QB], values[HD:, QB:]], axis=0).T


def reach(row):
    first = max(0, row + QB - SPAN)
    return first, row + QB - first


def pair_bias(begins, row):
    first, count = reach(row)
    key_at = first + lax.broadcasted_iota(jnp.int32, (count, QB), 0)
    query_at = row + lax.broadcasted_iota(jnp.int32, (count, QB), 1)
    seen = (key_at >= begins[:, row : row + QB]) & (key_at <= query_at)
    bias = jnp.where(seen, 0.0, -1e30)
    return jnp.concatenate([bias, bias], axis=1)


FACTOR = HD**-0.5 * LOG2E


def attend_part(begins, qkv, heads_out, logs, part):
    rows, width = heads_out.shape

    def pair(h, _):
        lanes = pl.ds(pl.multiple_of(h * 2 * HD, 2 * HD), 2 * HD)
        for at in range(part, rows // QB, 2):
            row = at * QB
            first, count = reach(row)
            query = paired(qkv[0, row : row + QB, lanes])
            scores = over_columns(qkv[1, first : first + count, lanes], query) * FACTOR + pair_bias(begins, row)
            top = jnp.max(scores, axis=0, keepdims=True)
            probs = jnp.exp2(scores - top)
            total = jnp.sum(probs, axis=0, keepdims=True)
            got = over_rows(qkv[2, first : first + count, lanes], probs.astype(BF16))
            heads_out[row : row + QB, lanes] = unpaired(got * (1.0 / total)).astype(BF16)
            logs[h, at] = top + jnp.log2(total)
        return _

    lax.fori_loop(0, width // (2 * HD), pair, 0)


def attend_grads(begins, qkv, grads, logs, turn, ahead, behind, out, sum_k, sum_v, sum_b):
    rows, width = grads.shape
    scale = HD**-0.5

    def pair(h, _):
        lanes = pl.ds(pl.multiple_of(h * 2 * HD, 2 * HD), 2 * HD)
        sum_k[...] = jnp.zeros_like(sum_k)
        sum_v[...] = jnp.zeros_like(sum_v)
        bias_q = jnp.zeros((1, 2 * HD), F32)
        for at in range(rows // QB):
            row = at * QB
            first, count = reach(row)
            own, seen = slice(row, row + QB), slice(first, first + count)
            query, grad = paired(qkv[0, own, lanes]), paired(grads[own, lanes])
            key, value = qkv[1, seen, lanes], qkv[2, seen, lanes]
            scores = over_columns(key, query) * FACTOR + pair_bias(begins, row)
            probs = jnp.exp2(scores - logs[h, at])
            weighed = probs * over_columns(value, grad)
            inner = jnp.sum(weighed, axis=0, keepdims=True)
            score_grad = (weighed - probs * inner).astype(BF16)
            sum_v[seen, :] += jnp.dot(probs.astype(BF16), grad, preferred_element_type=F32)
            sum_k[seen, :] += jnp.dot(score_grad, query, preferred_element_type=F32)
            got = unpaired(over_rows(key, score_grad)) * scale
            got = turned(got, turn[own, :], -ahead[own, :], -behind[own, :]).astype(BF16)
            out[0, own, lanes] = got
            bias_q += jnp.sum(got.astype(F32), axis=0, keepdims=True)
        key_grad = turned(sum_k[...] * scale, turn[...], -ahead[...], -behind[...]).astype(BF16)
        value_grad = sum_v[...].astype(BF16)
        out[1, :, lanes] = key_grad
        out[2, :, lanes] = value_grad
        sum_b[0:1, lanes] = bias_q
        sum_b[1:2, lanes] = jnp.sum(key_grad.astype(F32), axis=0, keepdims=True)
        sum_b[2:3, lanes] = jnp.sum(value_grad.astype(F32), axis=0, keepdims=True)
        return _

    lax.fori_loop(0, width // (2 * HD), pair, 0)


def pipe_rows(place, lefts, weight, flipped, send, arrived=None, kept=None):
    rows, depth = lefts[0].shape
    share = rows // 4
    width = weight.shape[-2] if flipped else weight.shape[-1]
    tile = 512
    count = len(lefts)
    keep = arrived is not None
    core = place.core if keep else 1 - place.core

    def left_rows(ref):
        return jnp.concatenate(
            [ref[pl.ds(pl.multiple_of((2 * y + core) * share, share), share), :] for y in range(2)], axis=0
        )

    def body(w_ref, *refs):
        total = 0.0
        for j in range(count):
            if flipped:
                total += over_columns(left_rows(lefts[j]), w_ref[j])
            else:
                total += jnp.dot(left_rows(lefts[j]), w_ref[...], preferred_element_type=F32)
        if keep:
            low = total[:share] + refs[0][0].astype(F32)
            high = total[share:] + refs[0][1].astype(F32)
            first = place.chip == 0
            refs[-1][...] = jnp.where(first, high, low).astype(BF16)
            at = pl.ds(pl.multiple_of(pl.program_id(0) * tile, tile), tile)
            kept[:, at] = jnp.where(first, low, high)
        else:
            refs[-1][...] = total.reshape(2, share, tile).astype(BF16)

    if flipped:
        in_specs = [pl.BlockSpec((count, tile, depth), lambda i: (0, i, 0))]
    else:
        in_specs = [pl.BlockSpec((depth, tile), lambda i: (0, i))]
    pair = pl.BlockSpec((2, share, tile), lambda i: (0, 0, i))
    one = pl.BlockSpec((share, tile), lambda i: (0, i))
    pltpu.emit_pipeline(
        body,
        grid=(width // tile,),
        in_specs=in_specs + ([pair] if keep else []),
        out_specs=[one if keep else pair],
    )(weight, *([arrived] if keep else []), send)


def pipe_weight(place, order, first, columns, others, outs):
    block = outs[0].shape[1]

    def body(*refs):
        for z in range(2):
            at = place.block(order, first, 2 * pl.program_id(0) + z)
            taken = columns[:, pl.ds(pl.multiple_of(at * block, block), block)]
            for other, ref in zip(others, refs):
                ref[z] = over_rows(taken, other[...]).astype(BF16)

    pltpu.emit_pipeline(
        body,
        grid=(2,),
        out_specs=[pl.BlockSpec((2, block, out.shape[2]), lambda j: (j, 0, 0)) for out in outs],
    )(*outs)


def pipe_second(mine, kept, arrived, send):
    _, rows, width = kept.shape
    tile = min(128, rows)
    spec = pl.BlockSpec((2, tile, width), lambda i: (1 - mine, i, 0))

    def body(k_ref, a_ref, o_ref):
        o_ref[...] = (k_ref[...].astype(F32) + a_ref[...].astype(F32)).astype(BF16)

    pltpu.emit_pipeline(
        body,
        grid=(rows // tile,),
        in_specs=[spec, spec],
        out_specs=[pl.BlockSpec((2, tile, width), lambda i: (0, i, 0))],
    )(kept, arrived, send)


def pipe_third(mine, first, kept, arrived, second, send, own):
    _, rows, width = kept.shape
    tile = min(128, rows)
    spec = pl.BlockSpec((2, tile, width), lambda i: (mine, i, 0))
    one = pl.BlockSpec((tile, width), lambda i: (i, 0))

    def body(k_ref, a_ref, b_ref, s_ref, o_ref):
        low, high = (
            k_ref[at].astype(F32) + a_ref[at].astype(F32) + b_ref[at].astype(F32) for at in range(2)
        )
        s_ref[...] = jnp.where(first, high, low).astype(BF16)
        o_ref[...] = jnp.where(first, low, high)

    pltpu.emit_pipeline(
        body,
        grid=(rows // tile,),
        in_specs=[spec, spec, pl.BlockSpec((2, tile, width), lambda i: (0, i, 0))],
        out_specs=[one, one],
    )(kept, arrived, second, send, own)


def finished(results, qkv, out, gate_up, down, block_at, input_at, sums_at):
    wide, tall = [*gate_up, *qkv], [out, down]
    steps = 4
    block = results[qkv[0].own].shape[0]
    part = block // steps

    def kernel(*refs):
        given, made = refs[: 2 * len(wide + tall) + 3], refs[2 * len(wide + tall) + 3 :]

        def total(at):
            return given[2 * at][...] + given[2 * at + 1][...].astype(F32)

        for at in range(len(gate_up)):
            made[0][at] = total(at)
        for at in range(len(qkv)):
            made[1][at] = total(len(gate_up) + at)
        for at in range(len(tall)):

            @pl.when(pl.program_id(0) == 0)
            def _():
                made[2 + at][...] = total(len(wide) + at).T

        made[4][...] = given[-3][...]
        made[5][...] = given[-2][...]
        made[6][...] = given[-1][4:7, :]
        made[7][0:1, :], made[7][1:2, :] = given[-1][0:1, :], given[-1][2:3, :]
        made[8][0:1, :], made[8][1:2, :] = given[-1][1:2, :], given[-1][3:4, :]

    ins, in_specs = [], []
    for p in wide:
        for at in (p.own, p.third[1]):
            ins.append(results[at])
            in_specs.append(pl.BlockSpec((part, results[at].shape[1]), lambda i: (i, 0)))
    for p in tall:
        for at in (p.own, p.third[1]):
            ins.append(results[at])
            in_specs.append(at_zero(*results[at].shape))
    inner, width = results[down.own].shape[1], results[out.own].shape[1]
    share, full = results[block_at].shape
    by_row = pl.BlockSpec((share // steps, full), lambda i: (i, 0))
    got = pl.pallas_call(
        kernel,
        name="finished",
        grid=(steps,),
        in_specs=in_specs + [by_row, by_row, at_zero(8, full)],
        out_specs=[
            pl.BlockSpec((2, part, inner), lambda i: (0, i, 0)),
            pl.BlockSpec((3, part, width), lambda i: (0, i, 0)),
            at_zero(width, block), at_zero(inner, block), by_row, by_row,
            at_zero(3, full), at_zero(2, full), at_zero(2, full),
        ],
        out_shape=[
            shape((2, block, inner), F32), shape((3, block, width), F32), shape((width, block), F32),
            shape((inner, block), F32), shape((share, full), BF16), shape((share, full), F32),
            shape((3, full), F32), shape((2, full), F32), shape((2, full), F32),
        ],
        compiler_params=pltpu.CompilerParams(vmem_limit_bytes=VMEM_LIMIT),
    )(*ins, results[block_at], results[input_at], results[sums_at])
    return got[4], got[5], got[1], got[6], got[2], got[0], got[3], got[7], got[8]


def at_zero(*dims):
    return pl.BlockSpec(dims, lambda *_: (0,) * len(dims))


def forward(tokens, cotangent, qkv_weight, bias, out_weight, gate_up_weight, down_weight, gains, shifts, begins, tables):
    rows, full = tokens.shape
    width, inner = out_weight.shape[0], down_weight.shape[0]
    share = rows // 4
    half = share // 2
    ins = [
        tokens, cotangent, qkv_weight, bias[:, None, :], out_weight, gate_up_weight, down_weight,
        gains, shifts, begins, *tables,
    ]
    outs = Arrays()
    for dims in ((rows, full), (rows, full), (rows, inner), (rows, inner), (rows, inner), (rows, width), (3, rows, width)):
        outs.add(BF16, *dims)
    outs.add(F32, width // 128, rows // QB, 1, 2 * QB)
    outs.add(F32, share, full)
    given, made = len(ins), len(outs.shapes)
    scratch = Arrays()
    for _, dims in enumerate(outs.shapes[1:]):
        scratch.add(dims[1], *dims[0])
    cot_at, out_weight_at = scratch.add(BF16, rows, full), scratch.add(BF16, width, full)
    tables_at = [scratch.add(F32, rows, 128) for _ in range(3)]
    begins_at = scratch.add(jnp.int32, 1, rows)
    gains_at, shifts_at = scratch.add(F32, 2, full), scratch.add(F32, 2, full)
    own_at, kept_at = scratch.add(BF16, share, full), scratch.add(F32, share, full)
    to_core_at = scratch.add(BF16, 2, half, full)
    fore = [
        [to_core_at, scratch.add(BF16, 2, half, full), scratch.add(BF16, half, full), scratch.add(BF16, half, full)]
        for _ in range(2)
    ]
    kinds = [pltpu.VMEM(dims, kind) for dims, kind in scratch.shapes]
    kinds += [pltpu.SemaphoreType.DMA((16,)), pltpu.SemaphoreType.DMA((16,)), pltpu.SemaphoreType.DMA((24,))]

    def kernel(*refs):
        tok, cot, w_qkv, b_qkv, w_out, w_gate_up, w_down, gain_in, shift_in, begin_in, *tables_in = refs[:given]
        o, s = refs[given : given + made], refs[given + made :]
        sends, receives, locals_ = s[-3:]
        sec_v, hidden, gate_grad, up_grad, heads, qkv_v, logs, residual = s[: made - 1]
        cot_v, w_out_v, kept = s[cot_at], s[out_weight_at], s[kept_at]
        turn, ahead, behind = (s[at] for at in tables_at)
        begin, gain, shift, own = s[begins_at], s[gains_at], s[shifts_at], s[own_at]
        place = Place()
        partners = [place.to_core, place.to_chip]
        wires = Wires(sends, receives)
        stays = []

        def load(source, target):
            copy = pltpu.make_async_copy(source, target, locals_.at[len(stays)])
            copy.start()
            stays.append(copy)
            return copy

        def quarter(at, tensor, part=None):
            if part is None:
                return at.at[pl.ds(pl.multiple_of(tensor * share, share), share), :]
            return at.at[pl.ds(pl.multiple_of(tensor * share + part * half, half), half), :]

        mine, beyond = place.tensor, place.core + 2 * (1 - place.chip)
        barrier = pltpu.get_barrier_semaphore()
        for partner in partners:
            pl.semaphore_signal(barrier, inc=1, device_id=partner, device_id_type=MESH)
        early = [load(gain_in, gain), load(shift_in, shift)]
        soon = [
            load(tables_in[0], turn), load(tables_in[1], ahead), load(tables_in[2], behind),
            load(begin_in, begin),
        ]
        later = [load(quarter(tok, mine), own), load(w_out, w_out_v), load(cot, cot_v)]
        for copy in early:
            copy.wait()

        def norm_first(t_ref):
            unit, _ = norm_parts(t_ref[...].astype(F32))
            at = pl.ds(pl.multiple_of(pl.program_id(0) * half, half), half)
            sec_v[at, :] = (unit * gain[0:1, :] + shift[0:1, :]).astype(BF16)

        pltpu.emit_pipeline(
            norm_first, grid=(rows // half,), in_specs=[pl.BlockSpec((half, full), lambda i: (i, 0))]
        )(tok)
        keep_normed = load(sec_v, o[0])
        for copy in soon:
            copy.wait()

        def project(first_of, count, turns):
            def body(w_ref, b_ref):
                j = first_of + pl.program_id(0)
                lanes = pl.ds(pl.multiple_of(pl.program_id(1) * 256, 256), 256)
                for first in range(0, rows, 256):
                    at = slice(first, first + 256)
                    got = jnp.dot(sec_v[at, :], w_ref[0], preferred_element_type=F32) + b_ref[0]
                    if turns:
                        got = turned(got, turn[at, :], ahead[at, :], behind[at, :])
                    qkv_v[j, at, lanes] = got.astype(BF16)

            pltpu.emit_pipeline(
                body,
                grid=(count, width // 256),
                in_specs=[
                    pl.BlockSpec((1, full, 256), lambda j, i: (first_of + j, 0, i)),
                    pl.BlockSpec((1, 1, 256), lambda j, i: (first_of + j, 0, i)),
                ],
            )(w_qkv, b_qkv)

        project(0, 2, True)
        project(2, 1, False)

        def project_out(part):
            to_core, from_core = s[fore[part][0]], s[fore[part][1]]
            places = [(2 * y + c) * share + part * half for c in (1 - place.core, place.core) for y in range(2)]
            left = jnp.concatenate([heads[pl.ds(pl.multiple_of(at, half), half), :] for at in places], axis=0)
            for first in range(0, full, 512):
                at = slice(first, first + 512)
                got = jnp.dot(left, w_out_v[:, at], preferred_element_type=F32)
                to_core[:, :, at] = got[:share].reshape(2, half, 512).astype(BF16)
                kept[:, at] = got[share:]
            return wires.start(to_core, from_core, place.to_core)

        def add_core(part, flying):
            from_core, to_chip, from_chip = (s[at] for at in fore[part][1:])
            flying.wait_recv()
            wires.sent(flying)
            low = kept[:half, :] + from_core[0].astype(F32)
            high = kept[half:, :] + from_core[1].astype(F32)
            first = place.chip == 0
            at = slice(part * half, (part + 1) * half)
            residual[at, :] = own[at, :].astype(F32) + jnp.where(first, low, high)
            to_chip[...] = jnp.where(first, high, low).astype(BF16)
            return wires.start(to_chip, from_chip, place.to_chip)

        def norm_second(part, flying):
            flying.wait_recv()
            at = slice(part * half, (part + 1) * half)
            got = residual[at, :] + s[fore[part][3]][...].astype(F32)
            residual[at, :] = got
            unit, _ = norm_parts(got)
            rows_at = quarter(sec_v, mine, part)
            rows_at[...] = (unit * gain[1:2, :] + shift[1:2, :]).astype(BF16)
            return (
                wires.start(rows_at, rows_at, place.to_chip),
                wires.start(rows_at, rows_at, place.to_core),
            )

        def pass_on(part, chip_flying):
            chip_flying.wait_recv()
            rows_at = quarter(sec_v, beyond, part)
            return wires.start(rows_at, rows_at, place.to_core)

        def hidden_back(first, count, tile):
            def body(w_ref):
                lanes = pl.ds(pl.multiple_of((first + pl.program_id(0)) * tile, tile), tile)
                up_grad[:, lanes] = over_columns(cot_v[...], w_ref[...]).astype(BF16)

            pltpu.emit_pipeline(
                body, grid=(count,), in_specs=[pl.BlockSpec((tile, full), lambda i: (i, 0))]
            )(w_down.at[pl.ds(first * tile, count * tile), :])

        def gate_up(part, begin_at, count, tile):
            def body(w_ref):
                lanes = pl.ds(pl.multiple_of((begin_at + pl.program_id(0)) * tile, tile), tile)
                for q in range(0, 4, 2):
                    spots = [slice((q + z) * share + part * half, (q + z) * share + (part + 1) * half) for z in range(2)]
                    left = jnp.concatenate([sec_v[at, :] for at in spots], axis=0)
                    both = [jnp.dot(left, w_ref[j], preferred_element_type=F32) for j in range(2)]
                    for z, at in enumerate(spots):
                        gates, ups = (of[z * half : (z + 1) * half, :] for of in both)
                        sigmoid = 1.0 / (1.0 + jnp.exp(-gates))
                        active = gates * sigmoid
                        grad = up_grad[at, lanes].astype(F32)
                        hidden[at, lanes] = (active * ups).astype(BF16)
                        gate_grad[at, lanes] = (
                            grad * ups * (sigmoid * (1.0 + gates * (1.0 - sigmoid)))
                        ).astype(BF16)
                        up_grad[at, lanes] = (grad * active).astype(BF16)

            pltpu.emit_pipeline(
                body, grid=(count,), in_specs=[pl.BlockSpec((2, full, tile), lambda i: (0, 0, i))]
            )(w_gate_up.at[:, :, pl.ds(begin_at * tile, count * tile)])

        wide_tiles = inner // 256 - 1

        def gate_ups(part):
            gate_up(part, 0, wide_tiles, 256)
            gate_up(part, 2 * wide_tiles, inner // 128 - 2 * wide_tiles, 128)

        attend_part(begin, qkv_v, heads, logs, 0)
        keep_normed.wait()
        for copy in later:
            copy.wait()
        pl.semaphore_wait(barrier, len(partners))
        flying = project_out(0)
        attend_part(begin, qkv_v, heads, logs, 1)
        chip0 = add_core(0, flying)
        flying = project_out(1)
        kept_early = [load(heads, o[5]), load(qkv_v, o[6]), load(logs, o[7])]
        hidden_back(2 * wide_tiles, inner // 128 - 2 * wide_tiles, 128)
        chip1 = add_core(1, flying)
        hidden_back(0, wide_tiles, 256)
        chip0, core0 = norm_second(0, chip0)
        chip1, core1 = norm_second(1, chip1)
        both0 = pass_on(0, chip0)
        core0.wait_recv()
        both0.wait_recv()
        gate_ups(0)
        both1 = pass_on(1, chip1)
        core1.wait_recv()
        both1.wait_recv()
        kept_early += [load(sec_v, o[1]), load(residual, o[8])]
        gate_ups(1)

        late = [load(hidden, o[2]), load(gate_grad, o[3]), load(up_grad, o[4])]
        for copy in [*kept_early, *late]:
            copy.wait()
        wires.close()

    return pl.pallas_call(
        kernel,
        name="forward",
        in_specs=[ANY] * given,
        out_specs=[ANY] * made,
        out_shape=[shape(dims, kind) for dims, kind in outs.shapes],
        scratch_shapes=kinds,
        compiler_params=pltpu.CompilerParams(
            vmem_limit_bytes=62 << 20, collective_id=1, has_side_effects=True
        ),
    )(*ins)


def backward(
    tokens, cotangent, qkv_weight, out_weight, gate_up_weight, down_weight, gains, begins, tables, saved
):
    rows, full = tokens.shape
    width, inner = out_weight.shape[0], down_weight.shape[0]
    share, block = rows // 4, full // 8
    half = share // 2
    ins = [
        tokens, cotangent, qkv_weight, out_weight, gate_up_weight, down_weight, gains, begins, *tables, *saved,
    ]
    outs = Arrays()
    down, up = Piece(outs, X_FIRST, block, inner), Piece(outs, X_FIRST, block, inner)
    gate = Piece(outs, Z_FIRST, block, inner)
    out = Piece(outs, X_FIRST, block, width)
    qkv = [Piece(outs, X_FIRST, block, width) for _ in range(3)]
    pieces = [down, gate, up, out, *qkv]
    rows_out = [[outs.add(BF16, 2, share, full) for _ in range(2)] + [outs.add(BF16, share, full)] for _ in range(3)]
    block_at, input_at, sums_at = outs.add(BF16, share, full), outs.add(F32, share, full), outs.add(F32, 8, full)
    given, made = len(ins), len(outs.shapes)

    scratch = Arrays()
    for array in saved[1:]:
        scratch.add(array.dtype, *array.shape)
    cot_at, low_rows, out_weight_at = scratch.add(BF16, rows, full), scratch.add(BF16, rows, full), scratch.add(BF16, width, full)
    heads_grad_at, qkv_grad_at = scratch.add(BF16, rows, width), scratch.add(BF16, 3, rows, width)
    tables_at = [scratch.add(F32, rows, 128) for _ in range(3)]
    begins_at, gains_at = scratch.add(jnp.int32, 1, rows), scratch.add(F32, 2, full)
    own_at = scratch.add(BF16, share, full)
    residual_grad_at, kept_at = (scratch.add(F32, share, full) for _ in range(2))
    chip_in = [scratch.add(BF16, share, full) for _ in range(3)]
    sum_k_at, sum_v_at = scratch.add(F32, rows, 128), scratch.add(F32, rows, 128)
    sum_b_at = scratch.add(F32, 8, width)
    held_at, came_at = scratch.add(F32, 6, 8, full), scratch.add(F32, 5, 8, full)
    kinds = [pltpu.VMEM(dims, kind) for dims, kind in scratch.shapes]
    kinds += [pltpu.SemaphoreType.DMA((48,)), pltpu.SemaphoreType.DMA((48,)), pltpu.SemaphoreType.DMA((24,))]

    def kernel(*refs):
        tok, cot, w_qkv, w_out, w_gate_up, w_down, gain_in, begin_in = refs[:8]
        tables_in, saved_in = refs[8:11], refs[11:given]
        o, s = refs[given : given + made], refs[given + made :]
        sends, receives, locals_ = s[-3:]
        sec_v, hidden, gate_grad, up_grad, heads, qkv_v, logs, residual = s[: len(saved) - 1]
        cot_v, low_v, w_out_v = s[cot_at], s[low_rows], s[out_weight_at]
        heads_grad, qkv_grad = s[heads_grad_at], s[qkv_grad_at]
        turn, ahead, behind = (s[at] for at in tables_at)
        begin, gain, own = s[begins_at], s[gains_at], s[own_at]
        residual_grad, kept = s[residual_grad_at], s[kept_at]
        held, came, sum_b = s[held_at], s[came_at], s[sum_b_at]
        place = Place()
        partners = [*place.by_bit, place.to_core, place.to_chip]
        wires = Wires(sends, receives)
        stays = []

        def load(source, target):
            copy = pltpu.make_async_copy(source, target, locals_.at[len(stays)])
            copy.start()
            stays.append(copy)
            return copy

        def quarter(at, tensor, part=None):
            if part is None:
                return at.at[pl.ds(pl.multiple_of(tensor * share, share), share), :]
            return at.at[pl.ds(pl.multiple_of(tensor * share + part * half, half), half), :]

        mine, beyond = place.tensor, place.core + 2 * (1 - place.chip)
        barrier = pltpu.get_barrier_semaphore()
        for partner in partners:
            pl.semaphore_signal(barrier, inc=1, device_id=partner, device_id_type=MESH)
        loads = [load(cot, cot_v), load(saved_in[2], hidden)]
        loads_second = [load(saved_in[1], sec_v), load(saved_in[3], gate_grad), load(saved_in[4], up_grad)]
        loads_rest = [
            load(saved_in[5], heads), load(saved_in[6], qkv_v), load(saved_in[7], logs), load(saved_in[8], residual),
            load(w_out, w_out_v), load(gain_in, gain), load(begin_in, begin),
            load(tables_in[0], turn), load(tables_in[1], ahead), load(tables_in[2], behind),
        ]
        pl.semaphore_wait(barrier, len(partners))

        def first_half(those, columns, others):
            order = those[0].order
            pipe_weight(place, order, True, columns, others, [o[p.first[0]] for p in those])
            for p in those:
                p.flying = wires.start(o[p.first[0]], o[p.first[1]], place.by_bit[order[0]])

        def second_half(those, columns, others):
            pipe_weight(place, those[0].order, False, columns, others, [o[p.kept] for p in those])

        def then(p):
            p.flying.wait_recv()
            pipe_second(place.bit(p.order[1]), o[p.kept], o[p.first[1]], o[p.second[0]])
            p.flying = wires.start(o[p.second[0]], o[p.second[1]], place.by_bit[p.order[1]])

        def last(p):
            p.flying.wait_recv()
            pipe_third(
                place.bit(p.order[1]), place.bit(p.order[2]) == 0, o[p.kept], o[p.first[1]], o[p.second[1]],
                o[p.third[0]], o[p.own],
            )
            p.flying = wires.start(o[p.third[0]], o[p.third[1]], place.by_bit[p.order[2]])

        def rows_first(at, lefts, weight, flipped):
            pipe_rows(place, lefts, weight, flipped, o[rows_out[at][0]])
            return wires.start(o[rows_out[at][0]], o[rows_out[at][1]], place.to_core)

        def rows_then(at, lefts, weight, flipped, flying, into):
            flying.wait_recv()
            pipe_rows(place, lefts, weight, flipped, o[rows_out[at][2]], o[rows_out[at][1]], into)
            return wires.start(o[rows_out[at][2]], s[chip_in[at]], place.to_chip)

        def norm_grads(values, base, arrived, row, result, low):
            for part in range(2):
                at = slice(part * half, (part + 1) * half)
                unit, inverse = norm_parts(values[at, :].astype(F32))
                grad = kept[at, :] + arrived[at, :].astype(F32)
                got = base[at, :].astype(F32) + norm_back(unit, inverse, gain[row : row + 1, :], grad)
                result[at, :] = got
                if low is not None:
                    low[at, :] = got.astype(BF16)
                held[0, 2 * row : 2 * row + 1, :] += jnp.sum(grad * unit, axis=0, keepdims=True)
                held[0, 2 * row + 1 : 2 * row + 2, :] += jnp.sum(grad, axis=0, keepdims=True)

        def add_everywhere(step):
            order = [place.to_core, place.to_chip, place.by_bit[1], place.by_bit[2], place.by_bit[0]]
            return wires.start(held.at[step], came.at[step], order[step])

        def added(step, flying):
            flying.wait_recv()
            held[step + 1] = held[step] + came[step]

        grads = [gate_grad, up_grad]
        lows = [qkv_grad.at[j] for j in range(3)]
        for copy in loads:
            copy.wait()
        first_half([down], cot_v, [hidden])
        for copy in loads_second:
            copy.wait()
        first_half([gate], sec_v, [gate_grad])
        second_half([down], cot_v, [hidden])
        flying = rows_first(0, grads, w_gate_up, True)
        first_half([up], sec_v, [up_grad])
        chip = rows_then(0, grads, w_gate_up, True, flying, kept)
        second_half([gate], sec_v, [gate_grad])
        second_half([up], sec_v, [up_grad])
        renormed = load(saved_in[0], sec_v)
        for copy in loads_rest:
            copy.wait()
        held[0] = jnp.zeros_like(held[0])
        chip.wait_recv()
        norm_grads(residual, quarter(cot_v, mine), s[chip_in[0]], 1, residual_grad, quarter(low_v, mine))
        mine_v, beyond_v = quarter(low_v, mine), quarter(low_v, beyond)
        chip = wires.start(mine_v, mine_v, place.to_chip)
        core = wires.start(mine_v, mine_v, place.to_core)
        flying = rows_first(1, [hidden], w_down, False)
        branch_chip = rows_then(1, [hidden], w_down, False, flying, kept)
        then(down)
        chip.wait_recv()
        both = wires.start(beyond_v, beyond_v, place.to_core)
        core.wait_recv()
        both.wait_recv()
        for first in range(0, rows, 256):
            at = slice(first, first + 256)
            heads_grad[at, :] = over_columns(low_v[at, :], w_out_v[...]).astype(BF16)
        then(gate)
        first_half([out], low_v, [heads])
        attend_grads(
            begin, qkv_v, heads_grad, logs, turn, ahead, behind, qkv_grad, s[sum_k_at], s[sum_v_at], sum_b
        )
        renormed.wait()
        first_half(qkv, sec_v, lows)
        flying = rows_first(2, lows, w_qkv, True)
        branch_chip.wait_recv()
        own[...] = (residual[...] + kept[...] + s[chip_in[1]][...].astype(F32)).astype(BF16)
        keep_block = load(own, o[block_at])
        last(down)
        chip = rows_then(2, lows, w_qkv, True, flying, kept)
        second_half([out], low_v, [heads])
        second_half(qkv, sec_v, lows)
        then(up)
        chip.wait_recv()
        keep_block.wait()
        back = load(quarter(tok, mine), own)
        back.wait()
        norm_grads(own, residual_grad, s[chip_in[2]], 0, residual, None)
        keep_input = load(residual, o[input_at])
        held[0, 4:7, pl.ds(pl.multiple_of(place.tensor * width, 128), width)] = sum_b[0:3, :]
        flying = add_everywhere(0)
        added(0, flying)
        flying = add_everywhere(1)
        last(gate)
        added(1, flying)
        last(up)
        then(out)
        last(out)
        flying = add_everywhere(2)
        then(qkv[0])
        added(2, flying)
        flying = add_everywhere(3)
        then(qkv[1])
        last(qkv[0])
        added(3, flying)
        flying = add_everywhere(4)
        then(qkv[2])
        last(qkv[1])
        added(4, flying)
        keep_sums = load(held.at[5], o[sums_at])
        last(qkv[2])
        for p in pieces:
            p.flying.wait_recv()
        keep_input.wait()
        keep_sums.wait()
        wires.close()

    results = pl.pallas_call(
        kernel,
        name="backward",
        in_specs=[ANY] * given,
        out_specs=[ANY] * made,
        out_shape=[shape(dims, kind) for dims, kind in outs.shapes],
        scratch_shapes=kinds,
        compiler_params=pltpu.CompilerParams(
            vmem_limit_bytes=62 << 20, collective_id=2, has_side_effects=True
        ),
    )(*ins)
    return finished(results, qkv, out, [gate, up], down, block_at, input_at, sums_at)


def body(
    tokens,
    seq_lengths,
    qkv_weight,
    qkv_bias,
    out_weight,
    gate_up_weight,
    down_weight,
    norm_gains,
    norm_shifts,
    cotangent,
):
    row_count, full_width = tokens.shape
    local_width = qkv_weight.shape[2]
    tensor_at, dp_at, dp_size = lax.axis_index("tensor"), lax.axis_index("dp"), lax.axis_size("dp")
    marks = jnp.stack([tensor_at & 1, tensor_at >> 1, dp_at]).astype(jnp.int32)
    bits = dp_size.bit_length() - 1
    x_first = tuple(range(bits))
    z_first = (1, 0) + x_first[2:]
    fine = (full_width // dp_size) % 128 == 0

    def send(order, columns, other, turned_out, after):
        if not fine:
            return columns
        return weight_send(marks, order, columns, other, turned_out, after)

    def keep(order, columns, other, turned_out, sent, after):
        if not fine:
            return columns, None
        return weight_keep(
            marks, order, columns, other, turned_out, swap(sent, "dp", order[0]), after
        )

    def total(order, columns, other, turned_out, kept):
        if not fine:
            return plain_weight(columns, other, turned_out)
        return finish(order, kept[1], swap(kept[0], "dp", order[1]))

    begins, *tables = positions(seq_lengths[0], row_count)
    if dp_size == 8 and lax.axis_size("tensor") == 4:
        saved = forward(
            tokens, cotangent, qkv_weight, qkv_bias.astype(F32), out_weight, gate_up_weight, down_weight,
            norm_gains, norm_shifts, begins[None], tables,
        )
        return backward(
            tokens, cotangent, qkv_weight, out_weight, gate_up_weight, down_weight, norm_gains, begins[None],
            tables, saved,
        )
    normed, queries, keys, values = project(
        tokens, qkv_weight, qkv_bias, norm_gains[0], norm_shifts[0], tables
    )
    heads_out, logs = attend(begins, queries, keys, values)
    sent = rows_product(marks, [heads_out], out_weight, False)
    to_chip, own = rows_product(marks, [heads_out], out_weight, False, swap(sent, "tensor", 0))
    hidden_grad = hidden_back(marks, cotangent, down_weight, [own])
    residual, second_own = norm_rows(
        marks, tokens, own, swap(to_chip, "tensor", 1), norm_gains[1], norm_shifts[1], [hidden_grad]
    )
    second, hidden, hidden_t, gate_grad, up_grad = gate_up(
        marks, spread(second_own), gate_up_weight, hidden_grad
    )
    down_sent = send(x_first, cotangent, hidden_t, True, [])
    second_sent = rows_product(marks, [gate_grad, up_grad], gate_up_weight, True, None, [down_sent])
    up_sent = send(x_first, second, up_grad, False, [second_sent])
    to_chip, own = rows_product(
        marks, [gate_grad, up_grad], gate_up_weight, True, swap(second_sent, "tensor", 0), [up_sent]
    )
    gate_sent = send(z_first, second, gate_grad, False, [own])
    branch_sent = rows_product(marks, [hidden], down_weight, False, None, [gate_sent])
    branch_to_chip, branch_own = rows_product(
        marks, [hidden], down_weight, False, swap(branch_sent, "tensor", 0), [gate_sent]
    )
    residual_grad, residual_low_own, second_sums = norm_back_rows(
        marks, residual, cotangent, own, swap(to_chip, "tensor", 1), norm_gains[1], [branch_own]
    )
    block_out = (
        residual + branch_own + swap(branch_to_chip, "tensor", 1).astype(F32)
    ).astype(BF16)
    down_kept = keep(x_first, cotangent, hidden_t, True, down_sent, [residual_low_own])
    residual_low, heads_grad = heads_back(
        marks, spread(residual_low_own), out_weight, [down_kept[0]]
    )
    heads_t = heads_out.T
    out_sent = send(x_first, residual_low, heads_t, True, [heads_grad])
    projected_low = attend_back(begins, queries, keys, values, heads_grad, logs, tables)
    gate_kept = keep(z_first, second, gate_grad, False, gate_sent, [projected_low[0]])
    qkv_sent = []
    before = gate_kept[0]
    for grads in projected_low:
        before = send(x_first, normed, grads, False, [before])
        qkv_sent.append(before)
    normed_sent = rows_product(marks, projected_low, qkv_weight, True, None, [before])
    up_kept = keep(x_first, second, up_grad, False, up_sent, [normed_sent])
    to_chip, own = rows_product(
        marks, projected_low, qkv_weight, True, swap(normed_sent, "tensor", 0), [normed_sent]
    )
    input_grad, _, first_sums = norm_back_rows(
        marks, tokens, residual_grad, own, swap(to_chip, "tensor", 1), norm_gains[0], [up_kept[0]]
    )
    bias_local = jnp.stack([jnp.sum(g, axis=0, dtype=F32) for g in projected_low])
    bias_placed = lax.dynamic_update_slice(
        jnp.zeros((3, full_width), F32), bias_local, (0, tensor_at * local_width)
    )
    sums = everywhere(jnp.concatenate([first_sums, second_sums, bias_placed], axis=0))
    out_kept = keep(x_first, residual_low, heads_t, True, out_sent, [input_grad])
    qkv_kept = []
    before = out_kept[0]
    for grads, sent in zip(projected_low, qkv_sent):
        kept = keep(x_first, normed, grads, False, sent, [before])
        before = kept[0]
        qkv_kept.append(kept)
    return (
        block_out,
        input_grad,
        jnp.stack(
            [total(x_first, normed, g, False, k) for g, k in zip(projected_low, qkv_kept)]
        ),
        sums[4:7],
        total(x_first, residual_low, heads_t, True, out_kept),
        jnp.stack(
            [
                total(z_first, second, gate_grad, False, gate_kept),
                total(x_first, second, up_grad, False, up_kept),
            ]
        ),
        total(x_first, cotangent, hidden_t, True, down_kept),
        jnp.stack([sums[0], sums[2]]),
        jnp.stack([sums[1], sums[3]]),
    )


def solution(mesh):
    return jax.shard_map(
        body,
        mesh=mesh,
        in_specs=(
            P("dp", None),
            P("dp", None),
            P(None, None, "tensor"),
            P(None, "tensor"),
            P("tensor", None),
            P(None, None, "tensor"),
            P("tensor", None),
            P(),
            P(),
            P("dp", None),
        ),
        out_specs=(
            P(("dp", "tensor"), None),
            P(("dp", "tensor"), None),
            P(None, "dp", "tensor"),
            P(),
            P("tensor", "dp"),
            P(None, "dp", "tensor"),
            P("tensor", "dp"),
            P(),
            P(),
        ),
        check_vma=False,
    )
```
